32 devices in a mesh: sim: 8 (over y, x, core), section: 4 (over z).
Axes of the slice: x: 2, y: 2, z: 4, core: 2. Of those that a mesh axis runs over, the one named last changes fastest.
Arguments:
- density: float32 [4, 768, 512], P(None, 'sim', 'section'), may hold values from 0.5 to 2
- momentum: float32 [3, 4, 768, 512], P(None, None, 'sim', 'section'), may hold values from -1 to 1
- energy: float32 [4, 768, 512], P(None, 'sim', 'section'), may hold values from 4 to 8
- membership: int32 [192, 128], P(('sim', 'section')), may hold values from 0 to 63
- slot_of_brick: int32 [8, 4], P('sim'), may hold values from 0 to 3, each once within a row
Outputs:
- coded: float32 [5, 4, 768, 512], P(None, None, ('sim', 'section'))
- group_peak: float32 [5, 64], replicated
The draws below stay inside these ranges and needn't reach their ends.
Inputs may be any that keep to these rules, and one draw needn't show every extreme that they name: `slot_of_brick`: each row is a permutation of the 4 bricks.
All inputs are finite; a program needn't handle non-finite values.
Results may differ from the reference program's by a relative error of at most 0.0003.
Values sent between devices are 32-bit elements; how exact they have to be, the bound alone decides.
No kernel may reach another device: no remote copies, remote signals or barrier semaphores. Data moves between devices by JAX's collectives and lax.ppermute only.
A program may use at most 64 MiB of HBM per device.

```python
import jax
import jax.numpy as jnp
from jax import lax

XD = 128
ZP = 4
X = 512
Y = 768
GROUPS = 64
N_SIM = 8
N_SECTION = 4


def plant(drawn, rng, low, high):
    longest = drawn.shape.index(max(drawn.shape))
    spots = []
    for shift in (0, 1):
        where = [jax.random.randint(jax.random.fold_in(rng, axis), (), 0, length) for axis, length in enumerate(drawn.shape)]
        where[longest] = (where[longest] + shift) % drawn.shape[longest]
        spots.append(tuple(where))
    return drawn.at[spots[0]].set(low).at[spots[1]].set(high)


def shard_levels(rng, dims, split, smallest, largest):
    gain = 1.0
    for dim, blocks in split:
        draws = jax.random.uniform(jax.random.fold_in(jax.random.fold_in(rng, 6), dim), (blocks,), jnp.float32, smallest / len(split), largest / len(split))
        gain = gain * jnp.repeat(jnp.exp(draws), dims[dim] // blocks).reshape((-1,) + (1,) * (len(dims) - 1 - dim))
    return gain


def setup_inputs(seed: int = 0) -> dict:
    splits = jax.random.split(jax.random.key(seed), 6)
    density = jnp.clip(0.5 + 1.5 * jax.random.uniform(splits[0], (ZP, Y, X), jnp.float32) ** shard_levels(splits[0], (ZP, Y, X), ((1, 8), (2, 4)), -0.2, 0.2), 0.5, 2.0)
    momentum = jnp.clip(jax.random.uniform(splits[1], (3, ZP, Y, X), jnp.float32, -1.0, 1.0) * shard_levels(splits[1], (3, ZP, Y, X), ((2, 8), (3, 4)), -0.4, 0.0), -1.0, 1.0)
    energy = jnp.clip(4.0 + 4.0 * jax.random.uniform(splits[2], (ZP, Y, X), jnp.float32) ** shard_levels(splits[2], (ZP, Y, X), ((1, 8), (2, 4)), -0.2, 0.2), 4.0, 8.0)
    membership = plant(jax.random.randint(splits[3], (Y // 4, X // 4), 0, GROUPS), jax.random.fold_in(splits[3], 1), 0, GROUPS - 1).astype(jnp.int32)
    slot_of_brick = jax.vmap(lambda own: jax.random.permutation(own, N_SECTION))(jax.random.split(splits[4], N_SIM)).reshape((N_SIM, N_SECTION)).astype(jnp.int32)
    return {"density": density, "momentum": momentum, "energy": energy, "membership": membership, "slot_of_brick": slot_of_brick}


GAMMA_LESS = 0.4
COURANT = 0.05
DIFFUSE = 0.1
EPSILON = 1e-06
HIGH = lax.Precision.HIGHEST

def flux_update(padded):
    density_c = padded[0]
    momentum_x = padded[1]
    momentum_y = padded[2]
    momentum_z = padded[3]
    energy_c = padded[4]
    velocity_x = momentum_x / density_c
    velocity_y = momentum_y / density_c
    kinetic = 0.5 * (momentum_x * momentum_x + momentum_y * momentum_y + momentum_z * momentum_z) / density_c
    pressure = GAMMA_LESS * (energy_c - kinetic)
    flux_x = jnp.stack([momentum_x, momentum_x * velocity_x + pressure, momentum_y * velocity_x, momentum_z * velocity_x, (energy_c + pressure) * velocity_x])
    flux_y = jnp.stack([momentum_y, momentum_x * velocity_y, momentum_y * velocity_y + pressure, momentum_z * velocity_y, (energy_c + pressure) * velocity_y])
    center = padded[:, :, 1:-1, 1:-1]
    spread = padded[:, :, 1:-1, 2:] + padded[:, :, 1:-1, :-2] + padded[:, :, 2:, 1:-1] + padded[:, :, :-2, 1:-1] - 4.0 * center
    return center - COURANT * (flux_x[:, :, 1:-1, 2:] - flux_x[:, :, 1:-1, :-2]) - COURANT * (flux_y[:, :, 2:, 1:-1] - flux_y[:, :, :-2, 1:-1]) + DIFFUSE * spread

def predict(extended):
    h = extended.shape[2] - 6
    guess = (-extended[:, :, 0:h] + 9.0 * extended[:, :, 2:h + 2] + 9.0 * extended[:, :, 4:h + 4] - extended[:, :, 6:h + 6]) / 16.0
    return extended[:, :, 3:h + 3] - guess

def cosine_entry(k, d):
    factor = jnp.where(k == 0, 0.5, jnp.sqrt(0.5))
    return factor * jnp.cos(jnp.pi * (2.0 * d + 1.0) * k / 8.0)

def cosines():
    k = jnp.arange(4, dtype=jnp.float32)[:, None]
    m = jnp.arange(4, dtype=jnp.float32)[None, :]
    return cosine_entry(k, m).astype(jnp.float32)

def brick_matrix(brick_width):
    quarter = brick_width // 4
    m = jnp.arange(brick_width, dtype=jnp.int32)[:, None]
    column = jnp.arange(brick_width, dtype=jnp.int32)[None, :]
    k = column // quarter
    j = column % quarter
    d = m - 4 * j
    entries = cosine_entry(k.astype(jnp.float32), jnp.clip(d, 0, 3).astype(jnp.float32))
    return jnp.where((d >= 0) & (d < 4), entries, 0.0).astype(jnp.float32)

def transform(residual, brick_width):
    f, z, y, x = residual.shape
    along_z = jnp.einsum('kz,fzyx->fkyx', cosines(), residual, precision=HIGH)
    blocked = along_z.reshape(f, z, y // 4, 4, x)
    along_y = jnp.einsum('km,fzbmx->fzbkx', cosines(), blocked, precision=HIGH).reshape(f, z, y, x)
    bricks = along_y.reshape(f, z, y, x // brick_width, brick_width)
    return jnp.einsum('fzybm,mc->fzybc', bricks, brick_matrix(brick_width), precision=HIGH).reshape(f, z, y, x)

def reorder(coefficients, slot_of_brick, brick_width):
    f, z, y, x = coefficients.shape
    count = x // brick_width
    slabs = slot_of_brick.shape[0]
    placing = (slot_of_brick[:, :, None] == jnp.arange(count, dtype=jnp.int32)[None, None, :]).astype(jnp.float32)
    bricks = coefficients.reshape(f, z, slabs, y // slabs, count, brick_width)
    return jnp.einsum('sbp,fzsybx->fzsypx', placing, bricks, precision=HIGH).reshape(f, z, y, x)

def block_peaks(coefficients, brick_width):
    f, z, y, x = coefficients.shape
    magnitude = lax.optimization_barrier(jnp.max(jnp.abs(coefficients), axis=1))
    magnitude = lax.optimization_barrier(jnp.max(magnitude.reshape(f, y // 4, 4, x), axis=2))
    magnitude = magnitude.reshape(f, y // 4, x // brick_width, 4, brick_width // 4)
    return lax.optimization_barrier(jnp.max(magnitude, axis=3)).reshape(f, y // 4, x // 4)

def gather_peaks(peaks, membership, groups):
    labels = jnp.arange(groups, dtype=jnp.int32)

    def visit(carry, row):
        row_peaks, row_labels = row
        matches = row_labels[:, None] == labels[None, :]
        found = lax.optimization_barrier(jnp.max(jnp.where(matches[None], row_peaks[:, :, None], 0.0), axis=1))
        return (jnp.maximum(carry, found), None)
    start = jnp.zeros((peaks.shape[0], groups), jnp.float32)
    result, unused = lax.scan(visit, start, (jnp.moveaxis(peaks, 1, 0), membership))
    return result

def spread_peaks(group_peak, membership):
    labels = jnp.arange(group_peak.shape[1], dtype=jnp.int32)

    def visit(row_labels):
        matches = (row_labels[:, None] == labels[None, :]).astype(jnp.float32)
        return jnp.dot(group_peak, matches.T, precision=HIGH)
    return jnp.moveaxis(lax.map(visit, membership), 0, 1)

def normalize(coefficients, divisor, brick_width):
    f, z, y, x = coefficients.shape
    rows_count = y // 4
    widened = divisor.reshape(f, rows_count, x // brick_width, 1, brick_width // 4)
    widened = jnp.broadcast_to(widened, (f, rows_count, x // brick_width, 4, brick_width // 4)).reshape(f, rows_count, x)
    widened = jnp.broadcast_to(widened[:, None, :, None, :], (f, z, rows_count, 4, x)).reshape(f, z, y, x)
    return coefficients / (widened + EPSILON)

def reference(density, momentum, energy, membership, slot_of_brick):
    conserved = jnp.concatenate([density[None], momentum, energy[None]], axis=0)
    padded = jnp.pad(conserved, ((0, 0), (0, 0), (1, 1), (1, 1)), mode='wrap')
    updated = flux_update(padded)
    extended = jnp.pad(updated, ((0, 0), (0, 0), (3, 3), (0, 0)), mode='wrap')
    transformed = transform(predict(extended), XD)
    placed = reorder(transformed, slot_of_brick, XD)
    peaks = block_peaks(placed, XD)
    group_peak = gather_peaks(peaks, membership, GROUPS)
    coded = normalize(placed, spread_peaks(group_peak, membership), XD)
    return (coded, group_peak)
```

```python
import functools

import jax
import jax.numpy as jnp
import numpy as np
from jax import lax
from jax.experimental import pallas as pl
from jax.experimental.pallas import tpu as pltpu
from jax.sharding import PartitionSpec as P

GAMMA_LESS = 0.4
COURANT = 0.05
DIFFUSE = 0.1
EPSILON = 1e-06
FIELDS = 5
PAD = 8
LANES = 128
EVEN = 0.5
WIDE = float(np.sqrt(0.5) * np.cos(np.pi / 8))
NARROW = float(np.sqrt(0.5) * np.cos(3 * np.pi / 8))
VMEM_LIMIT = 48 * 1024 * 1024


def vmem():
    return pl.BlockSpec(memory_space=pltpu.VMEM)


def smem():
    return pl.BlockSpec(memory_space=pltpu.SMEM)


def lanes_of(shape):
    return lax.broadcasted_iota(jnp.int32, shape, 1)


def butterfly(a, b, c, d):
    s, t, u, v = a + d, b + c, a - d, b - c
    return (
        EVEN * (s + t),
        WIDE * u + NARROW * v,
        EVEN * (s - t),
        NARROW * u - WIDE * v,
    )


def brick_matrix(width):
    quarter = width // 4
    m = np.arange(width)[:, None]
    column = np.arange(width)[None, :]
    k, d = column // quarter, m - 4 * (column % quarter)
    factor = np.where(k == 0, 0.5, np.sqrt(0.5))
    entries = factor * np.cos(np.pi * (2 * np.clip(d, 0, 3) + 1) * k / 8)
    return np.where((d >= 0) & (d < 4), entries, 0.0).astype(np.float32)


def split_matrix(width):
    full = brick_matrix(width)
    high = full.astype(jnp.bfloat16)
    low = (full - high.astype(np.float32)).astype(jnp.bfloat16)
    return np.block([[high, low], [high, np.zeros_like(low)]]).astype(jnp.bfloat16)


def pack_kernel(density, momentum, energy, first_x, last_x, first_y, last_y, tl, tr, bl, br):
    depth, y, width = density.shape
    quarter = y // 4
    planes = [density.at[z] for z in range(depth)]
    planes += [momentum.at[f, z] for f in range(3) for z in range(depth)]
    planes += [energy.at[z] for z in range(depth)]
    lane = lanes_of((y, width))
    first = jnp.zeros((y, width), jnp.float32)
    last = jnp.zeros((y, width), jnp.float32)
    for j, plane in enumerate(planes):
        value = plane[...]
        first = jnp.where(lane == j, pltpu.roll(value, j, 1) if j else value, first)
        last = jnp.where(lane == j, pltpu.roll(value, j + 1, 1), last)
        first_y[4 * j : 4 * j + 4, :] = plane[0:4, :]
        last_y[4 * j : 4 * j + 4, :] = plane[y - 4 : y, :]
    for column, out in ((first, first_x), (last, last_x)):
        packed = column[0:quarter]
        for c in range(1, 4):
            packed = packed + pltpu.roll(column[c * quarter : (c + 1) * quarter], 32 * c, 1)
        out[...] = packed
    tl[...] = first[0:8]
    tr[...] = last[0:8]
    bl[...] = first[y - 8 : y]
    br[...] = last[y - 8 : y]


def pack(density, momentum, energy):
    depth, y, width = density.shape
    rows = 4 * FIELDS * depth
    shapes = [(y // 4, width)] * 2 + [(rows, width)] * 2 + [(8, width)] * 4
    return pl.pallas_call(
        pack_kernel,
        out_shape=[jax.ShapeDtypeStruct(s, jnp.float32) for s in shapes],
        in_specs=[vmem()] * 3,
        out_specs=[vmem()] * 8,
        compiler_params=pltpu.CompilerParams(vmem_limit_bytes=VMEM_LIMIT),
    )(density, momentum, energy)


def fluxes(c):
    rho, mx, my, mz, e = c
    inverse = 1.0 / rho
    u, v = mx * inverse, my * inverse
    pressure = GAMMA_LESS * (e - 0.5 * (mx * mx + my * my + mz * mz) * inverse)
    total = e + pressure
    flux_x = (mx, mx * u + pressure, my * u, mz * u, total * u)
    flux_y = (my, mx * v, my * v + pressure, mz * v, total * v)
    return flux_x, flux_y


def partner_of(me, k, count):
    if count & (count - 1) == 0:
        return me ^ k
    return lax.rem(me + k, count)


def main_kernel(count, groups, *refs):
    (density, momentum, energy, top, bottom, left, right, tl, tr, bl, br, membership, slots, matrix), refs = refs[:14], refs[14:]
    outs, peaks, refs = refs[:count], refs[count], refs[count + 1 :]
    pad, across, down, up, edges, folded, split, coefficients, staged, blocks, packed, table, sems = refs
    depth, y, width = density.shape
    nb, quarter = y // 4, y // 4
    rows = y // count
    tall = y + 2 * PAD
    copies = []
    sources = [density, momentum.at[0], momentum.at[1], momentum.at[2], energy]
    for f, source in enumerate(sources):
        copies.append(
            pltpu.make_async_copy(source, pad.at[pl.ds(f * depth, depth), pl.ds(PAD, y), :], sems.at[f])
        )
    for copy in copies:
        copy.start()
    for j in range(FIELDS * depth):
        pad[j, PAD - 4 : PAD, :] = top[4 * j : 4 * j + 4, :]
        pad[j, PAD + y : PAD + y + 4, :] = bottom[4 * j : 4 * j + 4, :]
        pad[j, 0:4, :] = jnp.ones((4, width), jnp.float32)
        pad[j, PAD + y + 4 : tall, :] = jnp.ones((4, width), jnp.float32)

    for side, (column, above, below) in enumerate(((left, tl, bl), (right, tr, br))):
        parts = [above[...]]
        for c in range(4):
            value = column[...]
            parts.append(pltpu.roll(value, LANES - 32 * c, 1) if c else value)
        parts.append(below[...])
        own = jnp.concatenate(parts, axis=0)
        fields = [pltpu.roll(own, LANES - depth * f, 1) if f else own for f in range(FIELDS)]
        flux_x, unused = fluxes(fields)
        sign = COURANT if side == 0 else -COURANT
        for f in range(FIELDS):
            edges[side, f] = DIFFUSE * fields[f] + sign * flux_x[f]

    for copy in copies:
        copy.wait()

    step = 16
    lane = lanes_of((step, width))
    is_first, is_last = lane == 0, lane == width - 1

    def flux_rows(i, carry):
        r = pl.ds(pl.multiple_of(i * step, step), step)
        low = [edges[0, f, r, :] for f in range(FIELDS)]
        high = [edges[1, f, r, :] for f in range(FIELDS)]
        for z in range(depth):
            c = [pad[f * depth + z, r, :] for f in range(FIELDS)]
            flux_x, flux_y = fluxes(c)
            for f in range(FIELDS):
                j = f * depth + z
                base = DIFFUSE * c[f]
                gx, gy = COURANT * flux_x[f], COURANT * flux_y[f]
                from_left = pltpu.roll(base + gx, 1, 1)
                from_right = pltpu.roll(base - gx, width - 1, 1)
                at_left = pltpu.roll(low[f], LANES - z, 1) if z else low[f]
                at_right = pltpu.roll(high[f], LANES - 1 - z, 1)
                across[j, r, :] = (
                    (1.0 - 4.0 * DIFFUSE) * c[f]
                    + jnp.where(is_first, at_left, from_left)
                    + jnp.where(is_last, at_right, from_right)
                )
                down[j, r, :] = base + gy
                up[j, r, :] = base - gy
        return carry

    lax.fori_loop(0, tall // step, flux_rows, 0)

    def predict_rows(j, carry):
        t = {}
        for o in range(-3, 7):
            t[o] = (
                across[j, pl.ds(PAD + o, nb, stride=4), :]
                + down[j, pl.ds(PAD + o - 1, nb, stride=4), :]
                + up[j, pl.ds(PAD + o + 1, nb, stride=4), :]
            )
        residual = [
            t[m] - (9.0 / 16.0) * (t[m - 1] + t[m + 1]) + (1.0 / 16.0) * (t[m - 3] + t[m + 3])
            for m in range(4)
        ]
        for k, value in enumerate(butterfly(*residual)):
            folded[j, k * nb : (k + 1) * nb, :] = value
        return carry

    lax.fori_loop(0, FIELDS * depth, predict_rows, 0)

    piece = 32

    def transform_field(f, carry):
        for start in range(0, y, piece):
            planes = [folded[f * depth + z, start : start + piece, :] for z in range(4)]
            for k, value in enumerate(butterfly(*planes)):
                high = value.astype(jnp.bfloat16)
                low = (value - high.astype(jnp.float32)).astype(jnp.bfloat16)
                split[k * y + start : k * y + start + piece, 0:width] = high
                split[k * y + start : k * y + start + piece, width : 2 * width] = low
        product = jnp.dot(split[...], matrix[...], preferred_element_type=jnp.float32)
        result = product[:, 0:width] + product[:, width : 2 * width]
        peak = None
        for k in range(4):
            for m in range(4):
                value = result[k * y + m * nb : k * y + (m + 1) * nb]
                coefficients[f * depth + k, pl.ds(m, nb, stride=4), :] = value
                size = jnp.abs(value)
                peak = size if peak is None else jnp.maximum(peak, size)
        peak = jnp.maximum(peak, pltpu.roll(peak, 64, 1))
        blocks[f] = jnp.maximum(peak, pltpu.roll(peak, 32, 1))
        return carry

    lax.fori_loop(0, FIELDS, transform_field, 0)

    me = lax.axis_index("section")
    if rows % 8 == 0:
        for k in range(count):
            p = partner_of(me, k, count)
            for j in range(FIELDS * depth):
                outs[k][j // depth, j % depth] = coefficients[j, pl.ds(pl.multiple_of(p * rows, 8), rows), :]
    else:
        for p in range(count):
            staged[p] = coefficients[:, p * rows : (p + 1) * rows, :]
        for k in range(count):
            p = partner_of(me, k, count)
            for j in range(FIELDS * depth):
                outs[k][j // depth, j % depth] = staged[p, j]

    slot = slots[0, me]
    tile = membership[:, pl.ds(pl.multiple_of(lax.div(slot, 4) * LANES, LANES), LANES)]
    within = lax.rem(slot, 4) * 32
    sixth = nb // 4
    band = lax.div(lanes_of((sixth, LANES)), 32)
    labels = jnp.zeros((sixth, LANES), jnp.int32)
    for c in range(4):
        turned = pltpu.roll(tile, lax.rem(32 * c - within + LANES, LANES), 1)
        labels = jnp.where(band == c, turned[c * sixth : (c + 1) * sixth], labels)
    for f in range(FIELDS):
        own = jnp.zeros((sixth, LANES), jnp.float32)
        for c in range(4):
            own = jnp.where(band == c, blocks[f, c * sixth : (c + 1) * sixth, :], own)
        packed[f, 0:sixth, :] = own
    lane8 = lanes_of((8, LANES))
    sub8 = lax.broadcasted_iota(jnp.int32, (8, LANES), 0)
    label_rows = [jnp.broadcast_to(labels[r : r + 1], (8, LANES)) for r in range(sixth)]

    def group_tile(g, carry):
        wanted = sub8 + g * 8
        matches = [label_rows[r] == wanted for r in range(sixth)]
        found = jnp.zeros((8, LANES), jnp.float32)
        for f in range(FIELDS):
            best = jnp.zeros((8, LANES), jnp.float32)
            for r in range(sixth):
                row = jnp.broadcast_to(packed[f, r : r + 1, :], (8, LANES))
                best = jnp.maximum(best, jnp.where(matches[r], row, 0.0))
            found = jnp.where(lane8 == f, jnp.max(best, axis=1, keepdims=True), found)
        table[pl.ds(pl.multiple_of(g * 8, 8), 8), :] = found
        return carry

    high = table.shape[0]
    if groups < high:
        table[...] = jnp.zeros((high, LANES), jnp.float32)
    lax.fori_loop(0, pl.cdiv(groups, 8), group_tile, 0)
    for g in range(high // LANES):
        peaks[:, g * LANES : (g + 1) * LANES] = jnp.transpose(table[g * LANES : (g + 1) * LANES, :])[0:8]


def transform_bricks(count, groups, density, momentum, energy, halos, membership, slots):
    depth, y, width = density.shape
    rows = y // count
    planes, tall = FIELDS * depth, y + 2 * PAD
    high = pl.cdiv(groups, LANES) * LANES
    matrix = jnp.asarray(split_matrix(width))
    chunk = jax.ShapeDtypeStruct((FIELDS, depth, rows, width), jnp.float32)
    hbm = pl.BlockSpec(memory_space=pl.ANY)
    results = pl.pallas_call(
        functools.partial(main_kernel, count, groups),
        out_shape=[chunk] * count + [jax.ShapeDtypeStruct((8, high), jnp.float32)],
        in_specs=[hbm] * 3 + [vmem()] * 8 + [vmem(), smem(), vmem()],
        out_specs=[vmem()] * (count + 1),
        scratch_shapes=[
            pltpu.VMEM((planes, tall, width), jnp.float32),
            pltpu.VMEM((planes, tall, width), jnp.float32),
            pltpu.VMEM((planes, tall, width), jnp.float32),
            pltpu.VMEM((planes, tall, width), jnp.float32),
            pltpu.VMEM((2, FIELDS, tall, width), jnp.float32),
            pltpu.VMEM((planes, y, width), jnp.float32),
            pltpu.VMEM((depth * y, 2 * width), jnp.bfloat16),
            pltpu.VMEM((planes, y, width), jnp.float32),
            pltpu.VMEM((1, 1, 8, LANES) if rows % 8 == 0 else (count, planes, rows, width), jnp.float32),
            pltpu.VMEM((FIELDS, y // 4, width), jnp.float32),
            pltpu.VMEM((FIELDS, 8, LANES), jnp.float32),
            pltpu.VMEM((high, LANES), jnp.float32),
            pltpu.SemaphoreType.DMA((FIELDS,)),
        ],
        compiler_params=pltpu.CompilerParams(vmem_limit_bytes=VMEM_LIMIT),
    )(density, momentum, energy, *halos, membership, slots, matrix)
    return results[:count], results[count]


def scale_kernel(count, groups, *refs):
    chunks, (peaks, membership, slots, coded, group_peak, labels, wide) = refs[:count], refs[count:]
    fields, depth, rows, width = chunks[0].shape
    nb = rows // 4
    high = peaks.shape[1]
    me = lax.axis_index("section")
    group_peak[...] = peaks[0:fields, 0:groups]
    labels[...] = jnp.zeros(labels.shape, jnp.int32)
    labels[0:nb, :] = membership[...]
    lane = lanes_of((8, LANES))
    inverse = 1.0 / (peaks[...] + EPSILON)
    tables = [
        [jnp.broadcast_to(inverse[f : f + 1, g * LANES : (g + 1) * LANES], (8, LANES)) for g in range(high // LANES)]
        for f in range(fields)
    ]
    for k in range(count):
        slot = slots[0, partner_of(me, k, count) if k == 0 or count & (count - 1) == 0 else lax.rem(me - k + count, count)]
        tile = labels[:, pl.ds(pl.multiple_of(lax.div(slot, 4) * LANES, LANES), LANES)]
        within = lax.rem(slot, 4) * 32 + lax.rem(lane, 32)
        own = jnp.take_along_axis(tile, within, axis=1)
        place = pl.ds(pl.multiple_of(slot * width, width), width)
        for f in range(fields):
            if high == LANES:
                found = jnp.take_along_axis(tables[f][0], own, axis=1)
            else:
                found = jnp.zeros((8, LANES), jnp.float32)
                inside = lax.rem(own, LANES)
                for g in range(high // LANES):
                    here = jnp.take_along_axis(tables[f][g], inside, axis=1)
                    found = jnp.where(lax.div(own, LANES) == g, here, found)
            for m in range(4):
                wide[k, f, pl.ds(m, nb, stride=4), :] = found[0:nb]
            factor = wide[k, f]
            for z in range(depth):
                coded[f, z, :, place] = chunks[k][f, z] * factor


def scale(count, groups, chunks, peaks, membership, slots):
    fields, depth, rows, width = chunks[0].shape
    return pl.pallas_call(
        functools.partial(scale_kernel, count, groups),
        out_shape=[
            jax.ShapeDtypeStruct((fields, depth, rows, width * count), jnp.float32),
            jax.ShapeDtypeStruct((fields, groups), jnp.float32),
        ],
        in_specs=[vmem()] * (count + 2) + [smem()],
        out_specs=[vmem()] * 2,
        scratch_shapes=[
            pltpu.VMEM((8, membership.shape[1]), jnp.int32),
            pltpu.VMEM((count, fields, rows, width), jnp.float32),
        ],
        compiler_params=pltpu.CompilerParams(vmem_limit_bytes=VMEM_LIMIT),
    )(*chunks, peaks, membership, slots)


def ring(axis, shift):
    count = lax.axis_size(axis)
    return [(i, (i + shift) % count) for i in range(count)]


def diagonal(sim_shift, section_shift):
    n_sim, n_section = lax.axis_size("sim"), lax.axis_size("section")
    return [
        (s * n_section + b, (s + sim_shift) % n_sim * n_section + (b + section_shift) % n_section)
        for s in range(n_sim)
        for b in range(n_section)
    ]


def exchange_pairs(count, k):
    if count & (count - 1) == 0:
        return [(i, i ^ k) for i in range(count)]
    return [(i, (i + k) % count) for i in range(count)]


def largest(value, axis):
    count = lax.axis_size(axis)
    span = 1
    while span < count:
        shift = min(span, count - span)
        value = jnp.maximum(value, lax.ppermute(value, axis, exchange_pairs(count, shift)))
        span += shift
    return value


def per_device(density, momentum, energy, membership, slot_of_brick):
    count = lax.axis_size("section")
    groups = 2 * lax.axis_size("sim") * count
    slab_membership = lax.all_gather(membership, "section", axis=0, tiled=True)
    first_x, last_x, first_y, last_y, tl, tr, bl, br = pack(density, momentum, energy)
    both = ("sim", "section")
    halos = (
        lax.ppermute(last_y, "sim", ring("sim", 1)),
        lax.ppermute(first_y, "sim", ring("sim", -1)),
        lax.ppermute(last_x, "section", ring("section", 1)),
        lax.ppermute(first_x, "section", ring("section", -1)),
        lax.ppermute(br, both, diagonal(1, 1)),
        lax.ppermute(bl, both, diagonal(1, -1)),
        lax.ppermute(tr, both, diagonal(-1, 1)),
        lax.ppermute(tl, both, diagonal(-1, -1)),
    )
    chunks, peaks = transform_bricks(count, groups, density, momentum, energy, halos, slab_membership, slot_of_brick)
    moved = [chunks[0]] + [
        lax.ppermute(chunks[k], "section", exchange_pairs(count, k)) for k in range(1, count)
    ]
    peaks = largest(largest(peaks, "section"), "sim")
    return tuple(scale(count, groups, moved, peaks, membership, slot_of_brick))


def solution(mesh):
    placed = (
        P(None, "sim", "section"),
        P(None, None, "sim", "section"),
        P(None, "sim", "section"),
        P(("sim", "section"), None),
        P("sim", None),
    )
    return jax.shard_map(
        per_device,
        mesh=mesh,
        in_specs=placed,
        out_specs=(P(None, None, ("sim", "section"), None), P()),
        check_vma=False,
    )
```

```python
import functools

import jax
import jax.numpy as jnp
import numpy as np
from jax import lax
from jax.experimental import pallas as pl
from jax.experimental.pallas import tpu as pltpu
from jax.sharding import PartitionSpec as P

GAMMA_LESS = 0.4
COURANT = 0.05
DIFFUSE = 0.1
EPSILON = 1e-06
FIELDS = 5
PAD = 8
COLUMN_ROWS = 8
LANES = 128
EVEN = 0.5
WIDE = float(np.sqrt(0.5) * np.cos(np.pi / 8))
NARROW = float(np.sqrt(0.5) * np.cos(3 * np.pi / 8))
VMEM_LIMIT = 48 * 1024 * 1024


def vmem():
    return pl.BlockSpec(memory_space=pltpu.VMEM)


def smem():
    return pl.BlockSpec(memory_space=pltpu.SMEM)


def lanes_of(shape):
    return lax.broadcasted_iota(jnp.int32, shape, 1)


def butterfly(a, b, c, d):
    s, t, u, v = a + d, b + c, a - d, b - c
    return (
        EVEN * (s + t),
        WIDE * u + NARROW * v,
        EVEN * (s - t),
        NARROW * u - WIDE * v,
    )


def brick_matrix(width):
    quarter = width // 4
    m = np.arange(width)[:, None]
    column = np.arange(width)[None, :]
    k, d = column // quarter, m - 4 * (column % quarter)
    factor = np.where(k == 0, 0.5, np.sqrt(0.5))
    entries = factor * np.cos(np.pi * (2 * np.clip(d, 0, 3) + 1) * k / 8)
    return np.where((d >= 0) & (d < 4), entries, 0.0).astype(np.float32)


def split_matrix(width):
    full = brick_matrix(width)
    high = full.astype(jnp.bfloat16)
    low = (full - high.astype(np.float32)).astype(jnp.bfloat16)
    return np.block([[high, low], [high, np.zeros_like(low)]]).astype(jnp.bfloat16)


def hbm():
    return pl.BlockSpec(memory_space=pltpu.HBM)


def kernel_params():
    return pltpu.CompilerParams(vmem_limit_bytes=VMEM_LIMIT)


def array(shape, dtype=jnp.float32):
    return jax.ShapeDtypeStruct(shape, dtype)


def pack_kernel(density, momentum, energy, membership, entries, planes, matrix, first_x, last_x, labels, held, sems):
    count, y, width = planes.shape
    depth = density.shape[0]
    quarter = y // 4
    copies = [pltpu.make_async_copy(membership, held, sems.at[FIELDS])]
    sources = [density, momentum.at[0], momentum.at[1], momentum.at[2], energy]
    for f, source in enumerate(sources):
        copies.append(pltpu.make_async_copy(source, planes.at[pl.ds(f * depth, depth)], sems.at[f]))
    for copy in copies:
        copy.start()
    matrix[...] = entries[...].astype(jnp.bfloat16)
    for copy in copies:
        copy.wait()
    lane = lanes_of((y, width))
    first = jnp.zeros((y, width), jnp.float32)
    last = jnp.zeros((y, width), jnp.float32)
    for j in range(count):
        value = planes[j]
        first = jnp.where(lane == j, pltpu.roll(value, j, 1) if j else value, first)
        last = jnp.where(lane == j, pltpu.roll(value, j + 1, 1), last)
    own_rows, own_columns = held.shape
    labels[...] = jnp.zeros(labels.shape, jnp.float32)
    for t in range(own_columns // LANES):
        part = held[:, t * LANES : (t + 1) * LANES].astype(jnp.float32)
        labels[t * own_rows : (t + 1) * own_rows, :] = part
    for column, out in ((first, first_x), (last, last_x)):
        packed = column[0:quarter]
        for c in range(1, 4):
            packed = packed + pltpu.roll(column[c * quarter : (c + 1) * quarter], 32 * c, 1)
        out[0:quarter, :] = packed
        out[quarter:, :] = labels[...]


def pack(density, momentum, energy, membership):
    depth, y, width = density.shape
    rows, columns = membership.shape
    label_rows = pl.cdiv(rows * columns // LANES, 8) * 8
    entries = jnp.asarray(split_matrix(width).astype(np.float32))
    shapes = [
        array((FIELDS * depth, y, width)),
        array(entries.shape, jnp.bfloat16),
        array((y // 4 + label_rows, width)),
        array((y // 4 + label_rows, width)),
        array((label_rows, width)),
    ]
    return pl.pallas_call(
        pack_kernel,
        out_shape=shapes,
        in_specs=[hbm()] * 4 + [vmem()],
        out_specs=[vmem()] * 5,
        scratch_shapes=[pltpu.VMEM((rows, columns), jnp.int32), pltpu.SemaphoreType.DMA((FIELDS + 1,))],
        compiler_params=kernel_params(),
    )(density, momentum, energy, membership, entries)


def fluxes(c):
    rho, mx, my, mz, e = c
    inverse = 1.0 / rho
    u, v = mx * inverse, my * inverse
    pressure = GAMMA_LESS * (e - 0.5 * (mx * mx + my * my + mz * mz) * inverse)
    total = e + pressure
    flux_x = (mx, mx * u + pressure, my * u, mz * u, total * u)
    flux_y = (my, mx * v, my * v + pressure, mz * v, total * v)
    return flux_x, flux_y


def column_terms(own, depth, sign):
    fields = [pltpu.roll(own, LANES - depth * f, 1) if f else own for f in range(FIELDS)]
    flux_x, unused = fluxes(fields)
    return [DIFFUSE * fields[f] + sign * flux_x[f] for f in range(FIELDS)]


def row_terms(c, low, high, z):
    rows, width = c[0].shape
    lane = lanes_of((rows, width))
    flux_x, flux_y = fluxes(c)
    terms = []
    for f in range(FIELDS):
        base = DIFFUSE * c[f]
        gx, gy = COURANT * flux_x[f], COURANT * flux_y[f]
        from_left = pltpu.roll(base + gx, 1, 1)
        from_right = pltpu.roll(base - gx, width - 1, 1)
        at_left = pltpu.roll(low[f], LANES - z, 1) if z else low[f]
        at_right = pltpu.roll(high[f], LANES - 1 - z, 1)
        across = (
            (1.0 - 4.0 * DIFFUSE) * c[f]
            + jnp.where(lane == 0, at_left, from_left)
            + jnp.where(lane == width - 1, at_right, from_right)
        )
        terms.append((across, base + gy, base - gy))
    return terms


def fold_rows(across, down, up, j, origin, number, stride):
    t = {}
    for o in range(-3, 7):
        t[o] = (
            across[j, pl.ds(origin + o, number, stride=stride), :]
            + down[j, pl.ds(origin + o - 1, number, stride=stride), :]
            + up[j, pl.ds(origin + o + 1, number, stride=stride), :]
        )
    residual = [
        t[m] - (9.0 / 16.0) * (t[m - 1] + t[m + 1]) + (1.0 / 16.0) * (t[m - 3] + t[m + 3])
        for m in range(4)
    ]
    return butterfly(*residual)


def halves(value):
    high = value.astype(jnp.bfloat16)
    return high, (value - high.astype(jnp.float32)).astype(jnp.bfloat16)


def over_lanes(peak):
    peak = jnp.maximum(peak, pltpu.roll(peak, 64, 1))
    return jnp.maximum(peak, pltpu.roll(peak, 32, 1))


def partner_of(me, k, count):
    if count & (count - 1) == 0:
        return me ^ k
    return lax.rem(me + k, count)


def sender_of(me, k, count):
    if count & (count - 1) == 0:
        return me ^ k
    return lax.rem(me - k + count, count)


def brick_kernel(count, *refs):
    planes, left, right, matrix = refs[:4]
    outs, refs = refs[4 : 4 + count], refs[4 + count :]
    first_y, last_y, blocks, rim_a, rim_d, rim_u, across, down, up, edges, folded, split, coefficients, staged = refs
    total, y, width = planes.shape
    depth = total // FIELDS
    nb, quarter = y // 4, y // 4
    rows = y // count

    for side, column in enumerate((left, right)):
        parts = []
        for c in range(4):
            value = column[0:quarter, :]
            parts.append(pltpu.roll(value, LANES - 32 * c, 1) if c else value)
        own = jnp.concatenate(parts, axis=0)
        for f, value in enumerate(column_terms(own, depth, COURANT if side == 0 else -COURANT)):
            edges[side, f] = value
        place = 4 * total + 4 * side
        first_y[place : place + 4, :] = own[0:4]
        last_y[place : place + 4, :] = own[y - 4 : y]
    for j in range(total):
        first_y[4 * j : 4 * j + 4, :] = planes[j, 0:4, :]
        last_y[4 * j : 4 * j + 4, :] = planes[j, y - 4 : y, :]

    step = 16

    def flux_rows(i, carry):
        r = pl.ds(pl.multiple_of(i * step, step), step)
        padded = pl.ds(pl.multiple_of(i * step + PAD, PAD), step)
        low = [edges[0, f, r, :] for f in range(FIELDS)]
        high = [edges[1, f, r, :] for f in range(FIELDS)]
        for z in range(depth):
            c = [planes[f * depth + z, r, :] for f in range(FIELDS)]
            for f, (a, d, u) in enumerate(row_terms(c, low, high, z)):
                j = f * depth + z
                across[j, padded, :] = a
                down[j, padded, :] = d
                up[j, padded, :] = u
        return carry

    lax.fori_loop(0, y // step, flux_rows, 0)

    def predict_rows(j, carry):
        for k, value in enumerate(fold_rows(across, down, up, j, PAD, nb, 4)):
            folded[j, k * nb : (k + 1) * nb, :] = value
        for source, rim in ((across, rim_a), (down, rim_d), (up, rim_u)):
            rim[j, 0:8, :] = source[j, PAD : PAD + 8, :]
            rim[j, 8:16, :] = source[j, y : y + 8, :]
        return carry

    lax.fori_loop(0, total, predict_rows, 0)

    piece = 32

    def transform_field(f, carry):
        for start in range(0, y, piece):
            values = [folded[f * depth + z, start : start + piece, :] for z in range(4)]
            for k, value in enumerate(butterfly(*values)):
                high, low = halves(value)
                split[k * y + start : k * y + start + piece, 0:width] = high
                split[k * y + start : k * y + start + piece, width : 2 * width] = low
        product = jnp.dot(split[...], matrix[...], preferred_element_type=jnp.float32)
        result = product[:, 0:width] + product[:, width : 2 * width]
        peak = None
        for k in range(4):
            for m in range(4):
                value = result[k * y + m * nb : k * y + (m + 1) * nb]
                coefficients[f * depth + k, pl.ds(m, nb, stride=4), :] = value
                size = jnp.abs(value)
                peak = size if peak is None else jnp.maximum(peak, size)
        blocks[f] = over_lanes(peak)
        return carry

    lax.fori_loop(0, FIELDS, transform_field, 0)

    me = lax.axis_index("section")
    if rows % 8 == 0:
        for k in range(count):
            p = partner_of(me, k, count)
            for j in range(total):
                outs[k][j // depth, j % depth] = coefficients[j, pl.ds(pl.multiple_of(p * rows, 8), rows), :]
    else:
        for p in range(count):
            staged[p] = coefficients[:, p * rows : (p + 1) * rows, :]
        for k in range(count):
            p = partner_of(me, k, count)
            for j in range(total):
                outs[k][j // depth, j % depth] = staged[p, j]


def transform_bricks(count, planes, left, right, matrix):
    total, y, width = planes.shape
    depth = total // FIELDS
    rows, tall = y // count, y + 2 * PAD
    chunk = array((FIELDS, depth, rows, width))
    message = array((4 * total + COLUMN_ROWS, width))
    rim = array((total, 2 * PAD, width))
    results = pl.pallas_call(
        functools.partial(brick_kernel, count),
        out_shape=[chunk] * count + [message] * 2 + [array((FIELDS, y // 4, width))] + [rim] * 3,
        in_specs=[vmem()] * 4,
        out_specs=[vmem()] * (count + 6),
        scratch_shapes=[
            pltpu.VMEM((total, tall, width), jnp.float32),
            pltpu.VMEM((total, tall, width), jnp.float32),
            pltpu.VMEM((total, tall, width), jnp.float32),
            pltpu.VMEM((2, FIELDS, y, width), jnp.float32),
            pltpu.VMEM((total, y, width), jnp.float32),
            pltpu.VMEM((depth * y, 2 * width), jnp.bfloat16),
            pltpu.VMEM((total, y, width), jnp.float32),
            pltpu.VMEM((1, 1, 8, LANES) if rows % 8 == 0 else (count, total, rows, width), jnp.float32),
        ],
        compiler_params=kernel_params(),
    )(planes, left, right, matrix)
    return results[:count], results[count : count + 2], results[count + 2], results[count + 3 :]


def mend_kernel(count, *refs):
    chunks, refs = refs[:count], refs[count:]
    top, bottom, blocks, rim_a, rim_d, rim_u, matrix = refs[:7]
    outs, mended, refs = refs[7 : 7 + count], refs[7 + count], refs[8 + count :]
    halo, columns, across, down, up, folded, split, result, fixed = refs
    fields, depth, rows, width = chunks[0].shape
    total = fields * depth
    nb = blocks.shape[1]

    halo[...] = jnp.ones(halo.shape, jnp.float32)
    columns[...] = jnp.ones(columns.shape, jnp.float32)
    for j in range(total):
        halo[j, 4:8, :] = top[4 * j : 4 * j + 4, :]
        halo[j, 8:12, :] = bottom[4 * j : 4 * j + 4, :]
    for side in range(2):
        place = 4 * total + 4 * side
        columns[side, 4:8, :] = top[place : place + 4, :]
        columns[side, 8:12, :] = bottom[place : place + 4, :]
    low = column_terms(columns[0], depth, COURANT)
    high = column_terms(columns[1], depth, -COURANT)
    for z in range(depth):
        c = [halo[f * depth + z] for f in range(fields)]
        for f, values in enumerate(row_terms(c, low, high, z)):
            j = f * depth + z
            for value, rim, target in zip(values, (rim_a, rim_d, rim_u), (across, down, up)):
                target[j, 0:8, :] = value[0:8]
                target[j, 8:24, :] = rim[j]
                target[j, 24:32, :] = value[8:16]
    for j in range(total):
        for k, value in enumerate(fold_rows(across, down, up, j, PAD, 2, 12)):
            folded[j, 2 * k : 2 * k + 2, :] = value
    for f in range(fields):
        values = butterfly(*[folded[f * depth + z] for z in range(4)])
        for half in range(2):
            both = jnp.concatenate(values[2 * half : 2 * half + 2], axis=0)
            upper, lower = halves(both)
            place = f * 32 + half * 16
            split[place : place + 16, 0:width] = upper
            split[place : place + 16, width : 2 * width] = lower
    product = jnp.dot(split[...], matrix[...], preferred_element_type=jnp.float32)
    result[...] = product[:, 0:width] + product[:, width : 2 * width]
    for j in range(total):
        for side in range(2):
            fixed[side, j] = result[pl.ds(8 * j + side, 4, stride=2), :]
    mended[...] = blocks[...]
    for f in range(fields):
        for side in range(2):
            size = jnp.abs(fixed[side, f * depth])
            for z in range(1, depth):
                size = jnp.maximum(size, jnp.abs(fixed[side, f * depth + z]))
            peak = over_lanes(jnp.max(size, axis=0, keepdims=True))
            row = side * (nb - 1)
            mended[f, row : row + 1, :] = peak

    me = lax.axis_index("section")
    for k in range(count):
        p = partner_of(me, k, count)
        outs[k][...] = chunks[k][...]
        for side, start in ((0, 0), (1, rows - 4)):

            @pl.when(p == side * (count - 1))
            def replace(k=k, side=side, start=start):
                for j in range(total):
                    outs[k][j // depth, j % depth, start : start + 4, :] = fixed[side, j]


def mend(count, chunks, top, bottom, blocks, rims, matrix):
    fields, depth, rows, width = chunks[0].shape
    total = fields * depth
    tall = pltpu.VMEM((total, 4 * PAD, width), jnp.float32)
    results = pl.pallas_call(
        functools.partial(mend_kernel, count),
        out_shape=[array(chunks[0].shape)] * count + [array(blocks.shape)],
        in_specs=[vmem()] * (count + 7),
        out_specs=[vmem()] * (count + 1),
        scratch_shapes=[
            pltpu.VMEM((total, 2 * PAD, width), jnp.float32),
            pltpu.VMEM((2, 2 * PAD, width), jnp.float32),
            tall,
            tall,
            tall,
            pltpu.VMEM((total, 8, width), jnp.float32),
            pltpu.VMEM((8 * total, 2 * width), jnp.bfloat16),
            pltpu.VMEM((8 * total, width), jnp.float32),
            pltpu.VMEM((2, total, 4, width), jnp.float32),
        ],
        compiler_params=kernel_params(),
    )(*chunks, top, bottom, blocks, *rims, matrix)
    return results[:count], results[count]


def group_kernel(count, groups, own_rows, *refs):
    blocks, slots, refs = refs[0], refs[1], refs[2:]
    messages, (peaks, gathered, listed, packed, table) = refs[:count], refs[count:]
    nb = blocks.shape[1]
    me = lax.axis_index("section")
    slot = slots[0, me]
    within = lax.rem(slot, 4) * 32
    tile = lax.div(slot, 4)
    for d, message in enumerate(messages):
        height = gathered.shape[1]
        value = message[message.shape[0] - height :, :]
        if count > 4:
            value = pltpu.roll(value, lax.rem(height - tile * own_rows, height), 0)
        gathered[lax.rem(me + count - d, count)] = value
    for q in range(count):
        listed[q * own_rows : (q + 1) * own_rows, :] = gathered[q, 0:own_rows, :]
    part = nb // 4
    band = lax.div(lanes_of((part, LANES)), 32)
    labels = jnp.zeros((part, LANES), jnp.float32)
    for c in range(4):
        turned = pltpu.roll(listed[c * part : (c + 1) * part, :], lax.rem(32 * c - within + LANES, LANES), 1)
        labels = jnp.where(band == c, turned, labels)
    for f in range(FIELDS):
        own = jnp.zeros((part, LANES), jnp.float32)
        for c in range(4):
            own = jnp.where(band == c, blocks[f, c * part : (c + 1) * part, :], own)
        packed[f, 0:part, :] = own
    lane8 = lanes_of((8, LANES))
    sub8 = lax.broadcasted_iota(jnp.int32, (8, LANES), 0)
    label_rows = [jnp.broadcast_to(labels[r : r + 1], (8, LANES)) for r in range(part)]

    def group_tile(g, carry):
        wanted = (sub8 + g * 8).astype(jnp.float32)
        matches = [label_rows[r] == wanted for r in range(part)]
        found = jnp.zeros((8, LANES), jnp.float32)
        for f in range(FIELDS):
            best = jnp.zeros((8, LANES), jnp.float32)
            for r in range(part):
                row = jnp.broadcast_to(packed[f, r : r + 1, :], (8, LANES))
                best = jnp.maximum(best, jnp.where(matches[r], row, 0.0))
            found = jnp.where(lane8 == f, jnp.max(best, axis=1, keepdims=True), found)
        table[pl.ds(pl.multiple_of(g * 8, 8), 8), :] = found
        return carry

    high = table.shape[0]
    if groups < high:
        table[...] = jnp.zeros((high, LANES), jnp.float32)
    lax.fori_loop(0, pl.cdiv(groups, 8), group_tile, 0)
    for g in range(high // LANES):
        peaks[:, g * LANES : (g + 1) * LANES] = jnp.transpose(table[g * LANES : (g + 1) * LANES, :])[0:8]


def group_maxima(count, groups, own_rows, blocks, slots, messages):
    high = pl.cdiv(groups, LANES) * LANES
    nb = blocks.shape[1]
    return pl.pallas_call(
        functools.partial(group_kernel, count, groups, own_rows),
        out_shape=array((8, high)),
        in_specs=[vmem(), smem()] + [vmem()] * count,
        out_specs=vmem(),
        scratch_shapes=[
            pltpu.VMEM((count, messages[0].shape[0], LANES), jnp.float32),
            pltpu.VMEM((nb, LANES), jnp.float32),
            pltpu.VMEM((FIELDS, 8, LANES), jnp.float32),
            pltpu.VMEM((high, LANES), jnp.float32),
        ],
        compiler_params=kernel_params(),
    )(blocks, slots, *messages)


def scale_kernel(count, groups, *refs):
    outer, inner, refs = refs[:count], refs[count : 2 * count - 2], refs[2 * count - 2 :]
    peaks, membership, slots, coded, group_peak, labels, wide = refs
    fields, depth, rows, width = outer[0].shape
    nb = rows // 4
    high = peaks.shape[1]
    me = lax.axis_index("section")
    is_inner = jnp.logical_and(me > 0, me < count - 1)
    group_peak[...] = peaks[0:fields, 0:groups]
    labels[...] = jnp.zeros(labels.shape, jnp.int32)
    labels[0:nb, :] = membership[...]
    lane = lanes_of((8, LANES))
    inverse = 1.0 / (peaks[...] + EPSILON)
    tables = [
        [jnp.broadcast_to(inverse[f : f + 1, g * LANES : (g + 1) * LANES], (8, LANES)) for g in range(high // LANES)]
        for f in range(fields)
    ]
    for k in range(count):
        slot = slots[0, sender_of(me, k, count)]
        tile = labels[:, pl.ds(pl.multiple_of(lax.div(slot, 4) * LANES, LANES), LANES)]
        within = lax.rem(slot, 4) * 32 + lax.rem(lane, 32)
        own = jnp.take_along_axis(tile, within, axis=1)
        place = pl.ds(pl.multiple_of(slot * width, width), width)
        for f in range(fields):
            if high == LANES:
                found = jnp.take_along_axis(tables[f][0], own, axis=1)
            else:
                found = jnp.zeros((8, LANES), jnp.float32)
                inside = lax.rem(own, LANES)
                for g in range(high // LANES):
                    here = jnp.take_along_axis(tables[f][g], inside, axis=1)
                    found = jnp.where(lax.div(own, LANES) == g, here, found)
            for m in range(4):
                wide[k, f, pl.ds(m, nb, stride=4), :] = found[0:nb]
            factor = wide[k, f]
            for z in range(depth):
                value = outer[k][f, z]
                if k >= 2:
                    value = jnp.where(is_inner, inner[k - 2][f, z], value)
                coded[f, z, :, place] = value * factor


def scale(count, groups, outer, inner, peaks, membership, slots):
    fields, depth, rows, width = outer[0].shape
    return pl.pallas_call(
        functools.partial(scale_kernel, count, groups),
        out_shape=[array((fields, depth, rows, width * count)), array((fields, groups))],
        in_specs=[vmem()] * (2 * count) + [smem()],
        out_specs=[vmem()] * 2,
        scratch_shapes=[
            pltpu.VMEM((8, membership.shape[1]), jnp.int32),
            pltpu.VMEM((count, fields, rows, width), jnp.float32),
        ],
        compiler_params=kernel_params(),
    )(*outer, *inner, peaks, membership, slots)


def ring(axis, shift):
    count = lax.axis_size(axis)
    return [(i, (i + shift) % count) for i in range(count)]


def exchange_pairs(count, k):
    if count & (count - 1) == 0:
        return [(i, i ^ k) for i in range(count)]
    return [(i, (i + k) % count) for i in range(count)]


def inner_pairs(count, k):
    return [(i, p) for i, p in exchange_pairs(count, k) if 0 < p < count - 1]


def outer_pairs(count, k):
    return [(i, p) for i, p in exchange_pairs(count, k) if p in (0, count - 1)]


def largest(value, axis):
    count = lax.axis_size(axis)
    if count <= 4:
        others = [lax.ppermute(value, axis, exchange_pairs(count, k)) for k in range(1, count)]
        return functools.reduce(jnp.maximum, others, value)
    span = 1
    while span < count:
        shift = min(span, count - span)
        value = jnp.maximum(value, lax.ppermute(value, axis, exchange_pairs(count, shift)))
        span += shift
    return value


def per_device(density, momentum, energy, membership, slot_of_brick):
    count = lax.axis_size("section")
    groups = 2 * lax.axis_size("sim") * count
    planes, matrix, first_x, last_x, labels = pack(density, momentum, energy, membership)
    left = lax.ppermute(last_x, "section", ring("section", 1))
    right = lax.ppermute(first_x, "section", ring("section", -1))
    messages = [labels, left]
    messages += [lax.ppermute(labels, "section", ring("section", d)) for d in range(2, count - 1)]
    messages.append(right)
    chunks, (first_y, last_y), blocks, rims = transform_bricks(count, planes, left, right, matrix)
    inner = [lax.ppermute(chunks[k], "section", inner_pairs(count, k)) for k in range(2, count)]
    top = lax.ppermute(last_y, "sim", ring("sim", 1))
    bottom = lax.ppermute(first_y, "sim", ring("sim", -1))
    chunks, blocks = mend(count, chunks, top, bottom, blocks, rims, matrix)
    outer = [chunks[0], lax.ppermute(chunks[1], "section", exchange_pairs(count, 1))]
    outer += [lax.ppermute(chunks[k], "section", outer_pairs(count, k)) for k in range(2, count)]
    peaks = group_maxima(count, groups, membership.shape[0], blocks, slot_of_brick, messages)
    peaks = largest(largest(peaks, "sim"), "section")
    return tuple(scale(count, groups, outer, inner, peaks, membership, slot_of_brick))


def solution(mesh):
    placed = (
        P(None, "sim", "section"),
        P(None, None, "sim", "section"),
        P(None, "sim", "section"),
        P(("sim", "section"), None),
        P("sim", None),
    )
    return jax.shard_map(
        per_device,
        mesh=mesh,
        in_specs=placed,
        out_specs=(P(None, None, ("sim", "section"), None), P()),
        check_vma=False,
    )
```

```python
import functools

import jax
import jax.numpy as jnp
import numpy as np
from jax import lax
from jax.experimental import pallas as pl
from jax.experimental.pallas import tpu as pltpu
from jax.sharding import PartitionSpec as P

GAMMA_LESS = 0.4
COURANT = 0.05
DIFFUSE = 0.1
EPSILON = 1e-06
FIELDS = 5
PAD = 8
COLUMN_ROWS = 8
LABEL_ROWS = 8
LANES = 128
EVEN = 0.5
WIDE = float(np.sqrt(0.5) * np.cos(np.pi / 8))
NARROW = float(np.sqrt(0.5) * np.cos(3 * np.pi / 8))
VMEM_LIMIT = 48 * 1024 * 1024


def vmem():
    return pl.BlockSpec(memory_space=pltpu.VMEM)


def lanes_of(shape):
    return lax.broadcasted_iota(jnp.int32, shape, 1)


def butterfly(a, b, c, d):
    s, t, u, v = a + d, b + c, a - d, b - c
    return (
        EVEN * (s + t),
        WIDE * u + NARROW * v,
        EVEN * (s - t),
        NARROW * u - WIDE * v,
    )


def cosine(k, d):
    factor = 0.5 if k == 0 else np.sqrt(0.5)
    return float(factor * np.cos(np.pi * (2 * d + 1) * k / 8))


def write_matrix(matrix, width):
    step = 16
    row = lax.broadcasted_iota(jnp.int32, (step, width), 0)
    column = lanes_of((step, width))
    quarter = width // 4
    k, j, d = lax.div(column, quarter), lax.rem(column, quarter), lax.rem(row, 4)
    entry = jnp.zeros((step, width), jnp.float32)
    for a in range(4):
        for b in range(4):
            entry = jnp.where(jnp.logical_and(k == a, d == b), cosine(a, b), entry)
    high = entry.astype(jnp.bfloat16).astype(jnp.float32)
    low = entry - high
    zero = jnp.zeros((step, width), jnp.bfloat16)
    for start in range(0, width, step):
        own = j == lax.div(row + start, 4)
        upper = jnp.where(own, high, 0.0).astype(jnp.bfloat16)
        lower = jnp.where(own, low, 0.0).astype(jnp.bfloat16)
        matrix[start : start + step, 0:width] = upper
        matrix[start : start + step, width : 2 * width] = lower
        matrix[width + start : width + start + step, 0:width] = upper
        matrix[width + start : width + start + step, width : 2 * width] = zero


def kernel_params():
    return pltpu.CompilerParams(vmem_limit_bytes=VMEM_LIMIT)


def array(shape, dtype=jnp.float32):
    return jax.ShapeDtypeStruct(shape, dtype)


def pack_kernel(y, flat, matrix, first_x, last_x, labels):
    width = flat.shape[1]
    count = flat.shape[0] // y
    quarter = y // 4
    lane = lanes_of((y, width))
    first = jnp.zeros((y, width), jnp.float32)
    last = jnp.zeros((y, width), jnp.float32)
    for j in range(count):
        value = flat[j * y : (j + 1) * y, :]
        first = jnp.where(lane == j, pltpu.roll(value, j, 1) if j else value, first)
        last = jnp.where(lane == j, pltpu.roll(value, j + 1, 1), last)
    own = flat[count * y :, :]
    labels[...] = own
    for column, out in ((first, first_x), (last, last_x)):
        packed = column[0:quarter]
        for c in range(1, 4):
            packed = packed + pltpu.roll(column[c * quarter : (c + 1) * quarter], 32 * c, 1)
        out[0:quarter, :] = packed
        out[quarter:, :] = own
    write_matrix(matrix, width)


def flatten(density, momentum, energy, membership, slots):
    width = density.shape[2]
    rows, columns = membership.shape
    labels = membership.reshape(rows, columns // LANES, LANES).swapaxes(0, 1).reshape(-1, LANES)
    spare = LABEL_ROWS - 1 - labels.shape[0]
    labels = jnp.pad(labels, ((0, spare), (0, 0)))
    slots = jnp.pad(slots, ((0, 0), (0, LANES - slots.shape[1])))
    parts = [density.reshape(-1, width), momentum.reshape(-1, width), energy.reshape(-1, width)]
    parts += [labels.astype(jnp.float32), slots.astype(jnp.float32)]
    return jnp.concatenate(parts, axis=0)


def pack(flat, y):
    width = flat.shape[1]
    shapes = [
        array((2 * width, 2 * width), jnp.bfloat16),
        array((y // 4 + LABEL_ROWS, width)),
        array((y // 4 + LABEL_ROWS, width)),
        array((LABEL_ROWS, width)),
    ]
    return pl.pallas_call(
        functools.partial(pack_kernel, y),
        out_shape=shapes,
        in_specs=[vmem()],
        out_specs=[vmem()] * 4,
        compiler_params=kernel_params(),
    )(flat)


def slot_of(labels, brick):
    row = labels[LABEL_ROWS - 1 : LABEL_ROWS, :]
    return jnp.max(jnp.where(lanes_of(row.shape) == brick, row, 0.0)).astype(jnp.int32)


def fluxes(c):
    rho, mx, my, mz, e = c
    inverse = 1.0 / rho
    u, v = mx * inverse, my * inverse
    pressure = GAMMA_LESS * (e - 0.5 * (mx * mx + my * my + mz * mz) * inverse)
    total = e + pressure
    flux_x = (mx, mx * u + pressure, my * u, mz * u, total * u)
    flux_y = (my, mx * v, my * v + pressure, mz * v, total * v)
    return flux_x, flux_y


def column_terms(own, depth, sign):
    fields = [pltpu.roll(own, LANES - depth * f, 1) if f else own for f in range(FIELDS)]
    flux_x, unused = fluxes(fields)
    return [DIFFUSE * fields[f] + sign * flux_x[f] for f in range(FIELDS)]


def row_terms(c, low, high, z):
    rows, width = c[0].shape
    lane = lanes_of((rows, width))
    flux_x, flux_y = fluxes(c)
    terms = []
    for f in range(FIELDS):
        base = DIFFUSE * c[f]
        gx, gy = COURANT * flux_x[f], COURANT * flux_y[f]
        from_left = pltpu.roll(base + gx, 1, 1)
        from_right = pltpu.roll(base - gx, width - 1, 1)
        at_left = pltpu.roll(low[f], LANES - z, 1) if z else low[f]
        at_right = pltpu.roll(high[f], LANES - 1 - z, 1)
        across = (
            (1.0 - 4.0 * DIFFUSE) * c[f]
            + jnp.where(lane == 0, at_left, from_left)
            + jnp.where(lane == width - 1, at_right, from_right)
        )
        terms.append((across, base + gy, base - gy))
    return terms


def fold_rows(across, down, up, j, origin, number, stride):
    t = {}
    for o in range(-3, 7):
        t[o] = (
            across[j, pl.ds(origin + o, number, stride=stride), :]
            + down[j, pl.ds(origin + o - 1, number, stride=stride), :]
            + up[j, pl.ds(origin + o + 1, number, stride=stride), :]
        )
    residual = [
        t[m] - (9.0 / 16.0) * (t[m - 1] + t[m + 1]) + (1.0 / 16.0) * (t[m - 3] + t[m + 3])
        for m in range(4)
    ]
    return butterfly(*residual)


def halves(value):
    high = value.astype(jnp.bfloat16)
    return high, (value - high.astype(jnp.float32)).astype(jnp.bfloat16)


def over_lanes(peak):
    peak = jnp.maximum(peak, pltpu.roll(peak, 64, 1))
    return jnp.maximum(peak, pltpu.roll(peak, 32, 1))


def partner_of(me, k, count):
    if count & (count - 1) == 0:
        return me ^ k
    return lax.rem(me + k, count)


def sender_of(me, k, count):
    if count & (count - 1) == 0:
        return me ^ k
    return lax.rem(me - k + count, count)


def brick_kernel(count, total, y, *refs):
    flat, left, right, matrix = refs[:4]
    outs, refs = refs[4 : 4 + count], refs[4 + count :]
    first_y, last_y, blocks, rim_a, rim_d, rim_u, across, down, up, edges, folded, split, coefficients, staged = refs
    width = flat.shape[1]
    depth = total // FIELDS
    nb, quarter = y // 4, y // 4
    rows = y // count

    for side, column in enumerate((left, right)):
        parts = []
        for c in range(4):
            value = column[0:quarter, :]
            parts.append(pltpu.roll(value, LANES - 32 * c, 1) if c else value)
        own = jnp.concatenate(parts, axis=0)
        for f, value in enumerate(column_terms(own, depth, COURANT if side == 0 else -COURANT)):
            edges[side, f] = value
        place = 4 * total + 4 * side
        first_y[place : place + 4, :] = own[0:4]
        last_y[place : place + 4, :] = own[y - 4 : y]
    for j in range(total):
        first_y[4 * j : 4 * j + 4, :] = flat[j * y : j * y + 4, :]
        last_y[4 * j : 4 * j + 4, :] = flat[(j + 1) * y - 4 : (j + 1) * y, :]

    step = 16

    def flux_rows(i, carry):
        r = pl.ds(pl.multiple_of(i * step, step), step)
        padded = pl.ds(pl.multiple_of(i * step + PAD, PAD), step)
        low = [edges[0, f, r, :] for f in range(FIELDS)]
        high = [edges[1, f, r, :] for f in range(FIELDS)]
        for z in range(depth):
            c = [
                flat[pl.ds(pl.multiple_of((f * depth + z) * y + i * step, step), step), :]
                for f in range(FIELDS)
            ]
            for f, (a, d, u) in enumerate(row_terms(c, low, high, z)):
                j = f * depth + z
                across[j, padded, :] = a
                down[j, padded, :] = d
                up[j, padded, :] = u
        return carry

    lax.fori_loop(0, y // step, flux_rows, 0)

    def predict_rows(j, carry):
        for k, value in enumerate(fold_rows(across, down, up, j, PAD, nb, 4)):
            folded[j, k * nb : (k + 1) * nb, :] = value
        for source, rim in ((across, rim_a), (down, rim_d), (up, rim_u)):
            rim[j, 0:8, :] = source[j, PAD : PAD + 8, :]
            rim[j, 8:16, :] = source[j, y : y + 8, :]
        return carry

    lax.fori_loop(0, total, predict_rows, 0)

    piece = 32

    def transform_field(f, carry):
        for start in range(0, y, piece):
            values = [folded[f * depth + z, start : start + piece, :] for z in range(4)]
            for k, value in enumerate(butterfly(*values)):
                high, low = halves(value)
                split[k * y + start : k * y + start + piece, 0:width] = high
                split[k * y + start : k * y + start + piece, width : 2 * width] = low
        product = jnp.dot(split[...], matrix[...], preferred_element_type=jnp.float32)
        result = product[:, 0:width] + product[:, width : 2 * width]
        peak = None
        for k in range(4):
            for m in range(4):
                value = result[k * y + m * nb : k * y + (m + 1) * nb]
                coefficients[f * depth + k, pl.ds(m, nb, stride=4), :] = value
                size = jnp.abs(value)
                peak = size if peak is None else jnp.maximum(peak, size)
        blocks[f] = over_lanes(peak)
        return carry

    lax.fori_loop(0, FIELDS, transform_field, 0)

    me = lax.axis_index("section")
    if rows % 8 == 0:
        for k in range(count):
            p = partner_of(me, k, count)
            for j in range(total):
                outs[k][j // depth, j % depth] = coefficients[j, pl.ds(pl.multiple_of(p * rows, 8), rows), :]
    else:
        for p in range(count):
            staged[p] = coefficients[:, p * rows : (p + 1) * rows, :]
        for k in range(count):
            p = partner_of(me, k, count)
            for j in range(total):
                outs[k][j // depth, j % depth] = staged[p, j]


def transform_bricks(count, total, y, flat, left, right, matrix):
    width = flat.shape[1]
    depth = total // FIELDS
    rows, tall = y // count, y + 2 * PAD
    chunk = array((FIELDS, depth, rows, width))
    message = array((4 * total + COLUMN_ROWS, width))
    rim = array((total, 2 * PAD, width))
    results = pl.pallas_call(
        functools.partial(brick_kernel, count, total, y),
        out_shape=[chunk] * count + [message] * 2 + [array((FIELDS, y // 4, width))] + [rim] * 3,
        in_specs=[vmem()] * 4,
        out_specs=[vmem()] * (count + 6),
        scratch_shapes=[
            pltpu.VMEM((total, tall, width), jnp.float32),
            pltpu.VMEM((total, tall, width), jnp.float32),
            pltpu.VMEM((total, tall, width), jnp.float32),
            pltpu.VMEM((2, FIELDS, y, width), jnp.float32),
            pltpu.VMEM((total, y, width), jnp.float32),
            pltpu.VMEM((depth * y, 2 * width), jnp.bfloat16),
            pltpu.VMEM((total, y, width), jnp.float32),
            pltpu.VMEM((1, 1, 8, LANES) if rows % 8 == 0 else (count, total, rows, width), jnp.float32),
        ],
        compiler_params=kernel_params(),
    )(flat, left, right, matrix)
    return results[:count], results[count : count + 2], results[count + 2], results[count + 3 :]


def mend_kernel(count, *refs):
    chunks, refs = refs[:count], refs[count:]
    top, bottom, blocks, rim_a, rim_d, rim_u, matrix = refs[:7]
    outs, mended, refs = refs[7 : 7 + count], refs[7 + count], refs[8 + count :]
    halo, columns, across, down, up, folded, split, result, fixed = refs
    fields, depth, rows, width = chunks[0].shape
    total = fields * depth
    nb = blocks.shape[1]

    halo[...] = jnp.ones(halo.shape, jnp.float32)
    columns[...] = jnp.ones(columns.shape, jnp.float32)
    for j in range(total):
        halo[j, 4:8, :] = top[4 * j : 4 * j + 4, :]
        halo[j, 8:12, :] = bottom[4 * j : 4 * j + 4, :]
    for side in range(2):
        place = 4 * total + 4 * side
        columns[side, 4:8, :] = top[place : place + 4, :]
        columns[side, 8:12, :] = bottom[place : place + 4, :]
    low = column_terms(columns[0], depth, COURANT)
    high = column_terms(columns[1], depth, -COURANT)
    for z in range(depth):
        c = [halo[f * depth + z] for f in range(fields)]
        for f, values in enumerate(row_terms(c, low, high, z)):
            j = f * depth + z
            for value, rim, target in zip(values, (rim_a, rim_d, rim_u), (across, down, up)):
                target[j, 0:8, :] = value[0:8]
                target[j, 8:24, :] = rim[j]
                target[j, 24:32, :] = value[8:16]
    for j in range(total):
        for k, value in enumerate(fold_rows(across, down, up, j, PAD, 2, 12)):
            folded[j, 2 * k : 2 * k + 2, :] = value
    for f in range(fields):
        values = butterfly(*[folded[f * depth + z] for z in range(4)])
        for half in range(2):
            both = jnp.concatenate(values[2 * half : 2 * half + 2], axis=0)
            upper, lower = halves(both)
            place = f * 32 + half * 16
            split[place : place + 16, 0:width] = upper
            split[place : place + 16, width : 2 * width] = lower
    product = jnp.dot(split[...], matrix[...], preferred_element_type=jnp.float32)
    result[...] = product[:, 0:width] + product[:, width : 2 * width]
    for j in range(total):
        for side in range(2):
            fixed[side, j] = result[pl.ds(8 * j + side, 4, stride=2), :]
    mended[...] = blocks[...]
    for f in range(fields):
        for side in range(2):
            size = jnp.abs(fixed[side, f * depth])
            for z in range(1, depth):
                size = jnp.maximum(size, jnp.abs(fixed[side, f * depth + z]))
            peak = over_lanes(jnp.max(size, axis=0, keepdims=True))
            row = side * (nb - 1)
            mended[f, row : row + 1, :] = peak

    me = lax.axis_index("section")
    for k in range(count):
        p = partner_of(me, k, count)
        outs[k][...] = chunks[k][...]
        for side, start in ((0, 0), (1, rows - 4)):

            @pl.when(p == side * (count - 1))
            def replace(k=k, side=side, start=start):
                for j in range(total):
                    outs[k][j // depth, j % depth, start : start + 4, :] = fixed[side, j]


def mend(count, chunks, top, bottom, blocks, rims, matrix):
    fields, depth, rows, width = chunks[0].shape
    total = fields * depth
    tall = pltpu.VMEM((total, 4 * PAD, width), jnp.float32)
    results = pl.pallas_call(
        functools.partial(mend_kernel, count),
        out_shape=[array(chunks[0].shape)] * count + [array(blocks.shape)],
        in_specs=[vmem()] * (count + 7),
        out_specs=[vmem()] * (count + 1),
        scratch_shapes=[
            pltpu.VMEM((total, 2 * PAD, width), jnp.float32),
            pltpu.VMEM((2, 2 * PAD, width), jnp.float32),
            tall,
            tall,
            tall,
            pltpu.VMEM((total, 8, width), jnp.float32),
            pltpu.VMEM((8 * total, 2 * width), jnp.bfloat16),
            pltpu.VMEM((8 * total, width), jnp.float32),
            pltpu.VMEM((2, total, 4, width), jnp.float32),
        ],
        compiler_params=kernel_params(),
    )(*chunks, top, bottom, blocks, *rims, matrix)
    return results[:count], results[count]


def group_kernel(count, groups, own_rows, *refs):
    blocks, refs = refs[0], refs[1:]
    messages, (peaks, gathered, listed, packed, table) = refs[:count], refs[count:]
    nb = blocks.shape[1]
    me = lax.axis_index("section")
    slot = slot_of(messages[0], me)
    within = lax.rem(slot, 4) * 32
    tile = lax.div(slot, 4)
    for d, message in enumerate(messages):
        height = gathered.shape[1]
        value = message[message.shape[0] - height :, :]
        if count > 4:
            value = pltpu.roll(value, lax.rem(height - tile * own_rows, height), 0)
        gathered[lax.rem(me + count - d, count)] = value
    for q in range(count):
        listed[q * own_rows : (q + 1) * own_rows, :] = gathered[q, 0:own_rows, :]
    part = nb // 4
    band = lax.div(lanes_of((part, LANES)), 32)
    labels = jnp.zeros((part, LANES), jnp.float32)
    for c in range(4):
        turned = pltpu.roll(listed[c * part : (c + 1) * part, :], lax.rem(32 * c - within + LANES, LANES), 1)
        labels = jnp.where(band == c, turned, labels)
    for f in range(FIELDS):
        own = jnp.zeros((part, LANES), jnp.float32)
        for c in range(4):
            own = jnp.where(band == c, blocks[f, c * part : (c + 1) * part, :], own)
        packed[f, 0:part, :] = own
    lane8 = lanes_of((8, LANES))
    sub8 = lax.broadcasted_iota(jnp.int32, (8, LANES), 0)
    label_rows = [jnp.broadcast_to(labels[r : r + 1], (8, LANES)) for r in range(part)]

    def group_tile(g, carry):
        wanted = (sub8 + g * 8).astype(jnp.float32)
        matches = [label_rows[r] == wanted for r in range(part)]
        found = jnp.zeros((8, LANES), jnp.float32)
        for f in range(FIELDS):
            best = jnp.zeros((8, LANES), jnp.float32)
            for r in range(part):
                row = jnp.broadcast_to(packed[f, r : r + 1, :], (8, LANES))
                best = jnp.maximum(best, jnp.where(matches[r], row, 0.0))
            found = jnp.where(lane8 == f, jnp.max(best, axis=1, keepdims=True), found)
        table[pl.ds(pl.multiple_of(g * 8, 8), 8), :] = found
        return carry

    high = table.shape[0]
    if groups < high:
        table[...] = jnp.zeros((high, LANES), jnp.float32)
    lax.fori_loop(0, pl.cdiv(groups, 8), group_tile, 0)
    for g in range(high // LANES):
        peaks[:, g * LANES : (g + 1) * LANES] = jnp.transpose(table[g * LANES : (g + 1) * LANES, :])[0:8]


def group_maxima(count, groups, own_rows, blocks, messages):
    high = pl.cdiv(groups, LANES) * LANES
    nb = blocks.shape[1]
    return pl.pallas_call(
        functools.partial(group_kernel, count, groups, own_rows),
        out_shape=array((8, high)),
        in_specs=[vmem()] * (count + 1),
        out_specs=vmem(),
        scratch_shapes=[
            pltpu.VMEM((count, messages[0].shape[0], LANES), jnp.float32),
            pltpu.VMEM((nb, LANES), jnp.float32),
            pltpu.VMEM((FIELDS, 8, LANES), jnp.float32),
            pltpu.VMEM((high, LANES), jnp.float32),
        ],
        compiler_params=kernel_params(),
    )(blocks, *messages)


def scale_kernel(count, groups, *refs):
    outer, inner, refs = refs[:count], refs[count : 2 * count - 2], refs[2 * count - 2 :]
    peaks, labels, coded, group_peak, wide = refs
    fields, depth, rows, width = outer[0].shape
    nb = rows // 4
    high = peaks.shape[1]
    me = lax.axis_index("section")
    is_inner = jnp.logical_and(me > 0, me < count - 1)
    group_peak[...] = peaks[0:fields, 0:groups]
    own_labels = labels[...].astype(jnp.int32)
    lane = lanes_of((8, LANES))
    inverse = 1.0 / (peaks[...] + EPSILON)
    tables = [
        [jnp.broadcast_to(inverse[f : f + 1, g * LANES : (g + 1) * LANES], (8, LANES)) for g in range(high // LANES)]
        for f in range(fields)
    ]
    for k in range(count):
        slot = slot_of(labels, sender_of(me, k, count))
        tile = own_labels
        if count > 4:
            tile = pltpu.roll(tile, lax.rem(LABEL_ROWS - lax.div(slot, 4) * nb, LABEL_ROWS), 0)
        within = lax.rem(slot, 4) * 32 + lax.rem(lane, 32)
        own = jnp.take_along_axis(tile, within, axis=1)
        place = pl.ds(pl.multiple_of(slot * width, width), width)
        for f in range(fields):
            if high == LANES:
                found = jnp.take_along_axis(tables[f][0], own, axis=1)
            else:
                found = jnp.zeros((8, LANES), jnp.float32)
                inside = lax.rem(own, LANES)
                for g in range(high // LANES):
                    here = jnp.take_along_axis(tables[f][g], inside, axis=1)
                    found = jnp.where(lax.div(own, LANES) == g, here, found)
            for m in range(4):
                wide[k, f, pl.ds(m, nb, stride=4), :] = found[0:nb]
            factor = wide[k, f]
            for z in range(depth):
                value = outer[k][f, z]
                if k >= 2:
                    value = jnp.where(is_inner, inner[k - 2][f, z], value)
                coded[f, z, :, place] = value * factor


def scale(count, groups, outer, inner, peaks, labels):
    fields, depth, rows, width = outer[0].shape
    return pl.pallas_call(
        functools.partial(scale_kernel, count, groups),
        out_shape=[array((fields, depth, rows, width * count)), array((fields, groups))],
        in_specs=[vmem()] * (2 * count),
        out_specs=[vmem()] * 2,
        scratch_shapes=[
            pltpu.VMEM((count, fields, rows, width), jnp.float32),
        ],
        compiler_params=kernel_params(),
    )(*outer, *inner, peaks, labels)


def ring(axis, shift):
    count = lax.axis_size(axis)
    return [(i, (i + shift) % count) for i in range(count)]


def exchange_pairs(count, k):
    if count & (count - 1) == 0:
        return [(i, i ^ k) for i in range(count)]
    return [(i, (i + k) % count) for i in range(count)]


def inner_pairs(count, k):
    return [(i, p) for i, p in exchange_pairs(count, k) if 0 < p < count - 1]


def outer_pairs(count, k):
    return [(i, p) for i, p in exchange_pairs(count, k) if p in (0, count - 1)]


def largest(value, axis):
    count = lax.axis_size(axis)
    span = 1
    while span < count:
        shift = min(span, count - span)
        value = jnp.maximum(value, lax.ppermute(value, axis, exchange_pairs(count, shift)))
        span += shift
    return value


def per_device(density, momentum, energy, membership, slot_of_brick):
    count = lax.axis_size("section")
    groups = 2 * lax.axis_size("sim") * count
    depth, y = density.shape[:2]
    total = FIELDS * depth
    flat = flatten(density, momentum, energy, membership, slot_of_brick)
    matrix, first_x, last_x, labels = pack(flat, y)
    left = lax.ppermute(last_x, "section", ring("section", 1))
    right = lax.ppermute(first_x, "section", ring("section", -1))
    far = [lax.ppermute(labels, "section", ring("section", d)) for d in range(2, count - 1)]
    left, right, *far = lax.optimization_barrier((left, right, *far))
    messages = [labels, left, *far, right]
    chunks, (first_y, last_y), blocks, rims = transform_bricks(count, total, y, flat, left, right, matrix)
    inner = [lax.ppermute(chunks[k], "section", inner_pairs(count, k)) for k in range(2, count)]
    top = lax.ppermute(last_y, "sim", ring("sim", 1))
    bottom = lax.ppermute(first_y, "sim", ring("sim", -1))
    chunks, blocks = mend(count, chunks, top, bottom, blocks, rims, matrix)
    outer = [lax.ppermute(chunks[k], "section", outer_pairs(count, k)) for k in range(2, count)]
    outer = [chunks[0], lax.ppermute(chunks[1], "section", exchange_pairs(count, 1))] + outer
    peaks = group_maxima(count, groups, membership.shape[0], blocks, messages)
    peaks, inner[0] = lax.optimization_barrier((peaks, inner[0]))
    peaks = largest(peaks, "sim")
    peaks, *inner = lax.optimization_barrier((peaks, *inner))
    peaks = largest(peaks, "section")
    return tuple(scale(count, groups, outer, inner, peaks, labels))


def solution(mesh):
    placed = (
        P(None, "sim", "section"),
        P(None, None, "sim", "section"),
        P(None, "sim", "section"),
        P(("sim", "section"), None),
        P("sim", None),
    )
    return jax.shard_map(
        per_device,
        mesh=mesh,
        in_specs=placed,
        out_specs=(P(None, None, ("sim", "section"), None), P()),
        check_vma=False,
    )
```

```python
import functools

import jax
import jax.numpy as jnp
import numpy as np
from jax import lax
from jax.experimental import pallas as pl
from jax.experimental.pallas import tpu as pltpu
from jax.sharding import PartitionSpec as P

GAMMA_LESS = 0.4
COURANT = 0.05
DIFFUSE = 0.1
EPSILON = 1e-06
FIELDS = 5
PAD = 8
COLUMN_ROWS = 8
LABEL_ROWS = 8
LANES = 128
EVEN = 0.5
WIDE = float(np.sqrt(0.5) * np.cos(np.pi / 8))
NARROW = float(np.sqrt(0.5) * np.cos(3 * np.pi / 8))
VMEM_LIMIT = 48 * 1024 * 1024


def vmem():
    return pl.BlockSpec(memory_space=pltpu.VMEM)


def lanes_of(shape):
    return lax.broadcasted_iota(jnp.int32, shape, 1)


def butterfly(a, b, c, d):
    s, t, u, v = a + d, b + c, a - d, b - c
    return (
        EVEN * (s + t),
        WIDE * u + NARROW * v,
        EVEN * (s - t),
        NARROW * u - WIDE * v,
    )


def cosine(k, d):
    factor = 0.5 if k == 0 else np.sqrt(0.5)
    return float(factor * np.cos(np.pi * (2 * d + 1) * k / 8))


def write_matrix(matrix, width):
    step = 16
    row = lax.broadcasted_iota(jnp.int32, (step, width), 0)
    column = lanes_of((step, width))
    quarter = width // 4
    k, j, d = lax.div(column, quarter), lax.rem(column, quarter), lax.rem(row, 4)
    entry = jnp.zeros((step, width), jnp.float32)
    for a in range(4):
        for b in range(4):
            entry = jnp.where(jnp.logical_and(k == a, d == b), cosine(a, b), entry)
    high = entry.astype(jnp.bfloat16).astype(jnp.float32)
    low = entry - high
    zero = jnp.zeros((step, width), jnp.bfloat16)
    for start in range(0, width, step):
        own = j == lax.div(row + start, 4)
        upper = jnp.where(own, high, 0.0).astype(jnp.bfloat16)
        lower = jnp.where(own, low, 0.0).astype(jnp.bfloat16)
        matrix[start : start + step, 0:width] = upper
        matrix[start : start + step, width : 2 * width] = lower
        matrix[width + start : width + start + step, 0:width] = upper
        matrix[width + start : width + start + step, width : 2 * width] = zero


def kernel_params():
    return pltpu.CompilerParams(vmem_limit_bytes=VMEM_LIMIT)


def array(shape, dtype=jnp.float32):
    return jax.ShapeDtypeStruct(shape, dtype)


def pack_kernel(conserved, membership, slots, matrix, first_x, last_x, labels):
    fields, depth, y, width = conserved.shape
    quarter = y // 4
    lane = lanes_of((y, width))
    first = jnp.zeros((y, width), jnp.float32)
    last = jnp.zeros((y, width), jnp.float32)
    for j in range(fields * depth):
        value = conserved[j // depth, j % depth]
        first = jnp.where(lane == j, pltpu.roll(value, j, 1) if j else value, first)
        last = jnp.where(lane == j, pltpu.roll(value, j + 1, 1), last)
    rows, columns = membership.shape
    labels[...] = jnp.zeros(labels.shape, jnp.float32)
    for t in range(columns // LANES):
        part = membership[:, t * LANES : (t + 1) * LANES].astype(jnp.float32)
        labels[t * rows : (t + 1) * rows, :] = part
    labels[LABEL_ROWS - 1 : LABEL_ROWS, 0 : slots.shape[1]] = slots[...].astype(jnp.float32)
    own = labels[...]
    for column, out in ((first, first_x), (last, last_x)):
        packed = column[0:quarter]
        for c in range(1, 4):
            packed = packed + pltpu.roll(column[c * quarter : (c + 1) * quarter], 32 * c, 1)
        out[0:quarter, :] = packed
        out[quarter:, :] = own
    write_matrix(matrix, width)


def pack(conserved, membership, slots):
    y, width = conserved.shape[2:]
    shapes = [
        array((2 * width, 2 * width), jnp.bfloat16),
        array((y // 4 + LABEL_ROWS, width)),
        array((y // 4 + LABEL_ROWS, width)),
        array((LABEL_ROWS, width)),
    ]
    return pl.pallas_call(
        pack_kernel,
        out_shape=shapes,
        in_specs=[vmem()] * 3,
        out_specs=[vmem()] * 4,
        compiler_params=kernel_params(),
    )(conserved, membership, slots)


def slot_of(labels, brick):
    row = labels[LABEL_ROWS - 1 : LABEL_ROWS, :]
    return jnp.max(jnp.where(lanes_of(row.shape) == brick, row, 0.0)).astype(jnp.int32)


def fluxes(c):
    rho, mx, my, mz, e = c
    inverse = 1.0 / rho
    u, v = mx * inverse, my * inverse
    pressure = GAMMA_LESS * (e - 0.5 * (mx * mx + my * my + mz * mz) * inverse)
    total = e + pressure
    flux_x = (mx, mx * u + pressure, my * u, mz * u, total * u)
    flux_y = (my, mx * v, my * v + pressure, mz * v, total * v)
    return flux_x, flux_y


def column_terms(own, depth, sign):
    fields = [pltpu.roll(own, LANES - depth * f, 1) if f else own for f in range(FIELDS)]
    flux_x, unused = fluxes(fields)
    return [DIFFUSE * fields[f] + sign * flux_x[f] for f in range(FIELDS)]


def row_terms(c, low, high, z):
    rows, width = c[0].shape
    lane = lanes_of((rows, width))
    flux_x, flux_y = fluxes(c)
    terms = []
    for f in range(FIELDS):
        base = DIFFUSE * c[f]
        gx, gy = COURANT * flux_x[f], COURANT * flux_y[f]
        from_left = pltpu.roll(base + gx, 1, 1)
        from_right = pltpu.roll(base - gx, width - 1, 1)
        at_left = pltpu.roll(low[f], LANES - z, 1) if z else low[f]
        at_right = pltpu.roll(high[f], LANES - 1 - z, 1)
        across = (
            (1.0 - 4.0 * DIFFUSE) * c[f]
            + jnp.where(lane == 0, at_left, from_left)
            + jnp.where(lane == width - 1, at_right, from_right)
        )
        terms.append((across, base + gy, base - gy))
    return terms


def fold_rows(across, down, up, j, origin, number, stride):
    t = {}
    for o in range(-3, 7):
        t[o] = (
            across[j, pl.ds(origin + o, number, stride=stride), :]
            + down[j, pl.ds(origin + o - 1, number, stride=stride), :]
            + up[j, pl.ds(origin + o + 1, number, stride=stride), :]
        )
    residual = [
        t[m] - (9.0 / 16.0) * (t[m - 1] + t[m + 1]) + (1.0 / 16.0) * (t[m - 3] + t[m + 3])
        for m in range(4)
    ]
    return butterfly(*residual)


def halves(value):
    high = value.astype(jnp.bfloat16)
    return high, (value - high.astype(jnp.float32)).astype(jnp.bfloat16)


def over_lanes(peak):
    peak = jnp.maximum(peak, pltpu.roll(peak, 64, 1))
    return jnp.maximum(peak, pltpu.roll(peak, 32, 1))


def partner_of(me, k, count):
    if count & (count - 1) == 0:
        return me ^ k
    return lax.rem(me + k, count)


def sender_of(me, k, count):
    if count & (count - 1) == 0:
        return me ^ k
    return lax.rem(me - k + count, count)


def brick_kernel(count, *refs):
    conserved, left, right, matrix = refs[:4]
    outs, refs = refs[4 : 4 + count], refs[4 + count :]
    first_y, last_y, blocks, rim_a, rim_d, rim_u, across, down, up, edges, folded, split, coefficients, staged = refs
    fields, depth, y, width = conserved.shape
    total = fields * depth
    nb, quarter = y // 4, y // 4
    rows = y // count

    for side, column in enumerate((left, right)):
        parts = []
        for c in range(4):
            value = column[0:quarter, :]
            parts.append(pltpu.roll(value, LANES - 32 * c, 1) if c else value)
        own = jnp.concatenate(parts, axis=0)
        for f, value in enumerate(column_terms(own, depth, COURANT if side == 0 else -COURANT)):
            edges[side, f] = value
        place = 4 * total + 4 * side
        first_y[place : place + 4, :] = own[0:4]
        last_y[place : place + 4, :] = own[y - 4 : y]
    for j in range(total):
        first_y[4 * j : 4 * j + 4, :] = conserved[j // depth, j % depth, 0:4, :]
        last_y[4 * j : 4 * j + 4, :] = conserved[j // depth, j % depth, y - 4 : y, :]

    step = 16

    def flux_rows(i, carry):
        r = pl.ds(pl.multiple_of(i * step, step), step)
        padded = pl.ds(pl.multiple_of(i * step + PAD, PAD), step)
        low = [edges[0, f, r, :] for f in range(FIELDS)]
        high = [edges[1, f, r, :] for f in range(FIELDS)]
        for z in range(depth):
            c = [conserved[f, z, r, :] for f in range(FIELDS)]
            for f, (a, d, u) in enumerate(row_terms(c, low, high, z)):
                j = f * depth + z
                across[j, padded, :] = a
                down[j, padded, :] = d
                up[j, padded, :] = u
        return carry

    lax.fori_loop(0, y // step, flux_rows, 0)

    def predict_rows(j, carry):
        for k, value in enumerate(fold_rows(across, down, up, j, PAD, nb, 4)):
            folded[j, k * nb : (k + 1) * nb, :] = value
        for source, rim in ((across, rim_a), (down, rim_d), (up, rim_u)):
            rim[j, 0:8, :] = source[j, PAD : PAD + 8, :]
            rim[j, 8:16, :] = source[j, y : y + 8, :]
        return carry

    lax.fori_loop(0, total, predict_rows, 0)

    piece = 32

    def transform_field(f, carry):
        for start in range(0, y, piece):
            values = [folded[f * depth + z, start : start + piece, :] for z in range(4)]
            for k, value in enumerate(butterfly(*values)):
                high, low = halves(value)
                split[k * y + start : k * y + start + piece, 0:width] = high
                split[k * y + start : k * y + start + piece, width : 2 * width] = low
        product = jnp.dot(split[...], matrix[...], preferred_element_type=jnp.float32)
        result = product[:, 0:width] + product[:, width : 2 * width]
        peak = None
        for k in range(4):
            for m in range(4):
                value = result[k * y + m * nb : k * y + (m + 1) * nb]
                coefficients[f * depth + k, pl.ds(m, nb, stride=4), :] = value
                size = jnp.abs(value)
                peak = size if peak is None else jnp.maximum(peak, size)
        blocks[f] = over_lanes(peak)
        return carry

    lax.fori_loop(0, FIELDS, transform_field, 0)

    me = lax.axis_index("section")
    if rows % 8 == 0:
        for k in range(count):
            p = partner_of(me, k, count)
            for j in range(total):
                outs[k][j // depth, j % depth] = coefficients[j, pl.ds(pl.multiple_of(p * rows, 8), rows), :]
    else:
        for p in range(count):
            staged[p] = coefficients[:, p * rows : (p + 1) * rows, :]
        for k in range(count):
            p = partner_of(me, k, count)
            for j in range(total):
                outs[k][j // depth, j % depth] = staged[p, j]


def transform_bricks(count, conserved, left, right, matrix):
    fields, depth, y, width = conserved.shape
    total = fields * depth
    rows, tall = y // count, y + 2 * PAD
    chunk = array((FIELDS, depth, rows, width))
    message = array((4 * total + COLUMN_ROWS, width))
    rim = array((total, 2 * PAD, width))
    results = pl.pallas_call(
        functools.partial(brick_kernel, count),
        out_shape=[chunk] * count + [message] * 2 + [array((FIELDS, y // 4, width))] + [rim] * 3,
        in_specs=[vmem()] * 4,
        out_specs=[vmem()] * (count + 6),
        scratch_shapes=[
            pltpu.VMEM((total, tall, width), jnp.float32),
            pltpu.VMEM((total, tall, width), jnp.float32),
            pltpu.VMEM((total, tall, width), jnp.float32),
            pltpu.VMEM((2, FIELDS, y, width), jnp.float32),
            pltpu.VMEM((total, y, width), jnp.float32),
            pltpu.VMEM((depth * y, 2 * width), jnp.bfloat16),
            pltpu.VMEM((total, y, width), jnp.float32),
            pltpu.VMEM((1, 1, 8, LANES) if rows % 8 == 0 else (count, total, rows, width), jnp.float32),
        ],
        compiler_params=kernel_params(),
    )(conserved, left, right, matrix)
    return results[:count], results[count : count + 2], results[count + 2], results[count + 3 :]


def mend_kernel(count, *refs):
    chunks, refs = refs[:count], refs[count:]
    top, bottom, blocks, rim_a, rim_d, rim_u, matrix = refs[:7]
    outs, mended, refs = refs[7 : 7 + count], refs[7 + count], refs[8 + count :]
    halo, columns, across, down, up, folded, split, result, fixed = refs
    fields, depth, rows, width = chunks[0].shape
    total = fields * depth
    nb = blocks.shape[1]

    halo[...] = jnp.ones(halo.shape, jnp.float32)
    columns[...] = jnp.ones(columns.shape, jnp.float32)
    for j in range(total):
        halo[j, 4:8, :] = top[4 * j : 4 * j + 4, :]
        halo[j, 8:12, :] = bottom[4 * j : 4 * j + 4, :]
    for side in range(2):
        place = 4 * total + 4 * side
        columns[side, 4:8, :] = top[place : place + 4, :]
        columns[side, 8:12, :] = bottom[place : place + 4, :]
    low = column_terms(columns[0], depth, COURANT)
    high = column_terms(columns[1], depth, -COURANT)
    for z in range(depth):
        c = [halo[f * depth + z] for f in range(fields)]
        for f, values in enumerate(row_terms(c, low, high, z)):
            j = f * depth + z
            for value, rim, target in zip(values, (rim_a, rim_d, rim_u), (across, down, up)):
                target[j, 0:8, :] = value[0:8]
                target[j, 8:24, :] = rim[j]
                target[j, 24:32, :] = value[8:16]
    for j in range(total):
        for k, value in enumerate(fold_rows(across, down, up, j, PAD, 2, 12)):
            folded[j, 2 * k : 2 * k + 2, :] = value
    for f in range(fields):
        values = butterfly(*[folded[f * depth + z] for z in range(4)])
        for half in range(2):
            both = jnp.concatenate(values[2 * half : 2 * half + 2], axis=0)
            upper, lower = halves(both)
            place = f * 32 + half * 16
            split[place : place + 16, 0:width] = upper
            split[place : place + 16, width : 2 * width] = lower
    product = jnp.dot(split[...], matrix[...], preferred_element_type=jnp.float32)
    result[...] = product[:, 0:width] + product[:, width : 2 * width]
    for j in range(total):
        for side in range(2):
            fixed[side, j] = result[pl.ds(8 * j + side, 4, stride=2), :]
    mended[...] = blocks[...]
    for f in range(fields):
        for side in range(2):
            size = jnp.abs(fixed[side, f * depth])
            for z in range(1, depth):
                size = jnp.maximum(size, jnp.abs(fixed[side, f * depth + z]))
            peak = over_lanes(jnp.max(size, axis=0, keepdims=True))
            row = side * (nb - 1)
            mended[f, row : row + 1, :] = peak

    me = lax.axis_index("section")
    for k in range(count):
        p = partner_of(me, k, count)
        outs[k][...] = chunks[k][...]
        for side, start in ((0, 0), (1, rows - 4)):

            @pl.when(p == side * (count - 1))
            def replace(k=k, side=side, start=start):
                for j in range(total):
                    outs[k][j // depth, j % depth, start : start + 4, :] = fixed[side, j]


def mend(count, chunks, top, bottom, blocks, rims, matrix):
    fields, depth, rows, width = chunks[0].shape
    total = fields * depth
    tall = pltpu.VMEM((total, 4 * PAD, width), jnp.float32)
    results = pl.pallas_call(
        functools.partial(mend_kernel, count),
        out_shape=[array(chunks[0].shape)] * count + [array(blocks.shape)],
        in_specs=[vmem()] * (count + 7),
        out_specs=[vmem()] * (count + 1),
        scratch_shapes=[
            pltpu.VMEM((total, 2 * PAD, width), jnp.float32),
            pltpu.VMEM((2, 2 * PAD, width), jnp.float32),
            tall,
            tall,
            tall,
            pltpu.VMEM((total, 8, width), jnp.float32),
            pltpu.VMEM((8 * total, 2 * width), jnp.bfloat16),
            pltpu.VMEM((8 * total, width), jnp.float32),
            pltpu.VMEM((2, total, 4, width), jnp.float32),
        ],
        compiler_params=kernel_params(),
    )(*chunks, top, bottom, blocks, *rims, matrix)
    return results[:count], results[count]


def group_kernel(count, groups, own_rows, *refs):
    blocks, refs = refs[0], refs[1:]
    messages, (peaks, gathered, listed, packed, table) = refs[:count], refs[count:]
    nb = blocks.shape[1]
    me = lax.axis_index("section")
    slot = slot_of(messages[0], me)
    within = lax.rem(slot, 4) * 32
    tile = lax.div(slot, 4)
    for d, message in enumerate(messages):
        height = gathered.shape[1]
        value = message[message.shape[0] - height :, :]
        if count > 4:
            value = pltpu.roll(value, lax.rem(height - tile * own_rows, height), 0)
        gathered[lax.rem(me + count - d, count)] = value
    for q in range(count):
        listed[q * own_rows : (q + 1) * own_rows, :] = gathered[q, 0:own_rows, :]
    part = nb // 4
    band = lax.div(lanes_of((part, LANES)), 32)
    labels = jnp.zeros((part, LANES), jnp.float32)
    for c in range(4):
        turned = pltpu.roll(listed[c * part : (c + 1) * part, :], lax.rem(32 * c - within + LANES, LANES), 1)
        labels = jnp.where(band == c, turned, labels)
    for f in range(FIELDS):
        own = jnp.zeros((part, LANES), jnp.float32)
        for c in range(4):
            own = jnp.where(band == c, blocks[f, c * part : (c + 1) * part, :], own)
        packed[f, 0:part, :] = own
    lane8 = lanes_of((8, LANES))
    sub8 = lax.broadcasted_iota(jnp.int32, (8, LANES), 0)
    label_rows = [jnp.broadcast_to(labels[r : r + 1], (8, LANES)) for r in range(part)]

    def group_tile(g, carry):
        wanted = (sub8 + g * 8).astype(jnp.float32)
        matches = [label_rows[r] == wanted for r in range(part)]
        found = jnp.zeros((8, LANES), jnp.float32)
        for f in range(FIELDS):
            best = jnp.zeros((8, LANES), jnp.float32)
            for r in range(part):
                row = jnp.broadcast_to(packed[f, r : r + 1, :], (8, LANES))
                best = jnp.maximum(best, jnp.where(matches[r], row, 0.0))
            found = jnp.where(lane8 == f, jnp.max(best, axis=1, keepdims=True), found)
        table[pl.ds(pl.multiple_of(g * 8, 8), 8), :] = found
        return carry

    high = table.shape[0]
    if groups < high:
        table[...] = jnp.zeros((high, LANES), jnp.float32)
    lax.fori_loop(0, pl.cdiv(groups, 8), group_tile, 0)
    for g in range(high // LANES):
        peaks[:, g * LANES : (g + 1) * LANES] = jnp.transpose(table[g * LANES : (g + 1) * LANES, :])[0:8]


def group_maxima(count, groups, own_rows, blocks, messages):
    high = pl.cdiv(groups, LANES) * LANES
    nb = blocks.shape[1]
    return pl.pallas_call(
        functools.partial(group_kernel, count, groups, own_rows),
        out_shape=array((8, high)),
        in_specs=[vmem()] * (count + 1),
        out_specs=vmem(),
        scratch_shapes=[
            pltpu.VMEM((count, messages[0].shape[0], LANES), jnp.float32),
            pltpu.VMEM((nb, LANES), jnp.float32),
            pltpu.VMEM((FIELDS, 8, LANES), jnp.float32),
            pltpu.VMEM((high, LANES), jnp.float32),
        ],
        compiler_params=kernel_params(),
    )(blocks, *messages)


def scale_kernel(count, groups, *refs):
    outer, inner, refs = refs[:count], refs[count : 2 * count - 2], refs[2 * count - 2 :]
    peaks, labels, coded, group_peak, wide = refs
    fields, depth, rows, width = outer[0].shape
    nb = rows // 4
    high = peaks.shape[1]
    me = lax.axis_index("section")
    is_inner = jnp.logical_and(me > 0, me < count - 1)
    group_peak[...] = peaks[0:fields, 0:groups]
    own_labels = labels[...].astype(jnp.int32)
    lane = lanes_of((8, LANES))
    inverse = 1.0 / (peaks[...] + EPSILON)
    tables = [
        [jnp.broadcast_to(inverse[f : f + 1, g * LANES : (g + 1) * LANES], (8, LANES)) for g in range(high // LANES)]
        for f in range(fields)
    ]
    for k in range(count):
        slot = slot_of(labels, sender_of(me, k, count))
        tile = own_labels
        if count > 4:
            tile = pltpu.roll(tile, lax.rem(LABEL_ROWS - lax.div(slot, 4) * nb, LABEL_ROWS), 0)
        within = lax.rem(slot, 4) * 32 + lax.rem(lane, 32)
        own = jnp.take_along_axis(tile, within, axis=1)
        place = pl.ds(pl.multiple_of(slot * width, width), width)
        for f in range(fields):
            if high == LANES:
                found = jnp.take_along_axis(tables[f][0], own, axis=1)
            else:
                found = jnp.zeros((8, LANES), jnp.float32)
                inside = lax.rem(own, LANES)
                for g in range(high // LANES):
                    here = jnp.take_along_axis(tables[f][g], inside, axis=1)
                    found = jnp.where(lax.div(own, LANES) == g, here, found)
            for m in range(4):
                wide[k, f, pl.ds(m, nb, stride=4), :] = found[0:nb]
            factor = wide[k, f]
            for z in range(depth):
                value = outer[k][f, z]
                if k >= 2:
                    value = jnp.where(is_inner, inner[k - 2][f, z], value)
                coded[f, z, :, place] = value * factor


def scale(count, groups, outer, inner, peaks, labels):
    fields, depth, rows, width = outer[0].shape
    return pl.pallas_call(
        functools.partial(scale_kernel, count, groups),
        out_shape=[array((fields, depth, rows, width * count)), array((fields, groups))],
        in_specs=[vmem()] * (2 * count),
        out_specs=[vmem()] * 2,
        scratch_shapes=[
            pltpu.VMEM((count, fields, rows, width), jnp.float32),
        ],
        compiler_params=kernel_params(),
    )(*outer, *inner, peaks, labels)


def ring(axis, shift):
    count = lax.axis_size(axis)
    return [(i, (i + shift) % count) for i in range(count)]


def exchange_pairs(count, k):
    if count & (count - 1) == 0:
        return [(i, i ^ k) for i in range(count)]
    return [(i, (i + k) % count) for i in range(count)]


def inner_pairs(count, k):
    return [(i, p) for i, p in exchange_pairs(count, k) if 0 < p < count - 1]


def outer_pairs(count, k):
    return [(i, p) for i, p in exchange_pairs(count, k) if p in (0, count - 1)]


def steps_over(axis):
    count = lax.axis_size(axis)
    span, shifts = 1, []
    while span < count:
        shifts.append(min(span, count - span))
        span += shifts[-1]
    return shifts


def with_others(value, axis, shifts):
    count = lax.axis_size(axis)
    others = [lax.ppermute(value, axis, exchange_pairs(count, k)) for k in shifts]
    return functools.reduce(jnp.maximum, others, value)


def tied(value, others):
    value, *others = lax.optimization_barrier((value, *others))
    return value, others


def per_device(density, momentum, energy, membership, slot_of_brick):
    count = lax.axis_size("section")
    groups = 2 * lax.axis_size("sim") * count
    conserved = jnp.concatenate([density[None], momentum, energy[None]], axis=0)
    matrix, first_x, last_x, labels = pack(conserved, membership, slot_of_brick)
    left = lax.ppermute(last_x, "section", ring("section", 1))
    right = lax.ppermute(first_x, "section", ring("section", -1))
    far = [lax.ppermute(labels, "section", ring("section", d)) for d in range(2, count - 1)]
    chunks, (first_y, last_y), blocks, rims = transform_bricks(count, conserved, left, right, matrix)
    inner = [lax.ppermute(chunks[2], "section", inner_pairs(count, 2))]
    top = lax.ppermute(last_y, "sim", ring("sim", 1))
    bottom = lax.ppermute(first_y, "sim", ring("sim", -1))
    later = chunks[3:]
    chunks, blocks = mend(count, chunks, top, bottom, blocks, rims, matrix)
    blocks, later = tied(blocks, later)
    inner += [lax.ppermute(chunk, "section", inner_pairs(count, k)) for k, chunk in enumerate(later, 3)]
    peaks = group_maxima(count, groups, membership.shape[0], blocks, [labels, left, *far, right])
    outer = {0: chunks[0]}
    waiting = [*range(2, count), 1]
    shifts = steps_over("sim")
    for i, shift in enumerate(shifts):
        take = len(waiting) if i == len(shifts) - 1 else 1
        ready, waiting = waiting[:take], waiting[take:]
        peaks, leaving = tied(peaks, [chunks[k] for k in ready])
        for k, chunk in zip(ready, leaving):
            pairs = exchange_pairs(count, k) if k == 1 else outer_pairs(count, k)
            outer[k] = lax.ppermute(chunk, "section", pairs)
        if i == 1:
            peaks, inner[:1] = tied(peaks, inner[:1])
        peaks = with_others(peaks, "sim", [shift])
    peaks, (outer[2], *inner[1:]) = tied(peaks, [outer[2], *inner[1:]])
    if count <= 4:
        peaks = with_others(peaks, "section", range(1, count))
    else:
        for shift in steps_over("section"):
            peaks = with_others(peaks, "section", [shift])
    arrived = [outer[k] for k in range(count)]
    return tuple(scale(count, groups, arrived, inner, peaks, labels))


def solution(mesh):
    placed = (
        P(None, "sim", "section"),
        P(None, None, "sim", "section"),
        P(None, "sim", "section"),
        P(("sim", "section"), None),
        P("sim", None),
    )
    return jax.shard_map(
        per_device,
        mesh=mesh,
        in_specs=placed,
        out_specs=(P(None, None, ("sim", "section"), None), P()),
        check_vma=False,
    )
```

```python
import functools

import jax
import jax.numpy as jnp
import numpy as np
from jax import lax
from jax.experimental import pallas as pl
from jax.experimental.pallas import tpu as pltpu
from jax.sharding import PartitionSpec as P

GAMMA_LESS = 0.4
COURANT = 0.05
DIFFUSE = 0.1
EPSILON = 1e-06
FIELDS = 5
PAD = 8
COLUMN_ROWS = 8
LABEL_ROWS = 8
LANES = 128
EVEN = 0.5
WIDE = float(np.sqrt(0.5) * np.cos(np.pi / 8))
NARROW = float(np.sqrt(0.5) * np.cos(3 * np.pi / 8))
VMEM_LIMIT = 48 * 1024 * 1024


def vmem():
    return pl.BlockSpec(memory_space=pltpu.VMEM)


def lanes_of(shape):
    return lax.broadcasted_iota(jnp.int32, shape, 1)


def butterfly(a, b, c, d):
    s, t, u, v = a + d, b + c, a - d, b - c
    return (
        EVEN * (s + t),
        WIDE * u + NARROW * v,
        EVEN * (s - t),
        NARROW * u - WIDE * v,
    )


def cosine(k, d):
    factor = 0.5 if k == 0 else np.sqrt(0.5)
    return float(factor * np.cos(np.pi * (2 * d + 1) * k / 8))


def write_matrix(matrix, width):
    step = 16
    row = lax.broadcasted_iota(jnp.int32, (step, width), 0)
    column = lanes_of((step, width))
    quarter = width // 4
    k, j, d = lax.div(column, quarter), lax.rem(column, quarter), lax.rem(row, 4)
    entry = jnp.zeros((step, width), jnp.float32)
    for a in range(4):
        for b in range(4):
            entry = jnp.where(jnp.logical_and(k == a, d == b), cosine(a, b), entry)
    high = entry.astype(jnp.bfloat16).astype(jnp.float32)
    low = entry - high
    zero = jnp.zeros((step, width), jnp.bfloat16)
    for start in range(0, width, step):
        own = j == lax.div(row + start, 4)
        upper = jnp.where(own, high, 0.0).astype(jnp.bfloat16)
        lower = jnp.where(own, low, 0.0).astype(jnp.bfloat16)
        matrix[start : start + step, 0:width] = upper
        matrix[start : start + step, width : 2 * width] = lower
        matrix[width + start : width + start + step, 0:width] = upper
        matrix[width + start : width + start + step, width : 2 * width] = zero


def kernel_params():
    return pltpu.CompilerParams(vmem_limit_bytes=VMEM_LIMIT)


def array(shape, dtype=jnp.float32):
    return jax.ShapeDtypeStruct(shape, dtype)


def pack_kernel(conserved, membership, slots, matrix, first_x, last_x, labels):
    fields, depth, y, width = conserved.shape
    quarter = y // 4
    lane = lanes_of((y, width))
    first = jnp.zeros((y, width), jnp.float32)
    last = jnp.zeros((y, width), jnp.float32)
    for j in range(fields * depth):
        value = conserved[j // depth, j % depth]
        first = jnp.where(lane == j, pltpu.roll(value, j, 1) if j else value, first)
        last = jnp.where(lane == j, pltpu.roll(value, j + 1, 1), last)
    rows, columns = membership.shape
    labels[...] = jnp.zeros(labels.shape, jnp.float32)
    for t in range(columns // LANES):
        part = membership[:, t * LANES : (t + 1) * LANES].astype(jnp.float32)
        labels[t * rows : (t + 1) * rows, :] = part
    labels[LABEL_ROWS - 1 : LABEL_ROWS, 0 : slots.shape[1]] = slots[...].astype(jnp.float32)
    own = labels[...]
    for column, out in ((first, first_x), (last, last_x)):
        packed = column[0:quarter]
        for c in range(1, 4):
            packed = packed + pltpu.roll(column[c * quarter : (c + 1) * quarter], 32 * c, 1)
        out[0:quarter, :] = packed
        out[quarter:, :] = own
    write_matrix(matrix, width)


def pack(conserved, membership, slots):
    y, width = conserved.shape[2:]
    shapes = [
        array((2 * width, 2 * width), jnp.bfloat16),
        array((y // 4 + LABEL_ROWS, width)),
        array((y // 4 + LABEL_ROWS, width)),
        array((LABEL_ROWS, width)),
    ]
    return pl.pallas_call(
        pack_kernel,
        out_shape=shapes,
        in_specs=[vmem()] * 3,
        out_specs=[vmem()] * 4,
        compiler_params=kernel_params(),
    )(conserved, membership, slots)


def slot_of(labels, brick):
    row = labels[LABEL_ROWS - 1 : LABEL_ROWS, :]
    return jnp.max(jnp.where(lanes_of(row.shape) == brick, row, 0.0)).astype(jnp.int32)


def fluxes(c):
    rho, mx, my, mz, e = c
    inverse = 1.0 / rho
    u, v = mx * inverse, my * inverse
    pressure = GAMMA_LESS * (e - 0.5 * (mx * mx + my * my + mz * mz) * inverse)
    total = e + pressure
    flux_x = (mx, mx * u + pressure, my * u, mz * u, total * u)
    flux_y = (my, mx * v, my * v + pressure, mz * v, total * v)
    return flux_x, flux_y


def column_terms(own, depth, sign):
    fields = [pltpu.roll(own, LANES - depth * f, 1) if f else own for f in range(FIELDS)]
    flux_x, unused = fluxes(fields)
    return [DIFFUSE * fields[f] + sign * flux_x[f] for f in range(FIELDS)]


def row_terms(c, low, high, z):
    rows, width = c[0].shape
    lane = lanes_of((rows, width))
    flux_x, flux_y = fluxes(c)
    terms = []
    for f in range(FIELDS):
        base = DIFFUSE * c[f]
        gx, gy = COURANT * flux_x[f], COURANT * flux_y[f]
        from_left = pltpu.roll(base + gx, 1, 1)
        from_right = pltpu.roll(base - gx, width - 1, 1)
        at_left = pltpu.roll(low[f], LANES - z, 1) if z else low[f]
        at_right = pltpu.roll(high[f], LANES - 1 - z, 1)
        across = (
            (1.0 - 4.0 * DIFFUSE) * c[f]
            + jnp.where(lane == 0, at_left, from_left)
            + jnp.where(lane == width - 1, at_right, from_right)
        )
        terms.append((across, base + gy, base - gy))
    return terms


def fold_rows(across, down, up, j, origin, number, stride):
    t = {}
    for o in range(-3, 7):
        t[o] = (
            across[j, pl.ds(origin + o, number, stride=stride), :]
            + down[j, pl.ds(origin + o - 1, number, stride=stride), :]
            + up[j, pl.ds(origin + o + 1, number, stride=stride), :]
        )
    residual = [
        t[m] - (9.0 / 16.0) * (t[m - 1] + t[m + 1]) + (1.0 / 16.0) * (t[m - 3] + t[m + 3])
        for m in range(4)
    ]
    return butterfly(*residual)


def halves(value):
    high = value.astype(jnp.bfloat16)
    return high, (value - high.astype(jnp.float32)).astype(jnp.bfloat16)


def over_lanes(peak):
    peak = jnp.maximum(peak, pltpu.roll(peak, 64, 1))
    return jnp.maximum(peak, pltpu.roll(peak, 32, 1))


def partner_of(me, k, count):
    if count & (count - 1) == 0:
        return me ^ k
    return lax.rem(me + k, count)


def sender_of(me, k, count):
    if count & (count - 1) == 0:
        return me ^ k
    return lax.rem(me - k + count, count)


def brick_kernel(count, *refs):
    conserved, left, right, matrix = refs[:4]
    outs, refs = refs[4 : 4 + count], refs[4 + count :]
    first_y, last_y, blocks, rim_a, rim_d, rim_u, across, down, up, edges, folded, split, coefficients, staged = refs
    fields, depth, y, width = conserved.shape
    total = fields * depth
    nb, quarter = y // 4, y // 4
    rows = y // count

    for side, column in enumerate((left, right)):
        parts = []
        for c in range(4):
            value = column[0:quarter, :]
            parts.append(pltpu.roll(value, LANES - 32 * c, 1) if c else value)
        own = jnp.concatenate(parts, axis=0)
        for f, value in enumerate(column_terms(own, depth, COURANT if side == 0 else -COURANT)):
            edges[side, f] = value
        place = 4 * total + 4 * side
        first_y[place : place + 4, :] = own[0:4]
        last_y[place : place + 4, :] = own[y - 4 : y]
    for j in range(total):
        first_y[4 * j : 4 * j + 4, :] = conserved[j // depth, j % depth, 0:4, :]
        last_y[4 * j : 4 * j + 4, :] = conserved[j // depth, j % depth, y - 4 : y, :]

    step = 16

    def flux_rows(i, carry):
        r = pl.ds(pl.multiple_of(i * step, step), step)
        padded = pl.ds(pl.multiple_of(i * step + PAD, PAD), step)
        low = [edges[0, f, r, :] for f in range(FIELDS)]
        high = [edges[1, f, r, :] for f in range(FIELDS)]
        for z in range(depth):
            c = [conserved[f, z, r, :] for f in range(FIELDS)]
            for f, (a, d, u) in enumerate(row_terms(c, low, high, z)):
                j = f * depth + z
                across[j, padded, :] = a
                down[j, padded, :] = d
                up[j, padded, :] = u
        return carry

    lax.fori_loop(0, y // step, flux_rows, 0)

    def predict_rows(j, carry):
        for k, value in enumerate(fold_rows(across, down, up, j, PAD, nb, 4)):
            folded[j, k * nb : (k + 1) * nb, :] = value
        for source, rim in ((across, rim_a), (down, rim_d), (up, rim_u)):
            rim[j, 0:8, :] = source[j, PAD : PAD + 8, :]
            rim[j, 8:16, :] = source[j, y : y + 8, :]
        return carry

    lax.fori_loop(0, total, predict_rows, 0)

    piece = 32

    def transform_field(f, carry):
        for start in range(0, y, piece):
            values = [folded[f * depth + z, start : start + piece, :] for z in range(4)]
            for k, value in enumerate(butterfly(*values)):
                high, low = halves(value)
                split[k * y + start : k * y + start + piece, 0:width] = high
                split[k * y + start : k * y + start + piece, width : 2 * width] = low
        product = jnp.dot(split[...], matrix[...], preferred_element_type=jnp.float32)
        result = product[:, 0:width] + product[:, width : 2 * width]
        peak = None
        for k in range(4):
            for m in range(4):
                value = result[k * y + m * nb : k * y + (m + 1) * nb]
                coefficients[f * depth + k, pl.ds(m, nb, stride=4), :] = value
                size = jnp.abs(value)
                peak = size if peak is None else jnp.maximum(peak, size)
        blocks[f] = over_lanes(peak)
        return carry

    lax.fori_loop(0, FIELDS, transform_field, 0)

    me = lax.axis_index("section")
    if rows % 8 == 0:
        for k in range(count):
            p = partner_of(me, k, count)
            for j in range(total):
                outs[k][j // depth, j % depth] = coefficients[j, pl.ds(pl.multiple_of(p * rows, 8), rows), :]
    else:
        for p in range(count):
            staged[p] = coefficients[:, p * rows : (p + 1) * rows, :]
        for k in range(count):
            p = partner_of(me, k, count)
            for j in range(total):
                outs[k][j // depth, j % depth] = staged[p, j]


def transform_bricks(count, conserved, left, right, matrix):
    fields, depth, y, width = conserved.shape
    total = fields * depth
    rows, tall = y // count, y + 2 * PAD
    chunk = array((FIELDS, depth, rows, width))
    message = array((4 * total + COLUMN_ROWS, width))
    rim = array((total, 2 * PAD, width))
    results = pl.pallas_call(
        functools.partial(brick_kernel, count),
        out_shape=[chunk] * count + [message] * 2 + [array((FIELDS, y // 4, width))] + [rim] * 3,
        in_specs=[vmem()] * 4,
        out_specs=[vmem()] * (count + 6),
        scratch_shapes=[
            pltpu.VMEM((total, tall, width), jnp.float32),
            pltpu.VMEM((total, tall, width), jnp.float32),
            pltpu.VMEM((total, tall, width), jnp.float32),
            pltpu.VMEM((2, FIELDS, y, width), jnp.float32),
            pltpu.VMEM((total, y, width), jnp.float32),
            pltpu.VMEM((depth * y, 2 * width), jnp.bfloat16),
            pltpu.VMEM((total, y, width), jnp.float32),
            pltpu.VMEM((1, 1, 8, LANES) if rows % 8 == 0 else (count, total, rows, width), jnp.float32),
        ],
        compiler_params=kernel_params(),
    )(conserved, left, right, matrix)
    return results[:count], results[count : count + 2], results[count + 2], results[count + 3 :]


def leaving_order(count):
    return [*range(2, count), 1, 0]


def mend_kernel(count, *refs):
    chunks, refs = refs[:count], refs[count:]
    top, bottom, blocks, rim_a, rim_d, rim_u, matrix = refs[:7]
    outs, mended, refs = refs[7 : 7 + count], refs[7 + count], refs[8 + count :]
    halo, columns, across, down, up, folded, split, result, fixed = refs
    fields, depth, rows, width = chunks[0].shape
    total = fields * depth
    nb = blocks.shape[1]

    halo[...] = jnp.ones(halo.shape, jnp.float32)
    columns[...] = jnp.ones(columns.shape, jnp.float32)
    for j in range(total):
        halo[j, 4:8, :] = top[4 * j : 4 * j + 4, :]
        halo[j, 8:12, :] = bottom[4 * j : 4 * j + 4, :]
    for side in range(2):
        place = 4 * total + 4 * side
        columns[side, 4:8, :] = top[place : place + 4, :]
        columns[side, 8:12, :] = bottom[place : place + 4, :]
    low = column_terms(columns[0], depth, COURANT)
    high = column_terms(columns[1], depth, -COURANT)
    for z in range(depth):
        c = [halo[f * depth + z] for f in range(fields)]
        for f, values in enumerate(row_terms(c, low, high, z)):
            j = f * depth + z
            for value, rim, target in zip(values, (rim_a, rim_d, rim_u), (across, down, up)):
                target[j, 0:8, :] = value[0:8]
                target[j, 8:24, :] = rim[j]
                target[j, 24:32, :] = value[8:16]
    for j in range(total):
        for k, value in enumerate(fold_rows(across, down, up, j, PAD, 2, 12)):
            folded[j, 2 * k : 2 * k + 2, :] = value
    for f in range(fields):
        values = butterfly(*[folded[f * depth + z] for z in range(4)])
        for half in range(2):
            both = jnp.concatenate(values[2 * half : 2 * half + 2], axis=0)
            upper, lower = halves(both)
            place = f * 32 + half * 16
            split[place : place + 16, 0:width] = upper
            split[place : place + 16, width : 2 * width] = lower
    product = jnp.dot(split[...], matrix[...], preferred_element_type=jnp.float32)
    result[...] = product[:, 0:width] + product[:, width : 2 * width]
    for j in range(total):
        for side in range(2):
            fixed[side, j] = result[pl.ds(8 * j + side, 4, stride=2), :]
    mended[...] = blocks[...]
    for f in range(fields):
        for side in range(2):
            size = jnp.abs(fixed[side, f * depth])
            for z in range(1, depth):
                size = jnp.maximum(size, jnp.abs(fixed[side, f * depth + z]))
            peak = over_lanes(jnp.max(size, axis=0, keepdims=True))
            row = side * (nb - 1)
            mended[f, row : row + 1, :] = peak

    me = lax.axis_index("section")
    for i, k in enumerate(leaving_order(count)):
        p = partner_of(me, k, count)
        for side, start in ((0, 0), (1, rows - 4)):

            @pl.when(p == side * (count - 1))
            def replace(i=i, side=side, start=start):
                for j in range(total):
                    outs[i][j // depth, j % depth, start : start + 4, :] = fixed[side, j]


def mend(count, chunks, top, bottom, blocks, rims, matrix):
    fields, depth, rows, width = chunks[0].shape
    total = fields * depth
    tall = pltpu.VMEM((total, 4 * PAD, width), jnp.float32)
    results = pl.pallas_call(
        functools.partial(mend_kernel, count),
        out_shape=[array(chunks[0].shape)] * count + [array(blocks.shape)],
        in_specs=[vmem()] * (count + 7),
        out_specs=[vmem()] * (count + 1),
        input_output_aliases={k: k for k in range(count)},
        scratch_shapes=[
            pltpu.VMEM((total, 2 * PAD, width), jnp.float32),
            pltpu.VMEM((2, 2 * PAD, width), jnp.float32),
            tall,
            tall,
            tall,
            pltpu.VMEM((total, 8, width), jnp.float32),
            pltpu.VMEM((8 * total, 2 * width), jnp.bfloat16),
            pltpu.VMEM((8 * total, width), jnp.float32),
            pltpu.VMEM((2, total, 4, width), jnp.float32),
        ],
        compiler_params=kernel_params(),
    )(*[chunks[k] for k in leaving_order(count)], top, bottom, blocks, *rims, matrix)
    return dict(zip(leaving_order(count), results)), results[count]


def group_kernel(count, groups, own_rows, *refs):
    blocks, refs = refs[0], refs[1:]
    messages, (peaks, gathered, listed, packed, table) = refs[:count], refs[count:]
    nb = blocks.shape[1]
    me = lax.axis_index("section")
    slot = slot_of(messages[0], me)
    within = lax.rem(slot, 4) * 32
    tile = lax.div(slot, 4)
    for d, message in enumerate(messages):
        height = gathered.shape[1]
        value = message[message.shape[0] - height :, :]
        if count > 4:
            value = pltpu.roll(value, lax.rem(height - tile * own_rows, height), 0)
        gathered[lax.rem(me + count - d, count)] = value
    for q in range(count):
        listed[q * own_rows : (q + 1) * own_rows, :] = gathered[q, 0:own_rows, :]
    part = nb // 4
    band = lax.div(lanes_of((part, LANES)), 32)
    labels = jnp.zeros((part, LANES), jnp.float32)
    for c in range(4):
        turned = pltpu.roll(listed[c * part : (c + 1) * part, :], lax.rem(32 * c - within + LANES, LANES), 1)
        labels = jnp.where(band == c, turned, labels)
    for f in range(FIELDS):
        own = jnp.zeros((part, LANES), jnp.float32)
        for c in range(4):
            own = jnp.where(band == c, blocks[f, c * part : (c + 1) * part, :], own)
        packed[f, 0:part, :] = own
    lane8 = lanes_of((8, LANES))
    sub8 = lax.broadcasted_iota(jnp.int32, (8, LANES), 0)
    label_rows = [jnp.broadcast_to(labels[r : r + 1], (8, LANES)) for r in range(part)]

    def group_tile(g, carry):
        wanted = (sub8 + g * 8).astype(jnp.float32)
        matches = [label_rows[r] == wanted for r in range(part)]
        found = jnp.zeros((8, LANES), jnp.float32)
        for f in range(FIELDS):
            best = jnp.zeros((8, LANES), jnp.float32)
            for r in range(part):
                row = jnp.broadcast_to(packed[f, r : r + 1, :], (8, LANES))
                best = jnp.maximum(best, jnp.where(matches[r], row, 0.0))
            found = jnp.where(lane8 == f, jnp.max(best, axis=1, keepdims=True), found)
        table[pl.ds(pl.multiple_of(g * 8, 8), 8), :] = found
        return carry

    high = table.shape[0]
    if groups < high:
        table[...] = jnp.zeros((high, LANES), jnp.float32)
    lax.fori_loop(0, pl.cdiv(groups, 8), group_tile, 0)
    for g in range(high // LANES):
        peaks[:, g * LANES : (g + 1) * LANES] = jnp.transpose(table[g * LANES : (g + 1) * LANES, :])[0:8]


def group_maxima(count, groups, own_rows, blocks, messages):
    high = pl.cdiv(groups, LANES) * LANES
    nb = blocks.shape[1]
    return pl.pallas_call(
        functools.partial(group_kernel, count, groups, own_rows),
        out_shape=array((8, high)),
        in_specs=[vmem()] * (count + 1),
        out_specs=vmem(),
        scratch_shapes=[
            pltpu.VMEM((count, messages[0].shape[0], LANES), jnp.float32),
            pltpu.VMEM((nb, LANES), jnp.float32),
            pltpu.VMEM((FIELDS, 8, LANES), jnp.float32),
            pltpu.VMEM((high, LANES), jnp.float32),
        ],
        compiler_params=kernel_params(),
    )(blocks, *messages)


def scale_kernel(count, groups, *refs):
    chunks, refs = refs[:count], refs[count:]
    peaks, labels, coded, group_peak, wide = refs
    fields, depth, rows, width = chunks[0].shape
    nb = rows // 4
    high = peaks.shape[1]
    me = lax.axis_index("section")
    group_peak[...] = peaks[0:fields, 0:groups]
    own_labels = labels[...].astype(jnp.int32)
    lane = lanes_of((8, LANES))
    inverse = 1.0 / (peaks[...] + EPSILON)
    tables = [
        [jnp.broadcast_to(inverse[f : f + 1, g * LANES : (g + 1) * LANES], (8, LANES)) for g in range(high // LANES)]
        for f in range(fields)
    ]
    for i, k in enumerate(leaving_order(count)):
        slot = slot_of(labels, sender_of(me, k, count))
        tile = own_labels
        if count > 4:
            tile = pltpu.roll(tile, lax.rem(LABEL_ROWS - lax.div(slot, 4) * nb, LABEL_ROWS), 0)
        within = lax.rem(slot, 4) * 32 + lax.rem(lane, 32)
        own = jnp.take_along_axis(tile, within, axis=1)
        place = pl.ds(pl.multiple_of(slot * width, width), width)
        for f in range(fields):
            if high == LANES:
                found = jnp.take_along_axis(tables[f][0], own, axis=1)
            else:
                found = jnp.zeros((8, LANES), jnp.float32)
                inside = lax.rem(own, LANES)
                for g in range(high // LANES):
                    here = jnp.take_along_axis(tables[f][g], inside, axis=1)
                    found = jnp.where(lax.div(own, LANES) == g, here, found)
            for m in range(4):
                wide[i, f, pl.ds(m, nb, stride=4), :] = found[0:nb]
            factor = wide[i, f]
            for z in range(depth):
                coded[f, z, :, place] = chunks[i][f, z] * factor


def scale(count, groups, chunks, peaks, labels):
    fields, depth, rows, width = chunks[0].shape
    return pl.pallas_call(
        functools.partial(scale_kernel, count, groups),
        out_shape=[array((fields, depth, rows, width * count)), array((fields, groups))],
        in_specs=[vmem()] * (count + 2),
        out_specs=[vmem()] * 2,
        scratch_shapes=[
            pltpu.VMEM((count, fields, rows, width), jnp.float32),
        ],
        compiler_params=kernel_params(),
    )(*chunks, peaks, labels)


def ring(axis, shift):
    count = lax.axis_size(axis)
    return [(i, (i + shift) % count) for i in range(count)]


def exchange_pairs(count, k):
    if count & (count - 1) == 0:
        return [(i, i ^ k) for i in range(count)]
    return [(i, (i + k) % count) for i in range(count)]


def steps_over(axis):
    count = lax.axis_size(axis)
    span, shifts = 1, []
    while span < count:
        shifts.append(min(span, count - span))
        span += shifts[-1]
    return shifts


def with_others(value, axis, shifts):
    count = lax.axis_size(axis)
    others = [lax.ppermute(value, axis, exchange_pairs(count, k)) for k in shifts]
    return functools.reduce(jnp.maximum, others, value)


def per_device(density, momentum, energy, membership, slot_of_brick):
    count = lax.axis_size("section")
    groups = 2 * lax.axis_size("sim") * count
    conserved = jnp.concatenate([density[None], momentum, energy[None]], axis=0)
    matrix, first_x, last_x, labels = pack(conserved, membership, slot_of_brick)
    left = lax.ppermute(last_x, "section", ring("section", 1))
    right = lax.ppermute(first_x, "section", ring("section", -1))
    far = [lax.ppermute(labels, "section", ring("section", d)) for d in range(2, count - 1)]
    chunks, (first_y, last_y), blocks, rims = transform_bricks(count, conserved, left, right, matrix)
    top = lax.ppermute(last_y, "sim", ring("sim", 1))
    bottom = lax.ppermute(first_y, "sim", ring("sim", -1))
    top, *far = lax.optimization_barrier((top, *far))
    chunks, blocks = mend(count, chunks, top, bottom, blocks, rims, matrix)
    moved = {0: chunks[0]}
    for k in leaving_order(count)[:-1]:
        moved[k] = lax.ppermute(chunks[k], "section", exchange_pairs(count, k))
    peaks = group_maxima(count, groups, membership.shape[0], blocks, [labels, left, *far, right])
    for shift in steps_over("sim"):
        peaks = with_others(peaks, "sim", [shift])
    for shift in steps_over("section"):
        peaks = with_others(peaks, "section", [shift])
    return tuple(scale(count, groups, [moved[k] for k in leaving_order(count)], peaks, labels))


def solution(mesh):
    placed = (
        P(None, "sim", "section"),
        P(None, None, "sim", "section"),
        P(None, "sim", "section"),
        P(("sim", "section"), None),
        P("sim", None),
    )
    return jax.shard_map(
        per_device,
        mesh=mesh,
        in_specs=placed,
        out_specs=(P(None, None, ("sim", "section"), None), P()),
        check_vma=False,
    )
```

```python
import functools

import jax
import jax.numpy as jnp
import numpy as np
from jax import lax
from jax.experimental import pallas as pl
from jax.experimental.pallas import tpu as pltpu
from jax.sharding import PartitionSpec as P

GAMMA_LESS = 0.4
COURANT = 0.05
DIFFUSE = 0.1
EPSILON = 1e-06
FIELDS = 5
PAD = 8
COLUMN_ROWS = 8
LABEL_ROWS = 8
LANES = 128
EVEN = 0.5
WIDE = float(np.sqrt(0.5) * np.cos(np.pi / 8))
NARROW = float(np.sqrt(0.5) * np.cos(3 * np.pi / 8))
VMEM_LIMIT = 48 * 1024 * 1024


def vmem():
    return pl.BlockSpec(memory_space=pltpu.VMEM)


def lanes_of(shape):
    return lax.broadcasted_iota(jnp.int32, shape, 1)


def butterfly(a, b, c, d):
    s, t, u, v = a + d, b + c, a - d, b - c
    return (
        EVEN * (s + t),
        WIDE * u + NARROW * v,
        EVEN * (s - t),
        NARROW * u - WIDE * v,
    )


def cosine(k, d):
    factor = 0.5 if k == 0 else np.sqrt(0.5)
    return float(factor * np.cos(np.pi * (2 * d + 1) * k / 8))


def write_matrix(matrix, width):
    step = 16
    row = lax.broadcasted_iota(jnp.int32, (step, width), 0)
    column = lanes_of((step, width))
    quarter = width // 4
    k, j, d = lax.div(column, quarter), lax.rem(column, quarter), lax.rem(row, 4)
    entry = jnp.zeros((step, width), jnp.float32)
    for a in range(4):
        for b in range(4):
            entry = jnp.where(jnp.logical_and(k == a, d == b), cosine(a, b), entry)
    high = entry.astype(jnp.bfloat16).astype(jnp.float32)
    low = entry - high
    zero = jnp.zeros((step, width), jnp.bfloat16)
    for start in range(0, width, step):
        own = j == lax.div(row + start, 4)
        upper = jnp.where(own, high, 0.0).astype(jnp.bfloat16)
        lower = jnp.where(own, low, 0.0).astype(jnp.bfloat16)
        matrix[start : start + step, 0:width] = upper
        matrix[start : start + step, width : 2 * width] = lower
        matrix[width + start : width + start + step, 0:width] = upper
        matrix[width + start : width + start + step, width : 2 * width] = zero


def kernel_params():
    return pltpu.CompilerParams(vmem_limit_bytes=VMEM_LIMIT)


def array(shape, dtype=jnp.float32):
    return jax.ShapeDtypeStruct(shape, dtype)


def pack_kernel(conserved, membership, slots, matrix, first_x, last_x, labels):
    fields, depth, y, width = conserved.shape
    quarter = y // 4
    lane = lanes_of((y, width))
    first = jnp.zeros((y, width), jnp.float32)
    last = jnp.zeros((y, width), jnp.float32)
    for j in range(fields * depth):
        value = conserved[j // depth, j % depth]
        first = jnp.where(lane == j, pltpu.roll(value, j, 1) if j else value, first)
        last = jnp.where(lane == j, pltpu.roll(value, j + 1, 1), last)
    rows, columns = membership.shape
    labels[...] = jnp.zeros(labels.shape, jnp.float32)
    for t in range(columns // LANES):
        part = membership[:, t * LANES : (t + 1) * LANES].astype(jnp.float32)
        labels[t * rows : (t + 1) * rows, :] = part
    labels[LABEL_ROWS - 1 : LABEL_ROWS, 0 : slots.shape[1]] = slots[...].astype(jnp.float32)
    own = labels[...]
    for column, out in ((first, first_x), (last, last_x)):
        packed = column[0:quarter]
        for c in range(1, 4):
            packed = packed + pltpu.roll(column[c * quarter : (c + 1) * quarter], 32 * c, 1)
        out[0:quarter, :] = packed
        out[quarter:, :] = own
    write_matrix(matrix, width)


def pack(conserved, membership, slots):
    y, width = conserved.shape[2:]
    shapes = [
        array((2 * width, 2 * width), jnp.bfloat16),
        array((y // 4 + LABEL_ROWS, width)),
        array((y // 4 + LABEL_ROWS, width)),
        array((LABEL_ROWS, width)),
    ]
    return pl.pallas_call(
        pack_kernel,
        out_shape=shapes,
        in_specs=[vmem()] * 3,
        out_specs=[vmem()] * 4,
        compiler_params=kernel_params(),
    )(conserved, membership, slots)


def slot_of(labels, brick):
    row = labels[LABEL_ROWS - 1 : LABEL_ROWS, :]
    return jnp.max(jnp.where(lanes_of(row.shape) == brick, row, 0.0)).astype(jnp.int32)


def fluxes(c):
    rho, mx, my, mz, e = c
    inverse = 1.0 / rho
    u, v = mx * inverse, my * inverse
    pressure = GAMMA_LESS * (e - 0.5 * (mx * mx + my * my + mz * mz) * inverse)
    total = e + pressure
    flux_x = (mx, mx * u + pressure, my * u, mz * u, total * u)
    flux_y = (my, mx * v, my * v + pressure, mz * v, total * v)
    return flux_x, flux_y


def column_terms(own, depth, sign):
    fields = [pltpu.roll(own, LANES - depth * f, 1) if f else own for f in range(FIELDS)]
    flux_x, unused = fluxes(fields)
    return [DIFFUSE * fields[f] + sign * flux_x[f] for f in range(FIELDS)]


def row_terms(c):
    rows, width = c[0].shape
    lane = lanes_of((rows, width))
    flux_x, flux_y = fluxes(c)
    terms = []
    for f in range(FIELDS):
        base = DIFFUSE * c[f]
        gx, gy = COURANT * flux_x[f], COURANT * flux_y[f]
        from_left = jnp.where(lane == 0, 0.0, pltpu.roll(base + gx, 1, 1))
        from_right = jnp.where(lane == width - 1, 0.0, pltpu.roll(base - gx, width - 1, 1))
        terms.append(((1.0 - 4.0 * DIFFUSE) * c[f] + from_left + from_right, base + gy, base - gy))
    return terms


def beside(low, high, z):
    rows, width = low.shape
    lane = lanes_of((rows, width))
    at_left = pltpu.roll(low, LANES - z, 1) if z else low
    at_right = pltpu.roll(high, LANES - 1 - z, 1)
    return jnp.where(lane == 0, at_left, jnp.where(lane == width - 1, at_right, 0.0))


def fold_rows(across, down, up, j, origin, number, stride):
    t = {}
    for o in range(-3, 7):
        t[o] = (
            across[j, pl.ds(origin + o, number, stride=stride), :]
            + down[j, pl.ds(origin + o - 1, number, stride=stride), :]
            + up[j, pl.ds(origin + o + 1, number, stride=stride), :]
        )
    residual = [
        t[m] - (9.0 / 16.0) * (t[m - 1] + t[m + 1]) + (1.0 / 16.0) * (t[m - 3] + t[m + 3])
        for m in range(4)
    ]
    return butterfly(*residual)


def halves(value):
    high = value.astype(jnp.bfloat16)
    return high, (value - high.astype(jnp.float32)).astype(jnp.bfloat16)


def over_lanes(peak):
    peak = jnp.maximum(peak, pltpu.roll(peak, 64, 1))
    return jnp.maximum(peak, pltpu.roll(peak, 32, 1))


def partner_of(me, k, count):
    if count & (count - 1) == 0:
        return me ^ k
    return lax.rem(me + k, count)


def sender_of(me, k, count):
    if count & (count - 1) == 0:
        return me ^ k
    return lax.rem(me - k + count, count)


def flux_kernel(conserved, across, down, up):
    fields, depth, y, width = conserved.shape
    step = 16

    def flux_rows(i, carry):
        r = pl.ds(pl.multiple_of(i * step, step), step)
        padded = pl.ds(pl.multiple_of(i * step + PAD, PAD), step)
        for z in range(depth):
            for f, (a, d, u) in enumerate(row_terms([conserved[f, z, r, :] for f in range(fields)])):
                j = f * depth + z
                across[j, r, :] = a
                down[j, padded, :] = d
                up[j, padded, :] = u
        return carry

    lax.fori_loop(0, y // step, flux_rows, 0)


def own_fluxes(conserved):
    fields, depth, y, width = conserved.shape
    total = fields * depth
    tall = array((total, y + 2 * PAD, width))
    return pl.pallas_call(
        flux_kernel,
        out_shape=[array((total, y, width)), tall, tall],
        in_specs=[vmem()],
        out_specs=[vmem()] * 3,
        compiler_params=kernel_params(),
        cost_estimate=pl.CostEstimate(flops=40 * total * y * width, bytes_accessed=16 * total * y * width, transcendentals=0),
    )(conserved)


def edge_kernel(conserved, left, right, first_y, last_y, columns):
    fields, depth, y, width = conserved.shape
    total, quarter = fields * depth, y // 4
    for side, column in enumerate((left, right)):
        for c in range(4):
            value = column[0:quarter, :]
            value = pltpu.roll(value, LANES - 32 * c, 1) if c else value
            columns[side, c * quarter : (c + 1) * quarter, :] = value
        place = 4 * total + 4 * side
        first_y[place : place + 4, :] = columns[side, 0:4, :]
        last_y[place : place + 4, :] = columns[side, y - 4 : y, :]
    for j in range(total):
        first_y[4 * j : 4 * j + 4, :] = conserved[j // depth, j % depth, 0:4, :]
        last_y[4 * j : 4 * j + 4, :] = conserved[j // depth, j % depth, y - 4 : y, :]


def edge_rows(conserved, left, right):
    fields, depth, y, width = conserved.shape
    message = array((4 * fields * depth + COLUMN_ROWS, width))
    return pl.pallas_call(
        edge_kernel,
        out_shape=[message, message, array((2, y, width))],
        in_specs=[vmem()] * 3,
        out_specs=[vmem()] * 3,
        compiler_params=kernel_params(),
    )(conserved, left, right)


def brick_kernel(count, *refs):
    inside, down, up, columns, matrix = refs[:5]
    outs, refs = refs[5 : 5 + count], refs[5 + count :]
    blocks, rim_a, rim_d, rim_u, across, edges, folded, split, coefficients, staged = refs
    total, y, width = inside.shape
    depth = total // FIELDS
    nb = y // 4
    rows = y // count

    for side in range(2):
        for f, value in enumerate(column_terms(columns[side], depth, COURANT if side == 0 else -COURANT)):
            edges[side, f] = value

    step = 24

    def join_rows(i, carry):
        r = pl.ds(pl.multiple_of(i * step, 8), step)
        padded = pl.ds(pl.multiple_of(i * step + PAD, PAD), step)
        for f in range(FIELDS):
            low, high = edges[0, f, r, :], edges[1, f, r, :]
            for z in range(depth):
                j = f * depth + z
                across[j, padded, :] = inside[j, r, :] + beside(low, high, z)
        return carry

    lax.fori_loop(0, y // step, join_rows, 0)

    def predict_rows(j, carry):
        for k, value in enumerate(fold_rows(across, down, up, j, PAD, nb, 4)):
            folded[j, k * nb : (k + 1) * nb, :] = value
        for source, rim in ((across, rim_a), (down, rim_d), (up, rim_u)):
            rim[j, 0:8, :] = source[j, PAD : PAD + 8, :]
            rim[j, 8:16, :] = source[j, y : y + 8, :]
        return carry

    lax.fori_loop(0, total, predict_rows, 0)

    piece = 32

    def transform_field(f, carry):
        for start in range(0, y, piece):
            values = [folded[f * depth + z, start : start + piece, :] for z in range(4)]
            for k, value in enumerate(butterfly(*values)):
                high, low = halves(value)
                split[k * y + start : k * y + start + piece, 0:width] = high
                split[k * y + start : k * y + start + piece, width : 2 * width] = low
        product = jnp.dot(split[...], matrix[...], preferred_element_type=jnp.float32)
        result = product[:, 0:width] + product[:, width : 2 * width]
        peak = None
        for k in range(4):
            for m in range(4):
                value = result[k * y + m * nb : k * y + (m + 1) * nb]
                coefficients[f * depth + k, pl.ds(m, nb, stride=4), :] = value
                size = jnp.abs(value)
                peak = size if peak is None else jnp.maximum(peak, size)
        blocks[f] = over_lanes(peak)
        return carry

    lax.fori_loop(0, FIELDS, transform_field, 0)

    me = lax.axis_index("section")
    if rows % 8 == 0:
        for k in range(count):
            p = partner_of(me, k, count)
            for j in range(total):
                outs[k][j // depth, j % depth] = coefficients[j, pl.ds(pl.multiple_of(p * rows, 8), rows), :]
    else:
        for p in range(count):
            staged[p] = coefficients[:, p * rows : (p + 1) * rows, :]
        for k in range(count):
            p = partner_of(me, k, count)
            for j in range(total):
                outs[k][j // depth, j % depth] = staged[p, j]


def transform_bricks(count, inside, down, up, columns, matrix):
    total, y, width = inside.shape
    depth = total // FIELDS
    rows, tall = y // count, y + 2 * PAD
    chunk = array((FIELDS, depth, rows, width))
    rim = array((total, 2 * PAD, width))
    results = pl.pallas_call(
        functools.partial(brick_kernel, count),
        out_shape=[chunk] * count + [array((FIELDS, y // 4, width))] + [rim] * 3,
        in_specs=[vmem()] * 5,
        out_specs=[vmem()] * (count + 4),
        scratch_shapes=[
            pltpu.VMEM((total, tall, width), jnp.float32),
            pltpu.VMEM((2, FIELDS, y, width), jnp.float32),
            pltpu.VMEM((total, y, width), jnp.float32),
            pltpu.VMEM((depth * y, 2 * width), jnp.bfloat16),
            pltpu.VMEM((total, y, width), jnp.float32),
            pltpu.VMEM((1, 1, 8, LANES) if rows % 8 == 0 else (count, total, rows, width), jnp.float32),
        ],
        compiler_params=kernel_params(),
        cost_estimate=pl.CostEstimate(flops=80 * total * y * width, bytes_accessed=16 * total * y * width, transcendentals=0),
    )(inside, down, up, columns, matrix)
    return results[:count], results[count], results[count + 1 :]


def leaving_order(count):
    return [*range(2, count), 1, 0]


def mend_kernel(count, *refs):
    chunks, refs = refs[:count], refs[count:]
    top, bottom, blocks, rim_a, rim_d, rim_u, matrix = refs[:7]
    outs, mended, refs = refs[7 : 7 + count], refs[7 + count], refs[8 + count :]
    halo, columns, across, down, up, folded, split, result, fixed = refs
    fields, depth, rows, width = chunks[0].shape
    total = fields * depth
    nb = blocks.shape[1]

    halo[...] = jnp.ones(halo.shape, jnp.float32)
    columns[...] = jnp.ones(columns.shape, jnp.float32)
    for j in range(total):
        halo[j, 4:8, :] = top[4 * j : 4 * j + 4, :]
        halo[j, 8:12, :] = bottom[4 * j : 4 * j + 4, :]
    for side in range(2):
        place = 4 * total + 4 * side
        columns[side, 4:8, :] = top[place : place + 4, :]
        columns[side, 8:12, :] = bottom[place : place + 4, :]
    low = column_terms(columns[0], depth, COURANT)
    high = column_terms(columns[1], depth, -COURANT)
    for z in range(depth):
        c = [halo[f * depth + z] for f in range(fields)]
        for f, (a, d, u) in enumerate(row_terms(c)):
            j = f * depth + z
            values = (a + beside(low[f], high[f], z), d, u)
            for value, rim, target in zip(values, (rim_a, rim_d, rim_u), (across, down, up)):
                target[j, 0:8, :] = value[0:8]
                target[j, 8:24, :] = rim[j]
                target[j, 24:32, :] = value[8:16]
    for j in range(total):
        for k, value in enumerate(fold_rows(across, down, up, j, PAD, 2, 12)):
            folded[j, 2 * k : 2 * k + 2, :] = value
    for f in range(fields):
        values = butterfly(*[folded[f * depth + z] for z in range(4)])
        for half in range(2):
            both = jnp.concatenate(values[2 * half : 2 * half + 2], axis=0)
            upper, lower = halves(both)
            place = f * 32 + half * 16
            split[place : place + 16, 0:width] = upper
            split[place : place + 16, width : 2 * width] = lower
    product = jnp.dot(split[...], matrix[...], preferred_element_type=jnp.float32)
    result[...] = product[:, 0:width] + product[:, width : 2 * width]
    for j in range(total):
        for side in range(2):
            fixed[side, j] = result[pl.ds(8 * j + side, 4, stride=2), :]
    mended[...] = blocks[...]
    for f in range(fields):
        for side in range(2):
            size = jnp.abs(fixed[side, f * depth])
            for z in range(1, depth):
                size = jnp.maximum(size, jnp.abs(fixed[side, f * depth + z]))
            peak = over_lanes(jnp.max(size, axis=0, keepdims=True))
            row = side * (nb - 1)
            mended[f, row : row + 1, :] = peak

    me = lax.axis_index("section")
    for i, k in enumerate(leaving_order(count)):
        p = partner_of(me, k, count)
        for side, start in ((0, 0), (1, rows - 4)):

            @pl.when(p == side * (count - 1))
            def replace(i=i, side=side, start=start):
                for j in range(total):
                    outs[i][j // depth, j % depth, start : start + 4, :] = fixed[side, j]


def mend(count, chunks, top, bottom, blocks, rims, matrix):
    fields, depth, rows, width = chunks[0].shape
    total = fields * depth
    tall = pltpu.VMEM((total, 4 * PAD, width), jnp.float32)
    results = pl.pallas_call(
        functools.partial(mend_kernel, count),
        out_shape=[array(chunks[0].shape)] * count + [array(blocks.shape)],
        in_specs=[vmem()] * (count + 7),
        out_specs=[vmem()] * (count + 1),
        input_output_aliases={k: k for k in range(count)},
        scratch_shapes=[
            pltpu.VMEM((total, 2 * PAD, width), jnp.float32),
            pltpu.VMEM((2, 2 * PAD, width), jnp.float32),
            tall,
            tall,
            tall,
            pltpu.VMEM((total, 8, width), jnp.float32),
            pltpu.VMEM((8 * total, 2 * width), jnp.bfloat16),
            pltpu.VMEM((8 * total, width), jnp.float32),
            pltpu.VMEM((2, total, 4, width), jnp.float32),
        ],
        compiler_params=kernel_params(),
    )(*[chunks[k] for k in leaving_order(count)], top, bottom, blocks, *rims, matrix)
    return dict(zip(leaving_order(count), results)), results[count]


def group_kernel(count, groups, own_rows, *refs):
    blocks, refs = refs[0], refs[1:]
    messages, (peaks, gathered, listed, packed, table) = refs[:count], refs[count:]
    nb = blocks.shape[1]
    me = lax.axis_index("section")
    slot = slot_of(messages[0], me)
    within = lax.rem(slot, 4) * 32
    tile = lax.div(slot, 4)
    for d, message in enumerate(messages):
        height = gathered.shape[1]
        value = message[message.shape[0] - height :, :]
        if count > 4:
            value = pltpu.roll(value, lax.rem(height - tile * own_rows, height), 0)
        gathered[lax.rem(me + count - d, count)] = value
    for q in range(count):
        listed[q * own_rows : (q + 1) * own_rows, :] = gathered[q, 0:own_rows, :]
    part = nb // 4
    band = lax.div(lanes_of((part, LANES)), 32)
    labels = jnp.zeros((part, LANES), jnp.float32)
    for c in range(4):
        turned = pltpu.roll(listed[c * part : (c + 1) * part, :], lax.rem(32 * c - within + LANES, LANES), 1)
        labels = jnp.where(band == c, turned, labels)
    for f in range(FIELDS):
        own = jnp.zeros((part, LANES), jnp.float32)
        for c in range(4):
            own = jnp.where(band == c, blocks[f, c * part : (c + 1) * part, :], own)
        packed[f, 0:part, :] = own
    lane8 = lanes_of((8, LANES))
    sub8 = lax.broadcasted_iota(jnp.int32, (8, LANES), 0)
    label_rows = [jnp.broadcast_to(labels[r : r + 1], (8, LANES)) for r in range(part)]

    def group_tile(g, carry):
        wanted = (sub8 + g * 8).astype(jnp.float32)
        matches = [label_rows[r] == wanted for r in range(part)]
        found = jnp.zeros((8, LANES), jnp.float32)
        for f in range(FIELDS):
            best = jnp.zeros((8, LANES), jnp.float32)
            for r in range(part):
                row = jnp.broadcast_to(packed[f, r : r + 1, :], (8, LANES))
                best = jnp.maximum(best, jnp.where(matches[r], row, 0.0))
            found = jnp.where(lane8 == f, jnp.max(best, axis=1, keepdims=True), found)
        table[pl.ds(pl.multiple_of(g * 8, 8), 8), :] = found
        return carry

    high = table.shape[0]
    if groups < high:
        table[...] = jnp.zeros((high, LANES), jnp.float32)
    lax.fori_loop(0, pl.cdiv(groups, 8), group_tile, 0)
    for g in range(high // LANES):
        peaks[:, g * LANES : (g + 1) * LANES] = jnp.transpose(table[g * LANES : (g + 1) * LANES, :])[0:8]


def group_maxima(count, groups, own_rows, blocks, messages):
    high = pl.cdiv(groups, LANES) * LANES
    nb = blocks.shape[1]
    return pl.pallas_call(
        functools.partial(group_kernel, count, groups, own_rows),
        out_shape=array((8, high)),
        in_specs=[vmem()] * (count + 1),
        out_specs=vmem(),
        scratch_shapes=[
            pltpu.VMEM((count, messages[0].shape[0], LANES), jnp.float32),
            pltpu.VMEM((nb, LANES), jnp.float32),
            pltpu.VMEM((FIELDS, 8, LANES), jnp.float32),
            pltpu.VMEM((high, LANES), jnp.float32),
        ],
        compiler_params=kernel_params(),
    )(blocks, *messages)


def scale_kernel(count, groups, *refs):
    chunks, refs = refs[:count], refs[count:]
    peaks, labels, coded, group_peak, wide = refs
    fields, depth, rows, width = chunks[0].shape
    nb = rows // 4
    high = peaks.shape[1]
    me = lax.axis_index("section")
    group_peak[...] = peaks[0:fields, 0:groups]
    own_labels = labels[...].astype(jnp.int32)
    lane = lanes_of((8, LANES))
    inverse = 1.0 / (peaks[...] + EPSILON)
    tables = [
        [jnp.broadcast_to(inverse[f : f + 1, g * LANES : (g + 1) * LANES], (8, LANES)) for g in range(high // LANES)]
        for f in range(fields)
    ]
    for i, k in enumerate(leaving_order(count)):
        slot = slot_of(labels, sender_of(me, k, count))
        tile = own_labels
        if count > 4:
            tile = pltpu.roll(tile, lax.rem(LABEL_ROWS - lax.div(slot, 4) * nb, LABEL_ROWS), 0)
        within = lax.rem(slot, 4) * 32 + lax.rem(lane, 32)
        own = jnp.take_along_axis(tile, within, axis=1)
        place = pl.ds(pl.multiple_of(slot * width, width), width)
        for f in range(fields):
            if high == LANES:
                found = jnp.take_along_axis(tables[f][0], own, axis=1)
            else:
                found = jnp.zeros((8, LANES), jnp.float32)
                inside = lax.rem(own, LANES)
                for g in range(high // LANES):
                    here = jnp.take_along_axis(tables[f][g], inside, axis=1)
                    found = jnp.where(lax.div(own, LANES) == g, here, found)
            for m in range(4):
                wide[i, f, pl.ds(m, nb, stride=4), :] = found[0:nb]
            factor = wide[i, f]
            for z in range(depth):
                coded[f, z, :, place] = chunks[i][f, z] * factor


def scale(count, groups, chunks, peaks, labels):
    fields, depth, rows, width = chunks[0].shape
    return pl.pallas_call(
        functools.partial(scale_kernel, count, groups),
        out_shape=[array((fields, depth, rows, width * count)), array((fields, groups))],
        in_specs=[vmem()] * (count + 2),
        out_specs=[vmem()] * 2,
        scratch_shapes=[
            pltpu.VMEM((count, fields, rows, width), jnp.float32),
        ],
        compiler_params=kernel_params(),
    )(*chunks, peaks, labels)


def ring(axis, shift):
    count = lax.axis_size(axis)
    return [(i, (i + shift) % count) for i in range(count)]


def exchange_pairs(count, k):
    if count & (count - 1) == 0:
        return [(i, i ^ k) for i in range(count)]
    return [(i, (i + k) % count) for i in range(count)]


def steps_over(axis):
    count = lax.axis_size(axis)
    span, shifts = 1, []
    while span < count:
        shifts.append(min(span, count - span))
        span += shifts[-1]
    return shifts


def with_others(value, axis, shifts):
    count = lax.axis_size(axis)
    others = [lax.ppermute(value, axis, exchange_pairs(count, k)) for k in shifts]
    return functools.reduce(jnp.maximum, others, value)


def per_device(density, momentum, energy, membership, slot_of_brick):
    count = lax.axis_size("section")
    groups = 2 * lax.axis_size("sim") * count
    conserved = jnp.concatenate([density[None], momentum, energy[None]], axis=0)
    matrix, first_x, last_x, labels = pack(conserved, membership, slot_of_brick)
    left = lax.ppermute(last_x, "section", ring("section", 1))
    right = lax.ppermute(first_x, "section", ring("section", -1))
    far = [lax.ppermute(labels, "section", ring("section", d)) for d in range(2, count - 1)]
    inside, down, up = own_fluxes(conserved)
    left, right, inside = lax.optimization_barrier((left, right, inside))
    first_y, last_y, columns = edge_rows(conserved, left, right)
    first_y, last_y, *far = lax.optimization_barrier((first_y, last_y, *far))
    top = lax.ppermute(last_y, "sim", ring("sim", 1))
    bottom = lax.ppermute(first_y, "sim", ring("sim", -1))
    chunks, blocks, rims = transform_bricks(count, inside, down, up, columns, matrix)
    chunks, blocks = mend(count, chunks, top, bottom, blocks, rims, matrix)
    moved = {0: chunks[0]}
    for k in leaving_order(count)[:-1]:
        moved[k] = lax.ppermute(chunks[k], "section", exchange_pairs(count, k))
    peaks = group_maxima(count, groups, membership.shape[0], blocks, [labels, left, *far, right])
    for shift in steps_over("sim"):
        peaks = with_others(peaks, "sim", [shift])
    for shift in steps_over("section"):
        peaks = with_others(peaks, "section", [shift])
    return tuple(scale(count, groups, [moved[k] for k in leaving_order(count)], peaks, labels))


def solution(mesh):
    placed = (
        P(None, "sim", "section"),
        P(None, None, "sim", "section"),
        P(None, "sim", "section"),
        P(("sim", "section"), None),
        P("sim", None),
    )
    return jax.shard_map(
        per_device,
        mesh=mesh,
        in_specs=placed,
        out_specs=(P(None, None, ("sim", "section"), None), P()),
        check_vma=False,
    )
```

```python
import functools

import jax
import jax.numpy as jnp
import numpy as np
from jax import lax
from jax.experimental import pallas as pl
from jax.experimental.pallas import tpu as pltpu
from jax.sharding import PartitionSpec as P

GAMMA_LESS = 0.4
COURANT = 0.05
DIFFUSE = 0.1
EPSILON = 1e-06
FIELDS = 5
PAD = 8
COLUMN_ROWS = 8
LABEL_ROWS = 8
LANES = 128
EVEN = 0.5
WIDE = float(np.sqrt(0.5) * np.cos(np.pi / 8))
NARROW = float(np.sqrt(0.5) * np.cos(3 * np.pi / 8))
VMEM_LIMIT = 48 * 1024 * 1024


def vmem():
    return pl.BlockSpec(memory_space=pltpu.VMEM)


def lanes_of(shape):
    return lax.broadcasted_iota(jnp.int32, shape, 1)


def butterfly(a, b, c, d):
    s, t, u, v = a + d, b + c, a - d, b - c
    return (
        EVEN * (s + t),
        WIDE * u + NARROW * v,
        EVEN * (s - t),
        NARROW * u - WIDE * v,
    )


def cosine(k, d):
    factor = 0.5 if k == 0 else np.sqrt(0.5)
    return float(factor * np.cos(np.pi * (2 * d + 1) * k / 8))


def write_matrix(matrix, width):
    step = 16
    row = lax.broadcasted_iota(jnp.int32, (step, width), 0)
    column = lanes_of((step, width))
    quarter = width // 4
    k, j, d = lax.div(column, quarter), lax.rem(column, quarter), lax.rem(row, 4)
    entry = jnp.zeros((step, width), jnp.float32)
    for a in range(4):
        for b in range(4):
            entry = jnp.where(jnp.logical_and(k == a, d == b), cosine(a, b), entry)
    high = entry.astype(jnp.bfloat16).astype(jnp.float32)
    low = entry - high
    zero = jnp.zeros((step, width), jnp.bfloat16)
    for start in range(0, width, step):
        own = j == lax.div(row + start, 4)
        upper = jnp.where(own, high, 0.0).astype(jnp.bfloat16)
        lower = jnp.where(own, low, 0.0).astype(jnp.bfloat16)
        matrix[start : start + step, 0:width] = upper
        matrix[start : start + step, width : 2 * width] = lower
        matrix[width + start : width + start + step, 0:width] = upper
        matrix[width + start : width + start + step, width : 2 * width] = zero


def kernel_params():
    return pltpu.CompilerParams(vmem_limit_bytes=VMEM_LIMIT)


def array(shape, dtype=jnp.float32):
    return jax.ShapeDtypeStruct(shape, dtype)


def pack_kernel(conserved, membership, slots, matrix, first_x, last_x, labels):
    fields, depth, y, width = conserved.shape
    quarter = y // 4
    lane = lanes_of((y, width))
    first = jnp.zeros((y, width), jnp.float32)
    last = jnp.zeros((y, width), jnp.float32)
    for j in range(fields * depth):
        value = conserved[j // depth, j % depth]
        first = jnp.where(lane == j, pltpu.roll(value, j, 1) if j else value, first)
        last = jnp.where(lane == j, pltpu.roll(value, j + 1, 1), last)
    rows, columns = membership.shape
    labels[...] = jnp.zeros(labels.shape, jnp.float32)
    for t in range(columns // LANES):
        part = membership[:, t * LANES : (t + 1) * LANES].astype(jnp.float32)
        labels[t * rows : (t + 1) * rows, :] = part
    labels[LABEL_ROWS - 1 : LABEL_ROWS, 0 : slots.shape[1]] = slots[...].astype(jnp.float32)
    own = labels[...]
    for column, out in ((first, first_x), (last, last_x)):
        packed = column[0:quarter]
        for c in range(1, 4):
            packed = packed + pltpu.roll(column[c * quarter : (c + 1) * quarter], 32 * c, 1)
        out[0:quarter, :] = packed
        out[quarter:, :] = own
    write_matrix(matrix, width)


def pack(conserved, membership, slots):
    y, width = conserved.shape[2:]
    shapes = [
        array((2 * width, 2 * width), jnp.bfloat16),
        array((y // 4 + LABEL_ROWS, width)),
        array((y // 4 + LABEL_ROWS, width)),
        array((LABEL_ROWS, width)),
    ]
    return pl.pallas_call(
        pack_kernel,
        out_shape=shapes,
        in_specs=[vmem()] * 3,
        out_specs=[vmem()] * 4,
        compiler_params=kernel_params(),
    )(conserved, membership, slots)


def slot_of(labels, brick):
    row = labels[LABEL_ROWS - 1 : LABEL_ROWS, :]
    return jnp.max(jnp.where(lanes_of(row.shape) == brick, row, 0.0)).astype(jnp.int32)


def fluxes(c):
    rho, mx, my, mz, e = c
    inverse = 1.0 / rho
    u, v = mx * inverse, my * inverse
    pressure = GAMMA_LESS * (e - 0.5 * (mx * mx + my * my + mz * mz) * inverse)
    total = e + pressure
    flux_x = (mx, mx * u + pressure, my * u, mz * u, total * u)
    flux_y = (my, mx * v, my * v + pressure, mz * v, total * v)
    return flux_x, flux_y


def column_terms(own, depth, sign):
    fields = [pltpu.roll(own, LANES - depth * f, 1) if f else own for f in range(FIELDS)]
    flux_x, unused = fluxes(fields)
    return [DIFFUSE * fields[f] + sign * flux_x[f] for f in range(FIELDS)]


def row_terms(c):
    rows, width = c[0].shape
    lane = lanes_of((rows, width))
    flux_x, flux_y = fluxes(c)
    terms = []
    for f in range(FIELDS):
        base = DIFFUSE * c[f]
        gx, gy = COURANT * flux_x[f], COURANT * flux_y[f]
        from_left = jnp.where(lane == 0, 0.0, pltpu.roll(base + gx, 1, 1))
        from_right = jnp.where(lane == width - 1, 0.0, pltpu.roll(base - gx, width - 1, 1))
        terms.append(((1.0 - 4.0 * DIFFUSE) * c[f] + from_left + from_right, base + gy, base - gy))
    return terms


def beside(low, high, z):
    rows, width = low.shape
    lane = lanes_of((rows, width))
    at_left = pltpu.roll(low, LANES - z, 1) if z else low
    at_right = pltpu.roll(high, LANES - 1 - z, 1)
    return jnp.where(lane == 0, at_left, jnp.where(lane == width - 1, at_right, 0.0))


def fold_rows(across, down, up, j, origin, number, stride):
    t = {}
    for o in range(-3, 7):
        t[o] = (
            across[j, pl.ds(origin + o, number, stride=stride), :]
            + down[j, pl.ds(origin + o - 1, number, stride=stride), :]
            + up[j, pl.ds(origin + o + 1, number, stride=stride), :]
        )
    residual = [
        t[m] - (9.0 / 16.0) * (t[m - 1] + t[m + 1]) + (1.0 / 16.0) * (t[m - 3] + t[m + 3])
        for m in range(4)
    ]
    return butterfly(*residual)


def halves(value):
    high = value.astype(jnp.bfloat16)
    return high, (value - high.astype(jnp.float32)).astype(jnp.bfloat16)


def over_lanes(peak):
    peak = jnp.maximum(peak, pltpu.roll(peak, 64, 1))
    return jnp.maximum(peak, pltpu.roll(peak, 32, 1))


def partner_of(me, k, count):
    if count & (count - 1) == 0:
        return me ^ k
    return lax.rem(me + k, count)


def sender_of(me, k, count):
    if count & (count - 1) == 0:
        return me ^ k
    return lax.rem(me - k + count, count)


def flux_kernel(conserved, across, down, up):
    fields, depth, y, width = conserved.shape
    step = 16

    def flux_rows(i, carry):
        r = pl.ds(pl.multiple_of(i * step, step), step)
        padded = pl.ds(pl.multiple_of(i * step + PAD, PAD), step)
        for z in range(depth):
            for f, (a, d, u) in enumerate(row_terms([conserved[f, z, r, :] for f in range(fields)])):
                j = f * depth + z
                across[j, r, :] = a
                down[j, padded, :] = d
                up[j, padded, :] = u
        return carry

    lax.fori_loop(0, y // step, flux_rows, 0)


def own_fluxes(conserved):
    fields, depth, y, width = conserved.shape
    total = fields * depth
    tall = array((total, y + 2 * PAD, width))
    return pl.pallas_call(
        flux_kernel,
        out_shape=[array((total, y, width)), tall, tall],
        in_specs=[vmem()],
        out_specs=[vmem()] * 3,
        compiler_params=kernel_params(),
        cost_estimate=pl.CostEstimate(flops=40 * total * y * width, bytes_accessed=16 * total * y * width, transcendentals=0),
    )(conserved)


def edge_kernel(conserved, left, right, first_y, last_y, columns):
    fields, depth, y, width = conserved.shape
    total, quarter = fields * depth, y // 4
    for side, column in enumerate((left, right)):
        for c in range(4):
            value = column[0:quarter, :]
            value = pltpu.roll(value, LANES - 32 * c, 1) if c else value
            columns[side, c * quarter : (c + 1) * quarter, :] = value
        place = 4 * total + 4 * side
        first_y[place : place + 4, :] = columns[side, 0:4, :]
        last_y[place : place + 4, :] = columns[side, y - 4 : y, :]
    for j in range(total):
        first_y[4 * j : 4 * j + 4, :] = conserved[j // depth, j % depth, 0:4, :]
        last_y[4 * j : 4 * j + 4, :] = conserved[j // depth, j % depth, y - 4 : y, :]


def edge_rows(conserved, left, right):
    fields, depth, y, width = conserved.shape
    message = array((4 * fields * depth + COLUMN_ROWS, width))
    return pl.pallas_call(
        edge_kernel,
        out_shape=[message, message, array((2, y, width))],
        in_specs=[vmem()] * 3,
        out_specs=[vmem()] * 3,
        compiler_params=kernel_params(),
    )(conserved, left, right)


def brick_kernel(count, *refs):
    inside, down, up, columns, matrix = refs[:5]
    outs, refs = refs[5 : 5 + count], refs[5 + count :]
    blocks, rim_a, rim_d, rim_u, across, edges, split, coefficients, staged = refs
    total, y, width = inside.shape
    depth = total // FIELDS
    nb = y // 4
    rows = y // count

    for side in range(2):
        for f, value in enumerate(column_terms(columns[side], depth, COURANT if side == 0 else -COURANT)):
            edges[side, f] = value

    step = 24
    for start in range(0, y, step):
        for f in range(FIELDS):
            low, high = edges[0, f, start : start + step, :], edges[1, f, start : start + step, :]
            for z in range(depth):
                j = f * depth + z
                value = inside[j, start : start + step, :] + beside(low, high, z)
                across[j, PAD + start : PAD + start + step, :] = value
    for j in range(total):
        for source, rim in ((across, rim_a), (down, rim_d), (up, rim_u)):
            rim[j, 0:8, :] = source[j, PAD : PAD + 8, :]
            rim[j, 8:16, :] = source[j, y : y + 8, :]

    for f in range(FIELDS):
        rows_of = [fold_rows(across, down, up, f * depth + z, PAD, nb, 4) for z in range(4)]
        mixed = [butterfly(*[rows_of[z][m] for z in range(4)]) for m in range(4)]
        for k in range(4):
            high, low = halves(jnp.concatenate([mixed[m][k] for m in range(4)], axis=0))
            split[f, k * y : (k + 1) * y, 0:width] = high
            split[f, k * y : (k + 1) * y, width : 2 * width] = low
        product = jnp.dot(split[f], matrix[...], preferred_element_type=jnp.float32)
        result = product[:, 0:width] + product[:, width : 2 * width]
        peak = None
        for k in range(4):
            for m in range(4):
                value = result[k * y + m * nb : k * y + (m + 1) * nb]
                coefficients[f * depth + k, pl.ds(m, nb, stride=4), :] = value
                size = jnp.abs(value)
                peak = size if peak is None else jnp.maximum(peak, size)
        blocks[f] = over_lanes(peak)

    me = lax.axis_index("section")
    if rows % 8 == 0:
        for k in range(count):
            p = partner_of(me, k, count)
            for j in range(total):
                outs[k][j // depth, j % depth] = coefficients[j, pl.ds(pl.multiple_of(p * rows, 8), rows), :]
    else:
        for p in range(count):
            staged[p] = coefficients[:, p * rows : (p + 1) * rows, :]
        for k in range(count):
            p = partner_of(me, k, count)
            for j in range(total):
                outs[k][j // depth, j % depth] = staged[p, j]


def transform_bricks(count, inside, down, up, columns, matrix):
    total, y, width = inside.shape
    depth = total // FIELDS
    rows, tall = y // count, y + 2 * PAD
    chunk = array((FIELDS, depth, rows, width))
    rim = array((total, 2 * PAD, width))
    results = pl.pallas_call(
        functools.partial(brick_kernel, count),
        out_shape=[chunk] * count + [array((FIELDS, y // 4, width))] + [rim] * 3,
        in_specs=[vmem()] * 5,
        out_specs=[vmem()] * (count + 4),
        scratch_shapes=[
            pltpu.VMEM((total, tall, width), jnp.float32),
            pltpu.VMEM((2, FIELDS, y, width), jnp.float32),
            pltpu.VMEM((FIELDS, depth * y, 2 * width), jnp.bfloat16),
            pltpu.VMEM((total, y, width), jnp.float32),
            pltpu.VMEM((1, 1, 8, LANES) if rows % 8 == 0 else (count, total, rows, width), jnp.float32),
        ],
        compiler_params=kernel_params(),
        cost_estimate=pl.CostEstimate(flops=80 * total * y * width, bytes_accessed=16 * total * y * width, transcendentals=0),
    )(inside, down, up, columns, matrix)
    return results[:count], results[count], results[count + 1 :]


def leaving_order(count):
    return [*range(2, count), 1, 0]


def mend_kernel(count, *refs):
    chunks, refs = refs[:count], refs[count:]
    top, bottom, blocks, rim_a, rim_d, rim_u, matrix = refs[:7]
    outs, mended, refs = refs[7 : 7 + count], refs[7 + count], refs[8 + count :]
    halo, columns, across, down, up, folded, split, result, fixed = refs
    fields, depth, rows, width = chunks[0].shape
    total = fields * depth
    nb = blocks.shape[1]

    halo[...] = jnp.ones(halo.shape, jnp.float32)
    columns[...] = jnp.ones(columns.shape, jnp.float32)
    for j in range(total):
        halo[j, 4:8, :] = top[4 * j : 4 * j + 4, :]
        halo[j, 8:12, :] = bottom[4 * j : 4 * j + 4, :]
    for side in range(2):
        place = 4 * total + 4 * side
        columns[side, 4:8, :] = top[place : place + 4, :]
        columns[side, 8:12, :] = bottom[place : place + 4, :]
    low = column_terms(columns[0], depth, COURANT)
    high = column_terms(columns[1], depth, -COURANT)
    for z in range(depth):
        c = [halo[f * depth + z] for f in range(fields)]
        for f, (a, d, u) in enumerate(row_terms(c)):
            j = f * depth + z
            values = (a + beside(low[f], high[f], z), d, u)
            for value, rim, target in zip(values, (rim_a, rim_d, rim_u), (across, down, up)):
                target[j, 0:8, :] = value[0:8]
                target[j, 8:24, :] = rim[j]
                target[j, 24:32, :] = value[8:16]
    for j in range(total):
        for k, value in enumerate(fold_rows(across, down, up, j, PAD, 2, 12)):
            folded[j, 2 * k : 2 * k + 2, :] = value
    for f in range(fields):
        values = butterfly(*[folded[f * depth + z] for z in range(4)])
        for half in range(2):
            both = jnp.concatenate(values[2 * half : 2 * half + 2], axis=0)
            upper, lower = halves(both)
            place = f * 32 + half * 16
            split[place : place + 16, 0:width] = upper
            split[place : place + 16, width : 2 * width] = lower
    product = jnp.dot(split[...], matrix[...], preferred_element_type=jnp.float32)
    result[...] = product[:, 0:width] + product[:, width : 2 * width]
    for j in range(total):
        for side in range(2):
            fixed[side, j] = result[pl.ds(8 * j + side, 4, stride=2), :]
    mended[...] = blocks[...]
    for f in range(fields):
        for side in range(2):
            size = jnp.abs(fixed[side, f * depth])
            for z in range(1, depth):
                size = jnp.maximum(size, jnp.abs(fixed[side, f * depth + z]))
            peak = over_lanes(jnp.max(size, axis=0, keepdims=True))
            row = side * (nb - 1)
            mended[f, row : row + 1, :] = peak

    me = lax.axis_index("section")
    for i, k in enumerate(leaving_order(count)):
        p = partner_of(me, k, count)
        for side, start in ((0, 0), (1, rows - 4)):

            @pl.when(p == side * (count - 1))
            def replace(i=i, side=side, start=start):
                for j in range(total):
                    outs[i][j // depth, j % depth, start : start + 4, :] = fixed[side, j]


def mend(count, chunks, top, bottom, blocks, rims, matrix):
    fields, depth, rows, width = chunks[0].shape
    total = fields * depth
    tall = pltpu.VMEM((total, 4 * PAD, width), jnp.float32)
    results = pl.pallas_call(
        functools.partial(mend_kernel, count),
        out_shape=[array(chunks[0].shape)] * count + [array(blocks.shape)],
        in_specs=[vmem()] * (count + 7),
        out_specs=[vmem()] * (count + 1),
        input_output_aliases={k: k for k in range(count)},
        scratch_shapes=[
            pltpu.VMEM((total, 2 * PAD, width), jnp.float32),
            pltpu.VMEM((2, 2 * PAD, width), jnp.float32),
            tall,
            tall,
            tall,
            pltpu.VMEM((total, 8, width), jnp.float32),
            pltpu.VMEM((8 * total, 2 * width), jnp.bfloat16),
            pltpu.VMEM((8 * total, width), jnp.float32),
            pltpu.VMEM((2, total, 4, width), jnp.float32),
        ],
        compiler_params=kernel_params(),
    )(*[chunks[k] for k in leaving_order(count)], top, bottom, blocks, *rims, matrix)
    return dict(zip(leaving_order(count), results)), results[count]


def group_kernel(count, groups, own_rows, *refs):
    blocks, refs = refs[0], refs[1:]
    messages, (peaks, gathered, listed, packed, table) = refs[:count], refs[count:]
    nb = blocks.shape[1]
    me = lax.axis_index("section")
    slot = slot_of(messages[0], me)
    within = lax.rem(slot, 4) * 32
    tile = lax.div(slot, 4)
    for d, message in enumerate(messages):
        height = gathered.shape[1]
        value = message[message.shape[0] - height :, :]
        if count > 4:
            value = pltpu.roll(value, lax.rem(height - tile * own_rows, height), 0)
        gathered[lax.rem(me + count - d, count)] = value
    for q in range(count):
        listed[q * own_rows : (q + 1) * own_rows, :] = gathered[q, 0:own_rows, :]
    part = nb // 4
    band = lax.div(lanes_of((part, LANES)), 32)
    labels = jnp.zeros((part, LANES), jnp.float32)
    for c in range(4):
        turned = pltpu.roll(listed[c * part : (c + 1) * part, :], lax.rem(32 * c - within + LANES, LANES), 1)
        labels = jnp.where(band == c, turned, labels)
    for f in range(FIELDS):
        own = jnp.zeros((part, LANES), jnp.float32)
        for c in range(4):
            own = jnp.where(band == c, blocks[f, c * part : (c + 1) * part, :], own)
        packed[f, 0:part, :] = own
    lane8 = lanes_of((8, LANES))
    sub8 = lax.broadcasted_iota(jnp.int32, (8, LANES), 0)
    label_rows = [jnp.broadcast_to(labels[r : r + 1], (8, LANES)) for r in range(part)]

    def group_tile(g, carry):
        wanted = (sub8 + g * 8).astype(jnp.float32)
        matches = [label_rows[r] == wanted for r in range(part)]
        found = jnp.zeros((8, LANES), jnp.float32)
        for f in range(FIELDS):
            best = jnp.zeros((8, LANES), jnp.float32)
            for r in range(part):
                row = jnp.broadcast_to(packed[f, r : r + 1, :], (8, LANES))
                best = jnp.maximum(best, jnp.where(matches[r], row, 0.0))
            found = jnp.where(lane8 == f, jnp.max(best, axis=1, keepdims=True), found)
        table[pl.ds(pl.multiple_of(g * 8, 8), 8), :] = found
        return carry

    high = table.shape[0]
    if groups < high:
        table[...] = jnp.zeros((high, LANES), jnp.float32)
    lax.fori_loop(0, pl.cdiv(groups, 8), group_tile, 0)
    for g in range(high // LANES):
        peaks[:, g * LANES : (g + 1) * LANES] = jnp.transpose(table[g * LANES : (g + 1) * LANES, :])[0:8]


def group_maxima(count, groups, own_rows, blocks, messages):
    high = pl.cdiv(groups, LANES) * LANES
    nb = blocks.shape[1]
    return pl.pallas_call(
        functools.partial(group_kernel, count, groups, own_rows),
        out_shape=array((8, high)),
        in_specs=[vmem()] * (count + 1),
        out_specs=vmem(),
        scratch_shapes=[
            pltpu.VMEM((count, messages[0].shape[0], LANES), jnp.float32),
            pltpu.VMEM((nb, LANES), jnp.float32),
            pltpu.VMEM((FIELDS, 8, LANES), jnp.float32),
            pltpu.VMEM((high, LANES), jnp.float32),
        ],
        compiler_params=kernel_params(),
    )(blocks, *messages)


def scale_kernel(count, groups, *refs):
    chunks, refs = refs[:count], refs[count:]
    peaks, labels, coded, group_peak, wide = refs
    fields, depth, rows, width = chunks[0].shape
    nb = rows // 4
    high = peaks.shape[1]
    me = lax.axis_index("section")
    group_peak[...] = peaks[0:fields, 0:groups]
    own_labels = labels[...].astype(jnp.int32)
    lane = lanes_of((8, LANES))
    inverse = 1.0 / (peaks[...] + EPSILON)
    tables = [
        [jnp.broadcast_to(inverse[f : f + 1, g * LANES : (g + 1) * LANES], (8, LANES)) for g in range(high // LANES)]
        for f in range(fields)
    ]
    for i, k in enumerate(leaving_order(count)):
        slot = slot_of(labels, sender_of(me, k, count))
        tile = own_labels
        if count > 4:
            tile = pltpu.roll(tile, lax.rem(LABEL_ROWS - lax.div(slot, 4) * nb, LABEL_ROWS), 0)
        within = lax.rem(slot, 4) * 32 + lax.rem(lane, 32)
        own = jnp.take_along_axis(tile, within, axis=1)
        place = pl.ds(pl.multiple_of(slot * width, width), width)
        for f in range(fields):
            if high == LANES:
                found = jnp.take_along_axis(tables[f][0], own, axis=1)
            else:
                found = jnp.zeros((8, LANES), jnp.float32)
                inside = lax.rem(own, LANES)
                for g in range(high // LANES):
                    here = jnp.take_along_axis(tables[f][g], inside, axis=1)
                    found = jnp.where(lax.div(own, LANES) == g, here, found)
            for m in range(4):
                wide[i, f, pl.ds(m, nb, stride=4), :] = found[0:nb]
            factor = wide[i, f]
            for z in range(depth):
                coded[f, z, :, place] = chunks[i][f, z] * factor


def scale(count, groups, chunks, peaks, labels):
    fields, depth, rows, width = chunks[0].shape
    return pl.pallas_call(
        functools.partial(scale_kernel, count, groups),
        out_shape=[array((fields, depth, rows, width * count)), array((fields, groups))],
        in_specs=[vmem()] * (count + 2),
        out_specs=[vmem()] * 2,
        scratch_shapes=[
            pltpu.VMEM((count, fields, rows, width), jnp.float32),
        ],
        compiler_params=kernel_params(),
    )(*chunks, peaks, labels)


def ring(axis, shift):
    count = lax.axis_size(axis)
    return [(i, (i + shift) % count) for i in range(count)]


def exchange_pairs(count, k):
    if count & (count - 1) == 0:
        return [(i, i ^ k) for i in range(count)]
    return [(i, (i + k) % count) for i in range(count)]


def steps_over(axis):
    count = lax.axis_size(axis)
    span, shifts = 1, []
    while span < count:
        shifts.append(min(span, count - span))
        span += shifts[-1]
    return shifts


def with_others(value, axis, shifts):
    count = lax.axis_size(axis)
    others = [lax.ppermute(value, axis, exchange_pairs(count, k)) for k in shifts]
    return functools.reduce(jnp.maximum, others, value)


def per_device(density, momentum, energy, membership, slot_of_brick):
    count = lax.axis_size("section")
    groups = 2 * lax.axis_size("sim") * count
    conserved = jnp.concatenate([density[None], momentum, energy[None]], axis=0)
    matrix, first_x, last_x, labels = pack(conserved, membership, slot_of_brick)
    left = lax.ppermute(last_x, "section", ring("section", 1))
    right = lax.ppermute(first_x, "section", ring("section", -1))
    far = [lax.ppermute(labels, "section", ring("section", d)) for d in range(2, count - 1)]
    inside, down, up = own_fluxes(conserved)
    left, right, inside = lax.optimization_barrier((left, right, inside))
    first_y, last_y, columns = edge_rows(conserved, left, right)
    first_y, last_y, *far = lax.optimization_barrier((first_y, last_y, *far))
    top = lax.ppermute(last_y, "sim", ring("sim", 1))
    bottom = lax.ppermute(first_y, "sim", ring("sim", -1))
    chunks, blocks, rims = transform_bricks(count, inside, down, up, columns, matrix)
    chunks, blocks = mend(count, chunks, top, bottom, blocks, rims, matrix)
    moved = {0: chunks[0]}
    for k in leaving_order(count)[:-1]:
        moved[k] = lax.ppermute(chunks[k], "section", exchange_pairs(count, k))
    peaks = group_maxima(count, groups, membership.shape[0], blocks, [labels, left, *far, right])
    for shift in steps_over("sim"):
        peaks = with_others(peaks, "sim", [shift])
    for shift in steps_over("section"):
        peaks = with_others(peaks, "section", [shift])
    return tuple(scale(count, groups, [moved[k] for k in leaving_order(count)], peaks, labels))


def solution(mesh):
    placed = (
        P(None, "sim", "section"),
        P(None, None, "sim", "section"),
        P(None, "sim", "section"),
        P(("sim", "section"), None),
        P("sim", None),
    )
    return jax.shard_map(
        per_device,
        mesh=mesh,
        in_specs=placed,
        out_specs=(P(None, None, ("sim", "section"), None), P()),
        check_vma=False,
    )
```

```python
import functools

import jax
import jax.numpy as jnp
import numpy as np
from jax import lax
from jax.experimental import pallas as pl
from jax.experimental.pallas import tpu as pltpu
from jax.sharding import PartitionSpec as P

GAMMA_LESS = 0.4
COURANT = 0.05
DIFFUSE = 0.1
EPSILON = 1e-06
FIELDS = 5
PAD = 8
COLUMN_ROWS = 8
LABEL_ROWS = 8
LANES = 128
EVEN = 0.5
WIDE = float(np.sqrt(0.5) * np.cos(np.pi / 8))
NARROW = float(np.sqrt(0.5) * np.cos(3 * np.pi / 8))
VMEM_LIMIT = 48 * 1024 * 1024


def vmem():
    return pl.BlockSpec(memory_space=pltpu.VMEM)


def lanes_of(shape):
    return lax.broadcasted_iota(jnp.int32, shape, 1)


def butterfly(a, b, c, d):
    s, t, u, v = a + d, b + c, a - d, b - c
    return (
        EVEN * (s + t),
        WIDE * u + NARROW * v,
        EVEN * (s - t),
        NARROW * u - WIDE * v,
    )


def cosine(k, d):
    factor = 0.5 if k == 0 else np.sqrt(0.5)
    return float(factor * np.cos(np.pi * (2 * d + 1) * k / 8))


def write_matrix(matrix, width):
    step = 16
    row = lax.broadcasted_iota(jnp.int32, (step, width), 0)
    column = lanes_of((step, width))
    quarter = width // 4
    k, j, d = lax.div(column, quarter), lax.rem(column, quarter), lax.rem(row, 4)
    entry = jnp.zeros((step, width), jnp.float32)
    for a in range(4):
        for b in range(4):
            entry = jnp.where(jnp.logical_and(k == a, d == b), cosine(a, b), entry)
    high = entry.astype(jnp.bfloat16).astype(jnp.float32)
    low = entry - high
    zero = jnp.zeros((step, width), jnp.bfloat16)
    for start in range(0, width, step):
        own = j == lax.div(row + start, 4)
        upper = jnp.where(own, high, 0.0).astype(jnp.bfloat16)
        lower = jnp.where(own, low, 0.0).astype(jnp.bfloat16)
        matrix[start : start + step, 0:width] = upper
        matrix[start : start + step, width : 2 * width] = lower
        matrix[width + start : width + start + step, 0:width] = upper
        matrix[width + start : width + start + step, width : 2 * width] = zero


def kernel_params():
    return pltpu.CompilerParams(vmem_limit_bytes=VMEM_LIMIT)


def array(shape, dtype=jnp.float32):
    return jax.ShapeDtypeStruct(shape, dtype)


def pack_kernel(conserved, membership, slots, matrix, first_x, last_x, labels):
    fields, depth, y, width = conserved.shape
    quarter = y // 4
    lane = lanes_of((y, width))
    first = jnp.zeros((y, width), jnp.float32)
    last = jnp.zeros((y, width), jnp.float32)
    for j in range(fields * depth):
        value = conserved[j // depth, j % depth]
        first = jnp.where(lane == j, pltpu.roll(value, j, 1) if j else value, first)
        last = jnp.where(lane == j, pltpu.roll(value, j + 1, 1), last)
    rows, columns = membership.shape
    labels[...] = jnp.zeros(labels.shape, jnp.float32)
    for t in range(columns // LANES):
        part = membership[:, t * LANES : (t + 1) * LANES].astype(jnp.float32)
        labels[t * rows : (t + 1) * rows, :] = part
    labels[LABEL_ROWS - 1 : LABEL_ROWS, 0 : slots.shape[1]] = slots[...].astype(jnp.float32)
    own = labels[...]
    for column, out in ((first, first_x), (last, last_x)):
        packed = column[0:quarter]
        for c in range(1, 4):
            packed = packed + pltpu.roll(column[c * quarter : (c + 1) * quarter], 32 * c, 1)
        out[0:quarter, :] = packed
        out[quarter:, :] = own
    write_matrix(matrix, width)


def pack(conserved, membership, slots):
    y, width = conserved.shape[2:]
    shapes = [
        array((2 * width, 2 * width), jnp.bfloat16),
        array((y // 4 + LABEL_ROWS, width)),
        array((y // 4 + LABEL_ROWS, width)),
        array((LABEL_ROWS, width)),
    ]
    return pl.pallas_call(
        pack_kernel,
        out_shape=shapes,
        in_specs=[vmem()] * 3,
        out_specs=[vmem()] * 4,
        compiler_params=kernel_params(),
    )(conserved, membership, slots)


def slot_of(labels, brick):
    row = labels[LABEL_ROWS - 1 : LABEL_ROWS, :]
    return jnp.max(jnp.where(lanes_of(row.shape) == brick, row, 0.0)).astype(jnp.int32)


def fluxes(c):
    rho, mx, my, mz, e = c
    inverse = 1.0 / rho
    u, v = mx * inverse, my * inverse
    pressure = GAMMA_LESS * (e - 0.5 * (mx * mx + my * my + mz * mz) * inverse)
    total = e + pressure
    flux_x = (mx, mx * u + pressure, my * u, mz * u, total * u)
    flux_y = (my, mx * v, my * v + pressure, mz * v, total * v)
    return flux_x, flux_y


def column_terms(own, depth, sign):
    fields = [pltpu.roll(own, LANES - depth * f, 1) if f else own for f in range(FIELDS)]
    flux_x, unused = fluxes(fields)
    return [DIFFUSE * fields[f] + sign * flux_x[f] for f in range(FIELDS)]


def row_terms(c):
    rows, width = c[0].shape
    lane = lanes_of((rows, width))
    flux_x, flux_y = fluxes(c)
    terms = []
    for f in range(FIELDS):
        base = DIFFUSE * c[f]
        gx, gy = COURANT * flux_x[f], COURANT * flux_y[f]
        from_left = jnp.where(lane == 0, 0.0, pltpu.roll(base + gx, 1, 1))
        from_right = jnp.where(lane == width - 1, 0.0, pltpu.roll(base - gx, width - 1, 1))
        terms.append(((1.0 - 4.0 * DIFFUSE) * c[f] + from_left + from_right, base + gy, base - gy))
    return terms


def beside(low, high, z):
    rows, width = low.shape
    lane = lanes_of((rows, width))
    at_left = pltpu.roll(low, LANES - z, 1) if z else low
    at_right = pltpu.roll(high, LANES - 1 - z, 1)
    return jnp.where(lane == 0, at_left, jnp.where(lane == width - 1, at_right, 0.0))


def fold_rows(across, down, up, j, origin, number, stride):
    t = {}
    for o in range(-3, 7):
        t[o] = (
            across[j, pl.ds(origin + o, number, stride=stride), :]
            + down[j, pl.ds(origin + o - 1, number, stride=stride), :]
            + up[j, pl.ds(origin + o + 1, number, stride=stride), :]
        )
    residual = [
        t[m] - (9.0 / 16.0) * (t[m - 1] + t[m + 1]) + (1.0 / 16.0) * (t[m - 3] + t[m + 3])
        for m in range(4)
    ]
    return butterfly(*residual)


def halves(value):
    high = value.astype(jnp.bfloat16)
    return high, (value - high.astype(jnp.float32)).astype(jnp.bfloat16)


def over_lanes(peak):
    peak = jnp.maximum(peak, pltpu.roll(peak, 64, 1))
    return jnp.maximum(peak, pltpu.roll(peak, 32, 1))


def leaving_order(count, odd):
    return [*range(1, count)] if odd else [*range(2, count), 1]


def exchange_of(i, count):
    if i == count - 1:
        return 0
    odd = lax.rem(lax.axis_index("sim"), 2)
    return jnp.where(odd == 1, leaving_order(count, True)[i], leaving_order(count, False)[i])


def partner_of(me, k, count):
    if count & (count - 1) == 0:
        return me ^ k
    return lax.rem(me + k, count)


def sender_of(me, k, count):
    if count & (count - 1) == 0:
        return me ^ k
    return lax.rem(me - k + count, count)


def flux_kernel(conserved, across, down, up):
    fields, depth, y, width = conserved.shape
    step = 16

    def flux_rows(i, carry):
        r = pl.ds(pl.multiple_of(i * step, step), step)
        padded = pl.ds(pl.multiple_of(i * step + PAD, PAD), step)
        for z in range(depth):
            for f, (a, d, u) in enumerate(row_terms([conserved[f, z, r, :] for f in range(fields)])):
                j = f * depth + z
                across[j, r, :] = a
                down[j, padded, :] = d
                up[j, padded, :] = u
        return carry

    lax.fori_loop(0, y // step, flux_rows, 0)


def own_fluxes(conserved):
    fields, depth, y, width = conserved.shape
    total = fields * depth
    tall = array((total, y + 2 * PAD, width))
    return pl.pallas_call(
        flux_kernel,
        out_shape=[array((total, y, width)), tall, tall],
        in_specs=[vmem()],
        out_specs=[vmem()] * 3,
        compiler_params=kernel_params(),
        cost_estimate=pl.CostEstimate(flops=40 * total * y * width, bytes_accessed=16 * total * y * width, transcendentals=0),
    )(conserved)


def edge_kernel(conserved, left, right, first_y, last_y, columns):
    fields, depth, y, width = conserved.shape
    total, quarter = fields * depth, y // 4
    for side, column in enumerate((left, right)):
        for c in range(4):
            value = column[0:quarter, :]
            value = pltpu.roll(value, LANES - 32 * c, 1) if c else value
            columns[side, c * quarter : (c + 1) * quarter, :] = value
        place = 4 * total + 4 * side
        first_y[place : place + 4, :] = columns[side, 0:4, :]
        last_y[place : place + 4, :] = columns[side, y - 4 : y, :]
    for j in range(total):
        first_y[4 * j : 4 * j + 4, :] = conserved[j // depth, j % depth, 0:4, :]
        last_y[4 * j : 4 * j + 4, :] = conserved[j // depth, j % depth, y - 4 : y, :]


def edge_rows(conserved, left, right):
    fields, depth, y, width = conserved.shape
    message = array((4 * fields * depth + COLUMN_ROWS, width))
    return pl.pallas_call(
        edge_kernel,
        out_shape=[message, message, array((2, y, width))],
        in_specs=[vmem()] * 3,
        out_specs=[vmem()] * 3,
        compiler_params=kernel_params(),
    )(conserved, left, right)


def brick_kernel(count, *refs):
    inside, down, up, columns, matrix = refs[:5]
    outs, refs = refs[5 : 5 + count], refs[5 + count :]
    blocks, rim_a, rim_d, rim_u, across, edges, split, coefficients, staged = refs
    total, y, width = inside.shape
    depth = total // FIELDS
    nb = y // 4
    rows = y // count

    for side in range(2):
        for f, value in enumerate(column_terms(columns[side], depth, COURANT if side == 0 else -COURANT)):
            edges[side, f] = value

    step = 24
    for start in range(0, y, step):
        for f in range(FIELDS):
            low, high = edges[0, f, start : start + step, :], edges[1, f, start : start + step, :]
            for z in range(depth):
                j = f * depth + z
                value = inside[j, start : start + step, :] + beside(low, high, z)
                across[j, PAD + start : PAD + start + step, :] = value
    for j in range(total):
        for source, rim in ((across, rim_a), (down, rim_d), (up, rim_u)):
            rim[j, 0:8, :] = source[j, PAD : PAD + 8, :]
            rim[j, 8:16, :] = source[j, y : y + 8, :]

    for f in range(FIELDS):
        rows_of = [fold_rows(across, down, up, f * depth + z, PAD, nb, 4) for z in range(4)]
        mixed = [butterfly(*[rows_of[z][m] for z in range(4)]) for m in range(4)]
        for k in range(4):
            high, low = halves(jnp.concatenate([mixed[m][k] for m in range(4)], axis=0))
            split[f, k * y : (k + 1) * y, 0:width] = high
            split[f, k * y : (k + 1) * y, width : 2 * width] = low
        product = jnp.dot(split[f], matrix[...], preferred_element_type=jnp.float32)
        result = product[:, 0:width] + product[:, width : 2 * width]
        peak = None
        for k in range(4):
            for m in range(4):
                value = result[k * y + m * nb : k * y + (m + 1) * nb]
                coefficients[f * depth + k, pl.ds(m, nb, stride=4), :] = value
                size = jnp.abs(value)
                peak = size if peak is None else jnp.maximum(peak, size)
        blocks[f] = over_lanes(peak)

    me = lax.axis_index("section")
    if rows % 8 == 0:
        for i in range(count):
            p = partner_of(me, exchange_of(i, count), count)
            for j in range(total):
                outs[i][j // depth, j % depth] = coefficients[j, pl.ds(pl.multiple_of(p * rows, 8), rows), :]
    else:
        for p in range(count):
            staged[p] = coefficients[:, p * rows : (p + 1) * rows, :]
        for i in range(count):
            p = partner_of(me, exchange_of(i, count), count)
            for j in range(total):
                outs[i][j // depth, j % depth] = staged[p, j]


def transform_bricks(count, inside, down, up, columns, matrix):
    total, y, width = inside.shape
    depth = total // FIELDS
    rows, tall = y // count, y + 2 * PAD
    chunk = array((FIELDS, depth, rows, width))
    rim = array((total, 2 * PAD, width))
    results = pl.pallas_call(
        functools.partial(brick_kernel, count),
        out_shape=[chunk] * count + [array((FIELDS, y // 4, width))] + [rim] * 3,
        in_specs=[vmem()] * 5,
        out_specs=[vmem()] * (count + 4),
        scratch_shapes=[
            pltpu.VMEM((total, tall, width), jnp.float32),
            pltpu.VMEM((2, FIELDS, y, width), jnp.float32),
            pltpu.VMEM((FIELDS, depth * y, 2 * width), jnp.bfloat16),
            pltpu.VMEM((total, y, width), jnp.float32),
            pltpu.VMEM((1, 1, 8, LANES) if rows % 8 == 0 else (count, total, rows, width), jnp.float32),
        ],
        compiler_params=kernel_params(),
        cost_estimate=pl.CostEstimate(flops=80 * total * y * width, bytes_accessed=16 * total * y * width, transcendentals=0),
    )(inside, down, up, columns, matrix)
    return results[:count], results[count], results[count + 1 :]


def mend_kernel(count, *refs):
    chunks, refs = refs[:count], refs[count:]
    top, bottom, blocks, rim_a, rim_d, rim_u, matrix = refs[:7]
    outs, mended, refs = refs[7 : 7 + count], refs[7 + count], refs[8 + count :]
    halo, columns, across, down, up, folded, split, result, fixed = refs
    fields, depth, rows, width = chunks[0].shape
    total = fields * depth
    nb = blocks.shape[1]

    halo[...] = jnp.ones(halo.shape, jnp.float32)
    columns[...] = jnp.ones(columns.shape, jnp.float32)
    for j in range(total):
        halo[j, 4:8, :] = top[4 * j : 4 * j + 4, :]
        halo[j, 8:12, :] = bottom[4 * j : 4 * j + 4, :]
    for side in range(2):
        place = 4 * total + 4 * side
        columns[side, 4:8, :] = top[place : place + 4, :]
        columns[side, 8:12, :] = bottom[place : place + 4, :]
    low = column_terms(columns[0], depth, COURANT)
    high = column_terms(columns[1], depth, -COURANT)
    for z in range(depth):
        c = [halo[f * depth + z] for f in range(fields)]
        for f, (a, d, u) in enumerate(row_terms(c)):
            j = f * depth + z
            values = (a + beside(low[f], high[f], z), d, u)
            for value, rim, target in zip(values, (rim_a, rim_d, rim_u), (across, down, up)):
                target[j, 0:8, :] = value[0:8]
                target[j, 8:24, :] = rim[j]
                target[j, 24:32, :] = value[8:16]
    for j in range(total):
        for k, value in enumerate(fold_rows(across, down, up, j, PAD, 2, 12)):
            folded[j, 2 * k : 2 * k + 2, :] = value
    for f in range(fields):
        values = butterfly(*[folded[f * depth + z] for z in range(4)])
        for half in range(2):
            both = jnp.concatenate(values[2 * half : 2 * half + 2], axis=0)
            upper, lower = halves(both)
            place = f * 32 + half * 16
            split[place : place + 16, 0:width] = upper
            split[place : place + 16, width : 2 * width] = lower
    product = jnp.dot(split[...], matrix[...], preferred_element_type=jnp.float32)
    result[...] = product[:, 0:width] + product[:, width : 2 * width]
    for j in range(total):
        for side in range(2):
            fixed[side, j] = result[pl.ds(8 * j + side, 4, stride=2), :]
    mended[...] = blocks[...]
    for f in range(fields):
        for side in range(2):
            size = jnp.abs(fixed[side, f * depth])
            for z in range(1, depth):
                size = jnp.maximum(size, jnp.abs(fixed[side, f * depth + z]))
            peak = over_lanes(jnp.max(size, axis=0, keepdims=True))
            row = side * (nb - 1)
            mended[f, row : row + 1, :] = peak

    me = lax.axis_index("section")
    for i in range(count):
        p = partner_of(me, exchange_of(i, count), count)
        for side, start in ((0, 0), (1, rows - 4)):

            @pl.when(p == side * (count - 1))
            def replace(i=i, side=side, start=start):
                for j in range(total):
                    outs[i][j // depth, j % depth, start : start + 4, :] = fixed[side, j]


def mend(count, chunks, top, bottom, blocks, rims, matrix):
    fields, depth, rows, width = chunks[0].shape
    total = fields * depth
    tall = pltpu.VMEM((total, 4 * PAD, width), jnp.float32)
    results = pl.pallas_call(
        functools.partial(mend_kernel, count),
        out_shape=[array(chunks[0].shape)] * count + [array(blocks.shape)],
        in_specs=[vmem()] * (count + 7),
        out_specs=[vmem()] * (count + 1),
        input_output_aliases={k: k for k in range(count)},
        scratch_shapes=[
            pltpu.VMEM((total, 2 * PAD, width), jnp.float32),
            pltpu.VMEM((2, 2 * PAD, width), jnp.float32),
            tall,
            tall,
            tall,
            pltpu.VMEM((total, 8, width), jnp.float32),
            pltpu.VMEM((8 * total, 2 * width), jnp.bfloat16),
            pltpu.VMEM((8 * total, width), jnp.float32),
            pltpu.VMEM((2, total, 4, width), jnp.float32),
        ],
        compiler_params=kernel_params(),
    )(*chunks, top, bottom, blocks, *rims, matrix)
    return results[:count], results[count]


def group_kernel(count, groups, own_rows, *refs):
    blocks, refs = refs[0], refs[1:]
    messages, (peaks, gathered, listed, packed, table) = refs[:count], refs[count:]
    nb = blocks.shape[1]
    me = lax.axis_index("section")
    slot = slot_of(messages[0], me)
    within = lax.rem(slot, 4) * 32
    tile = lax.div(slot, 4)
    for d, message in enumerate(messages):
        height = gathered.shape[1]
        value = message[message.shape[0] - height :, :]
        if count > 4:
            value = pltpu.roll(value, lax.rem(height - tile * own_rows, height), 0)
        gathered[lax.rem(me + count - d, count)] = value
    for q in range(count):
        listed[q * own_rows : (q + 1) * own_rows, :] = gathered[q, 0:own_rows, :]
    part = nb // 4
    band = lax.div(lanes_of((part, LANES)), 32)
    labels = jnp.zeros((part, LANES), jnp.float32)
    for c in range(4):
        turned = pltpu.roll(listed[c * part : (c + 1) * part, :], lax.rem(32 * c - within + LANES, LANES), 1)
        labels = jnp.where(band == c, turned, labels)
    for f in range(FIELDS):
        own = jnp.zeros((part, LANES), jnp.float32)
        for c in range(4):
            own = jnp.where(band == c, blocks[f, c * part : (c + 1) * part, :], own)
        packed[f, 0:part, :] = own
    lane8 = lanes_of((8, LANES))
    sub8 = lax.broadcasted_iota(jnp.int32, (8, LANES), 0)
    label_rows = [jnp.broadcast_to(labels[r : r + 1], (8, LANES)) for r in range(part)]

    def group_tile(g, carry):
        wanted = (sub8 + g * 8).astype(jnp.float32)
        matches = [label_rows[r] == wanted for r in range(part)]
        found = jnp.zeros((8, LANES), jnp.float32)
        for f in range(FIELDS):
            best = jnp.zeros((8, LANES), jnp.float32)
            for r in range(part):
                row = jnp.broadcast_to(packed[f, r : r + 1, :], (8, LANES))
                best = jnp.maximum(best, jnp.where(matches[r], row, 0.0))
            found = jnp.where(lane8 == f, jnp.max(best, axis=1, keepdims=True), found)
        table[pl.ds(pl.multiple_of(g * 8, 8), 8), :] = found
        return carry

    high = table.shape[0]
    if groups < high:
        table[...] = jnp.zeros((high, LANES), jnp.float32)
    lax.fori_loop(0, pl.cdiv(groups, 8), group_tile, 0)
    for g in range(high // LANES):
        peaks[:, g * LANES : (g + 1) * LANES] = jnp.transpose(table[g * LANES : (g + 1) * LANES, :])[0:8]


def group_maxima(count, groups, own_rows, blocks, messages):
    high = pl.cdiv(groups, LANES) * LANES
    nb = blocks.shape[1]
    return pl.pallas_call(
        functools.partial(group_kernel, count, groups, own_rows),
        out_shape=array((8, high)),
        in_specs=[vmem()] * (count + 1),
        out_specs=vmem(),
        scratch_shapes=[
            pltpu.VMEM((count, messages[0].shape[0], LANES), jnp.float32),
            pltpu.VMEM((nb, LANES), jnp.float32),
            pltpu.VMEM((FIELDS, 8, LANES), jnp.float32),
            pltpu.VMEM((high, LANES), jnp.float32),
        ],
        compiler_params=kernel_params(),
    )(blocks, *messages)


def scale_kernel(count, groups, *refs):
    chunks, refs = refs[:count], refs[count:]
    peaks, labels, coded, group_peak, wide = refs
    fields, depth, rows, width = chunks[0].shape
    nb = rows // 4
    high = peaks.shape[1]
    me = lax.axis_index("section")
    group_peak[...] = peaks[0:fields, 0:groups]
    own_labels = labels[...].astype(jnp.int32)
    lane = lanes_of((8, LANES))
    inverse = 1.0 / (peaks[...] + EPSILON)
    tables = [
        [jnp.broadcast_to(inverse[f : f + 1, g * LANES : (g + 1) * LANES], (8, LANES)) for g in range(high // LANES)]
        for f in range(fields)
    ]
    for i in range(count):
        slot = slot_of(labels, sender_of(me, exchange_of(i, count), count))
        tile = own_labels
        if count > 4:
            tile = pltpu.roll(tile, lax.rem(LABEL_ROWS - lax.div(slot, 4) * nb, LABEL_ROWS), 0)
        within = lax.rem(slot, 4) * 32 + lax.rem(lane, 32)
        own = jnp.take_along_axis(tile, within, axis=1)
        place = pl.ds(pl.multiple_of(slot * width, width), width)
        for f in range(fields):
            if high == LANES:
                found = jnp.take_along_axis(tables[f][0], own, axis=1)
            else:
                found = jnp.zeros((8, LANES), jnp.float32)
                inside = lax.rem(own, LANES)
                for g in range(high // LANES):
                    here = jnp.take_along_axis(tables[f][g], inside, axis=1)
                    found = jnp.where(lax.div(own, LANES) == g, here, found)
            for m in range(4):
                wide[i, f, pl.ds(m, nb, stride=4), :] = found[0:nb]
            factor = wide[i, f]
            for z in range(depth):
                coded[f, z, :, place] = chunks[i][f, z] * factor


def scale(count, groups, chunks, peaks, labels):
    fields, depth, rows, width = chunks[0].shape
    return pl.pallas_call(
        functools.partial(scale_kernel, count, groups),
        out_shape=[array((fields, depth, rows, width * count)), array((fields, groups))],
        in_specs=[vmem()] * (count + 2),
        out_specs=[vmem()] * 2,
        scratch_shapes=[
            pltpu.VMEM((count, fields, rows, width), jnp.float32),
        ],
        compiler_params=kernel_params(),
    )(*chunks, peaks, labels)


def ring(axis, shift):
    count = lax.axis_size(axis)
    return [(i, (i + shift) % count) for i in range(count)]


def exchange_pairs(count, k):
    if count & (count - 1) == 0:
        return [(i, i ^ k) for i in range(count)]
    return [(i, (i + k) % count) for i in range(count)]


def leaving_pairs(count, i):
    pairs = []
    for sim in range(lax.axis_size("sim")):
        k = leaving_order(count, sim % 2 == 1)[i]
        pairs += [(sim * count + a, sim * count + b) for a, b in exchange_pairs(count, k)]
    return pairs


def steps_over(axis):
    count = lax.axis_size(axis)
    span, shifts = 1, []
    while span < count:
        shifts.append(min(span, count - span))
        span += shifts[-1]
    return shifts


def with_others(value, axis, shifts):
    count = lax.axis_size(axis)
    others = [lax.ppermute(value, axis, exchange_pairs(count, k)) for k in shifts]
    return functools.reduce(jnp.maximum, others, value)


def per_device(density, momentum, energy, membership, slot_of_brick):
    count = lax.axis_size("section")
    groups = 2 * lax.axis_size("sim") * count
    conserved = jnp.concatenate([density[None], momentum, energy[None]], axis=0)
    matrix, first_x, last_x, labels = pack(conserved, membership, slot_of_brick)
    left = lax.ppermute(last_x, "section", ring("section", 1))
    right = lax.ppermute(first_x, "section", ring("section", -1))
    far = [lax.ppermute(labels, "section", ring("section", d)) for d in range(2, count - 1)]
    inside, down, up = own_fluxes(conserved)
    left, right, inside = lax.optimization_barrier((left, right, inside))
    first_y, last_y, columns = edge_rows(conserved, left, right)
    first_y, last_y, *far = lax.optimization_barrier((first_y, last_y, *far))
    top = lax.ppermute(last_y, "sim", ring("sim", 1))
    bottom = lax.ppermute(first_y, "sim", ring("sim", -1))
    chunks, blocks, rims = transform_bricks(count, inside, down, up, columns, matrix)
    chunks, blocks = mend(count, chunks, top, bottom, blocks, rims, matrix)
    moved = [
        lax.ppermute(chunks[i], ("sim", "section"), leaving_pairs(count, i)) for i in range(count - 1)
    ]
    peaks = group_maxima(count, groups, membership.shape[0], blocks, [labels, left, *far, right])
    for shift in steps_over("sim"):
        peaks = with_others(peaks, "sim", [shift])
    peaks, moved[0] = lax.optimization_barrier((peaks, moved[0]))
    if count <= 4:
        peaks = with_others(peaks, "section", range(1, count))
    else:
        for shift in steps_over("section"):
            peaks = with_others(peaks, "section", [shift])
    return tuple(scale(count, groups, [*moved, chunks[count - 1]], peaks, labels))


def solution(mesh):
    placed = (
        P(None, "sim", "section"),
        P(None, None, "sim", "section"),
        P(None, "sim", "section"),
        P(("sim", "section"), None),
        P("sim", None),
    )
    return jax.shard_map(
        per_device,
        mesh=mesh,
        in_specs=placed,
        out_specs=(P(None, None, ("sim", "section"), None), P()),
        check_vma=False,
    )
```

```python
import functools

import jax
import jax.numpy as jnp
import numpy as np
from jax import lax
from jax.experimental import pallas as pl
from jax.experimental.pallas import tpu as pltpu
from jax.sharding import PartitionSpec as P

GAMMA_LESS = 0.4
COURANT = 0.05
DIFFUSE = 0.1
EPSILON = 1e-06
FIELDS = 5
PAD = 8
COLUMN_ROWS = 8
LABEL_ROWS = 8
LANES = 128
EVEN = 0.5
WIDE = float(np.sqrt(0.5) * np.cos(np.pi / 8))
NARROW = float(np.sqrt(0.5) * np.cos(3 * np.pi / 8))
VMEM_LIMIT = 48 * 1024 * 1024


def vmem():
    return pl.BlockSpec(memory_space=pltpu.VMEM)


def lanes_of(shape):
    return lax.broadcasted_iota(jnp.int32, shape, 1)


def butterfly(a, b, c, d):
    s, t, u, v = a + d, b + c, a - d, b - c
    return (
        EVEN * (s + t),
        WIDE * u + NARROW * v,
        EVEN * (s - t),
        NARROW * u - WIDE * v,
    )


def cosine(k, d):
    factor = 0.5 if k == 0 else np.sqrt(0.5)
    return float(factor * np.cos(np.pi * (2 * d + 1) * k / 8))


def write_matrix(matrix, width):
    step = 16
    row = lax.broadcasted_iota(jnp.int32, (step, width), 0)
    column = lanes_of((step, width))
    quarter = width // 4
    k, j, d = lax.div(column, quarter), lax.rem(column, quarter), lax.rem(row, 4)
    entry = jnp.zeros((step, width), jnp.float32)
    for a in range(4):
        for b in range(4):
            entry = jnp.where(jnp.logical_and(k == a, d == b), cosine(a, b), entry)
    high = entry.astype(jnp.bfloat16).astype(jnp.float32)
    low = entry - high
    zero = jnp.zeros((step, width), jnp.bfloat16)
    for start in range(0, width, step):
        own = j == lax.div(row + start, 4)
        upper = jnp.where(own, high, 0.0).astype(jnp.bfloat16)
        lower = jnp.where(own, low, 0.0).astype(jnp.bfloat16)
        matrix[start : start + step, 0:width] = upper
        matrix[start : start + step, width : 2 * width] = lower
        matrix[width + start : width + start + step, 0:width] = upper
        matrix[width + start : width + start + step, width : 2 * width] = zero


def kernel_params():
    return pltpu.CompilerParams(vmem_limit_bytes=VMEM_LIMIT)


def array(shape, dtype=jnp.float32):
    return jax.ShapeDtypeStruct(shape, dtype)


def pack_kernel(conserved, membership, slots, matrix, first_x, last_x, labels):
    fields, depth, y, width = conserved.shape
    quarter = y // 4
    lane = lanes_of((y, width))
    first = jnp.zeros((y, width), jnp.float32)
    last = jnp.zeros((y, width), jnp.float32)
    for j in range(fields * depth):
        value = conserved[j // depth, j % depth]
        first = jnp.where(lane == j, pltpu.roll(value, j, 1) if j else value, first)
        last = jnp.where(lane == j, pltpu.roll(value, j + 1, 1), last)
    rows, columns = membership.shape
    labels[...] = jnp.zeros(labels.shape, jnp.float32)
    for t in range(columns // LANES):
        part = membership[:, t * LANES : (t + 1) * LANES].astype(jnp.float32)
        labels[t * rows : (t + 1) * rows, :] = part
    labels[LABEL_ROWS - 1 : LABEL_ROWS, 0 : slots.shape[1]] = slots[...].astype(jnp.float32)
    own = labels[...]
    for column, out in ((first, first_x), (last, last_x)):
        packed = column[0:quarter]
        for c in range(1, 4):
            packed = packed + pltpu.roll(column[c * quarter : (c + 1) * quarter], 32 * c, 1)
        out[0:quarter, :] = packed
        out[quarter:, :] = own
    write_matrix(matrix, width)


def pack(conserved, membership, slots):
    y, width = conserved.shape[2:]
    shapes = [
        array((2 * width, 2 * width), jnp.bfloat16),
        array((y // 4 + LABEL_ROWS, width)),
        array((y // 4 + LABEL_ROWS, width)),
        array((LABEL_ROWS, width)),
    ]
    return pl.pallas_call(
        pack_kernel,
        out_shape=shapes,
        in_specs=[vmem()] * 3,
        out_specs=[vmem()] * 4,
        compiler_params=kernel_params(),
    )(conserved, membership, slots)


def slot_of(labels, brick):
    row = labels[LABEL_ROWS - 1 : LABEL_ROWS, :]
    return jnp.max(jnp.where(lanes_of(row.shape) == brick, row, 0.0)).astype(jnp.int32)


def fluxes(c):
    rho, mx, my, mz, e = c
    inverse = 1.0 / rho
    u, v = mx * inverse, my * inverse
    pressure = GAMMA_LESS * (e - 0.5 * (mx * mx + my * my + mz * mz) * inverse)
    total = e + pressure
    flux_x = (mx, mx * u + pressure, my * u, mz * u, total * u)
    flux_y = (my, mx * v, my * v + pressure, mz * v, total * v)
    return flux_x, flux_y


def column_terms(own, depth, sign):
    fields = [pltpu.roll(own, LANES - depth * f, 1) if f else own for f in range(FIELDS)]
    flux_x, unused = fluxes(fields)
    return [DIFFUSE * fields[f] + sign * flux_x[f] for f in range(FIELDS)]


def row_terms(c):
    rows, width = c[0].shape
    lane = lanes_of((rows, width))
    flux_x, flux_y = fluxes(c)
    terms = []
    for f in range(FIELDS):
        base = DIFFUSE * c[f]
        gx, gy = COURANT * flux_x[f], COURANT * flux_y[f]
        from_left = jnp.where(lane == 0, 0.0, pltpu.roll(base + gx, 1, 1))
        from_right = jnp.where(lane == width - 1, 0.0, pltpu.roll(base - gx, width - 1, 1))
        terms.append(((1.0 - 4.0 * DIFFUSE) * c[f] + from_left + from_right, base + gy, base - gy))
    return terms


def beside(low, high, z):
    rows, width = low.shape
    lane = lanes_of((rows, width))
    at_left = pltpu.roll(low, LANES - z, 1) if z else low
    at_right = pltpu.roll(high, LANES - 1 - z, 1)
    return jnp.where(lane == 0, at_left, jnp.where(lane == width - 1, at_right, 0.0))


def fold_rows(across, down, up, j, origin, number, stride):
    t = {}
    for o in range(-3, 7):
        t[o] = (
            across[j, pl.ds(origin + o, number, stride=stride), :]
            + down[j, pl.ds(origin + o - 1, number, stride=stride), :]
            + up[j, pl.ds(origin + o + 1, number, stride=stride), :]
        )
    residual = [
        t[m] - (9.0 / 16.0) * (t[m - 1] + t[m + 1]) + (1.0 / 16.0) * (t[m - 3] + t[m + 3])
        for m in range(4)
    ]
    return butterfly(*residual)


def halves(value):
    high = value.astype(jnp.bfloat16)
    return high, (value - high.astype(jnp.float32)).astype(jnp.bfloat16)


def over_lanes(peak):
    peak = jnp.maximum(peak, pltpu.roll(peak, 64, 1))
    return jnp.maximum(peak, pltpu.roll(peak, 32, 1))


def rounds_of(count):
    if count == 4:
        return [(None, 2), (2, 1), (3, 3), (1, None)]
    return [(k, k) for k in range(1, count)]


def arrivals_of(count):
    if count == 4:
        return [((0, 2), (3, 1)), ((1, 1), (1, 2)), ((2, 3), (2, 3))]
    return [((k - 1, k), (k - 1, k)) for k in range(1, count)]


def early_rounds(count):
    return 1 if count == 4 else 0


def is_inner(me, count):
    return jnp.logical_and(me > 0, me < count - 1)


def either(inner, outer, me, count):
    return inner if inner == outer else jnp.where(is_inner(me, count), inner, outer)


def leaving_for(me, i, count):
    if i == len(rounds_of(count)):
        return me
    inner, outer = rounds_of(count)[i]
    k = either(outer if inner is None else inner, inner if outer is None else outer, me, count)
    return partner_of(me, k, count)


def partner_of(me, k, count):
    if count & (count - 1) == 0:
        return me ^ k
    return lax.rem(me + k, count)


def sender_of(me, k, count):
    if count & (count - 1) == 0:
        return me ^ k
    return lax.rem(me - k + count, count)


def flux_kernel(conserved, across, down, up):
    fields, depth, y, width = conserved.shape
    step = 16

    def flux_rows(i, carry):
        r = pl.ds(pl.multiple_of(i * step, step), step)
        padded = pl.ds(pl.multiple_of(i * step + PAD, PAD), step)
        for z in range(depth):
            for f, (a, d, u) in enumerate(row_terms([conserved[f, z, r, :] for f in range(fields)])):
                j = f * depth + z
                across[j, r, :] = a
                down[j, padded, :] = d
                up[j, padded, :] = u
        return carry

    lax.fori_loop(0, y // step, flux_rows, 0)


def own_fluxes(conserved):
    fields, depth, y, width = conserved.shape
    total = fields * depth
    tall = array((total, y + 2 * PAD, width))
    return pl.pallas_call(
        flux_kernel,
        out_shape=[array((total, y, width)), tall, tall],
        in_specs=[vmem()],
        out_specs=[vmem()] * 3,
        compiler_params=kernel_params(),
        cost_estimate=pl.CostEstimate(flops=40 * total * y * width, bytes_accessed=16 * total * y * width, transcendentals=0),
    )(conserved)


def edge_kernel(conserved, left, right, first_y, last_y, columns):
    fields, depth, y, width = conserved.shape
    total, quarter = fields * depth, y // 4
    for side, column in enumerate((left, right)):
        for c in range(4):
            value = column[0:quarter, :]
            value = pltpu.roll(value, LANES - 32 * c, 1) if c else value
            columns[side, c * quarter : (c + 1) * quarter, :] = value
        place = 4 * total + 4 * side
        first_y[place : place + 4, :] = columns[side, 0:4, :]
        last_y[place : place + 4, :] = columns[side, y - 4 : y, :]
    for j in range(total):
        first_y[4 * j : 4 * j + 4, :] = conserved[j // depth, j % depth, 0:4, :]
        last_y[4 * j : 4 * j + 4, :] = conserved[j // depth, j % depth, y - 4 : y, :]


def edge_rows(conserved, left, right):
    fields, depth, y, width = conserved.shape
    message = array((4 * fields * depth + COLUMN_ROWS, width))
    return pl.pallas_call(
        edge_kernel,
        out_shape=[message, message, array((2, y, width))],
        in_specs=[vmem()] * 3,
        out_specs=[vmem()] * 3,
        compiler_params=kernel_params(),
    )(conserved, left, right)


def brick_kernel(count, *refs):
    inside, down, up, columns, matrix = refs[:5]
    number = len(rounds_of(count)) + 1
    outs, refs = refs[5 : 5 + number], refs[5 + number :]
    blocks, rim_a, rim_d, rim_u, across, edges, split, coefficients, staged = refs
    total, y, width = inside.shape
    depth = total // FIELDS
    nb = y // 4
    rows = y // count

    for side in range(2):
        for f, value in enumerate(column_terms(columns[side], depth, COURANT if side == 0 else -COURANT)):
            edges[side, f] = value

    step = 24
    for start in range(0, y, step):
        for f in range(FIELDS):
            low, high = edges[0, f, start : start + step, :], edges[1, f, start : start + step, :]
            for z in range(depth):
                j = f * depth + z
                value = inside[j, start : start + step, :] + beside(low, high, z)
                across[j, PAD + start : PAD + start + step, :] = value
    for j in range(total):
        for source, rim in ((across, rim_a), (down, rim_d), (up, rim_u)):
            rim[j, 0:8, :] = source[j, PAD : PAD + 8, :]
            rim[j, 8:16, :] = source[j, y : y + 8, :]

    for f in range(FIELDS):
        rows_of = [fold_rows(across, down, up, f * depth + z, PAD, nb, 4) for z in range(4)]
        mixed = [butterfly(*[rows_of[z][m] for z in range(4)]) for m in range(4)]
        for k in range(4):
            high, low = halves(jnp.concatenate([mixed[m][k] for m in range(4)], axis=0))
            split[f, k * y : (k + 1) * y, 0:width] = high
            split[f, k * y : (k + 1) * y, width : 2 * width] = low
        product = jnp.dot(split[f], matrix[...], preferred_element_type=jnp.float32)
        result = product[:, 0:width] + product[:, width : 2 * width]
        peak = None
        for k in range(4):
            for m in range(4):
                value = result[k * y + m * nb : k * y + (m + 1) * nb]
                coefficients[f * depth + k, pl.ds(m, nb, stride=4), :] = value
                size = jnp.abs(value)
                peak = size if peak is None else jnp.maximum(peak, size)
        blocks[f] = over_lanes(peak)

    me = lax.axis_index("section")
    if rows % 8 == 0:
        for i in range(number):
            p = leaving_for(me, i, count)
            for j in range(total):
                outs[i][j // depth, j % depth] = coefficients[j, pl.ds(pl.multiple_of(p * rows, 8), rows), :]
    else:
        for p in range(count):
            staged[p] = coefficients[:, p * rows : (p + 1) * rows, :]
        for i in range(number):
            p = leaving_for(me, i, count)
            for j in range(total):
                outs[i][j // depth, j % depth] = staged[p, j]


def transform_bricks(count, inside, down, up, columns, matrix):
    total, y, width = inside.shape
    depth = total // FIELDS
    rows, tall = y // count, y + 2 * PAD
    chunk = array((FIELDS, depth, rows, width))
    number = len(rounds_of(count)) + 1
    rim = array((total, 2 * PAD, width))
    results = pl.pallas_call(
        functools.partial(brick_kernel, count),
        out_shape=[chunk] * number + [array((FIELDS, y // 4, width))] + [rim] * 3,
        in_specs=[vmem()] * 5,
        out_specs=[vmem()] * (number + 4),
        scratch_shapes=[
            pltpu.VMEM((total, tall, width), jnp.float32),
            pltpu.VMEM((2, FIELDS, y, width), jnp.float32),
            pltpu.VMEM((FIELDS, depth * y, 2 * width), jnp.bfloat16),
            pltpu.VMEM((total, y, width), jnp.float32),
            pltpu.VMEM((1, 1, 8, LANES) if rows % 8 == 0 else (count, total, rows, width), jnp.float32),
        ],
        compiler_params=kernel_params(),
        cost_estimate=pl.CostEstimate(flops=80 * total * y * width, bytes_accessed=16 * total * y * width, transcendentals=0),
    )(inside, down, up, columns, matrix)
    return results[:number], results[number], results[number + 1 :]


def mend_kernel(count, *refs):
    early = early_rounds(count)
    number = len(rounds_of(count)) + 1 - early
    chunks, refs = refs[:number], refs[number:]
    top, bottom, blocks, rim_a, rim_d, rim_u, matrix = refs[:7]
    outs, mended, refs = refs[7 : 7 + number], refs[7 + number], refs[8 + number :]
    halo, columns, across, down, up, folded, split, result, fixed = refs
    fields, depth, rows, width = chunks[0].shape
    total = fields * depth
    nb = blocks.shape[1]

    halo[...] = jnp.ones(halo.shape, jnp.float32)
    columns[...] = jnp.ones(columns.shape, jnp.float32)
    for j in range(total):
        halo[j, 4:8, :] = top[4 * j : 4 * j + 4, :]
        halo[j, 8:12, :] = bottom[4 * j : 4 * j + 4, :]
    for side in range(2):
        place = 4 * total + 4 * side
        columns[side, 4:8, :] = top[place : place + 4, :]
        columns[side, 8:12, :] = bottom[place : place + 4, :]
    low = column_terms(columns[0], depth, COURANT)
    high = column_terms(columns[1], depth, -COURANT)
    for z in range(depth):
        c = [halo[f * depth + z] for f in range(fields)]
        for f, (a, d, u) in enumerate(row_terms(c)):
            j = f * depth + z
            values = (a + beside(low[f], high[f], z), d, u)
            for value, rim, target in zip(values, (rim_a, rim_d, rim_u), (across, down, up)):
                target[j, 0:8, :] = value[0:8]
                target[j, 8:24, :] = rim[j]
                target[j, 24:32, :] = value[8:16]
    for j in range(total):
        for k, value in enumerate(fold_rows(across, down, up, j, PAD, 2, 12)):
            folded[j, 2 * k : 2 * k + 2, :] = value
    for f in range(fields):
        values = butterfly(*[folded[f * depth + z] for z in range(4)])
        for half in range(2):
            both = jnp.concatenate(values[2 * half : 2 * half + 2], axis=0)
            upper, lower = halves(both)
            place = f * 32 + half * 16
            split[place : place + 16, 0:width] = upper
            split[place : place + 16, width : 2 * width] = lower
    product = jnp.dot(split[...], matrix[...], preferred_element_type=jnp.float32)
    result[...] = product[:, 0:width] + product[:, width : 2 * width]
    for j in range(total):
        for side in range(2):
            fixed[side, j] = result[pl.ds(8 * j + side, 4, stride=2), :]
    mended[...] = blocks[...]
    for f in range(fields):
        for side in range(2):
            size = jnp.abs(fixed[side, f * depth])
            for z in range(1, depth):
                size = jnp.maximum(size, jnp.abs(fixed[side, f * depth + z]))
            peak = over_lanes(jnp.max(size, axis=0, keepdims=True))
            row = side * (nb - 1)
            mended[f, row : row + 1, :] = peak

    me = lax.axis_index("section")
    for i in range(number):
        p = leaving_for(me, i + early, count)
        for side, start in ((0, 0), (1, rows - 4)):

            @pl.when(p == side * (count - 1))
            def replace(i=i, side=side, start=start):
                for j in range(total):
                    outs[i][j // depth, j % depth, start : start + 4, :] = fixed[side, j]


def mend(count, chunks, top, bottom, blocks, rims, matrix):
    number = len(chunks)
    fields, depth, rows, width = chunks[0].shape
    total = fields * depth
    tall = pltpu.VMEM((total, 4 * PAD, width), jnp.float32)
    results = pl.pallas_call(
        functools.partial(mend_kernel, count),
        out_shape=[array(chunks[0].shape)] * number + [array(blocks.shape)],
        in_specs=[vmem()] * (number + 7),
        out_specs=[vmem()] * (number + 1),
        input_output_aliases={i: i for i in range(number)},
        scratch_shapes=[
            pltpu.VMEM((total, 2 * PAD, width), jnp.float32),
            pltpu.VMEM((2, 2 * PAD, width), jnp.float32),
            tall,
            tall,
            tall,
            pltpu.VMEM((total, 8, width), jnp.float32),
            pltpu.VMEM((8 * total, 2 * width), jnp.bfloat16),
            pltpu.VMEM((8 * total, width), jnp.float32),
            pltpu.VMEM((2, total, 4, width), jnp.float32),
        ],
        compiler_params=kernel_params(),
    )(*chunks, top, bottom, blocks, *rims, matrix)
    return results[:number], results[number]


def group_kernel(count, groups, own_rows, *refs):
    blocks, refs = refs[0], refs[1:]
    messages, (peaks, gathered, listed, packed, table) = refs[:count], refs[count:]
    nb = blocks.shape[1]
    me = lax.axis_index("section")
    slot = slot_of(messages[0], me)
    within = lax.rem(slot, 4) * 32
    tile = lax.div(slot, 4)
    for d, message in enumerate(messages):
        height = gathered.shape[1]
        value = message[message.shape[0] - height :, :]
        if count > 4:
            value = pltpu.roll(value, lax.rem(height - tile * own_rows, height), 0)
        gathered[lax.rem(me + count - d, count)] = value
    for q in range(count):
        listed[q * own_rows : (q + 1) * own_rows, :] = gathered[q, 0:own_rows, :]
    part = nb // 4
    band = lax.div(lanes_of((part, LANES)), 32)
    labels = jnp.zeros((part, LANES), jnp.float32)
    for c in range(4):
        turned = pltpu.roll(listed[c * part : (c + 1) * part, :], lax.rem(32 * c - within + LANES, LANES), 1)
        labels = jnp.where(band == c, turned, labels)
    for f in range(FIELDS):
        own = jnp.zeros((part, LANES), jnp.float32)
        for c in range(4):
            own = jnp.where(band == c, blocks[f, c * part : (c + 1) * part, :], own)
        packed[f, 0:part, :] = own
    lane8 = lanes_of((8, LANES))
    sub8 = lax.broadcasted_iota(jnp.int32, (8, LANES), 0)
    label_rows = [jnp.broadcast_to(labels[r : r + 1], (8, LANES)) for r in range(part)]

    def group_tile(g, carry):
        wanted = (sub8 + g * 8).astype(jnp.float32)
        matches = [label_rows[r] == wanted for r in range(part)]
        found = jnp.zeros((8, LANES), jnp.float32)
        for f in range(FIELDS):
            best = jnp.zeros((8, LANES), jnp.float32)
            for r in range(part):
                row = jnp.broadcast_to(packed[f, r : r + 1, :], (8, LANES))
                best = jnp.maximum(best, jnp.where(matches[r], row, 0.0))
            found = jnp.where(lane8 == f, jnp.max(best, axis=1, keepdims=True), found)
        table[pl.ds(pl.multiple_of(g * 8, 8), 8), :] = found
        return carry

    high = table.shape[0]
    if groups < high:
        table[...] = jnp.zeros((high, LANES), jnp.float32)
    lax.fori_loop(0, pl.cdiv(groups, 8), group_tile, 0)
    for g in range(high // LANES):
        peaks[:, g * LANES : (g + 1) * LANES] = jnp.transpose(table[g * LANES : (g + 1) * LANES, :])[0:8]


def group_maxima(count, groups, own_rows, blocks, messages):
    high = pl.cdiv(groups, LANES) * LANES
    nb = blocks.shape[1]
    return pl.pallas_call(
        functools.partial(group_kernel, count, groups, own_rows),
        out_shape=array((8, high)),
        in_specs=[vmem()] * (count + 1),
        out_specs=vmem(),
        scratch_shapes=[
            pltpu.VMEM((count, messages[0].shape[0], LANES), jnp.float32),
            pltpu.VMEM((nb, LANES), jnp.float32),
            pltpu.VMEM((FIELDS, 8, LANES), jnp.float32),
            pltpu.VMEM((high, LANES), jnp.float32),
        ],
        compiler_params=kernel_params(),
    )(blocks, *messages)


def scale_kernel(count, groups, *refs):
    number = len(rounds_of(count)) + 1
    chunks, refs = refs[:number], refs[number:]
    peaks, labels, coded, group_peak, wide = refs
    fields, depth, rows, width = chunks[0].shape
    nb = rows // 4
    high = peaks.shape[1]
    me = lax.axis_index("section")
    group_peak[...] = peaks[0:fields, 0:groups]
    own_labels = labels[...].astype(jnp.int32)
    lane = lanes_of((8, LANES))
    inverse = 1.0 / (peaks[...] + EPSILON)
    tables = [
        [jnp.broadcast_to(inverse[f : f + 1, g * LANES : (g + 1) * LANES], (8, LANES)) for g in range(high // LANES)]
        for f in range(fields)
    ]
    own_chunk = (number - 1, 0)
    for i, (inner, outer) in enumerate([*arrivals_of(count), (own_chunk, own_chunk)]):
        slot = slot_of(labels, sender_of(me, either(inner[1], outer[1], me, count), count))
        tile = own_labels
        if count > 4:
            tile = pltpu.roll(tile, lax.rem(LABEL_ROWS - lax.div(slot, 4) * nb, LABEL_ROWS), 0)
        within = lax.rem(slot, 4) * 32 + lax.rem(lane, 32)
        own = jnp.take_along_axis(tile, within, axis=1)
        place = pl.ds(pl.multiple_of(slot * width, width), width)
        for f in range(fields):
            if high == LANES:
                found = jnp.take_along_axis(tables[f][0], own, axis=1)
            else:
                found = jnp.zeros((8, LANES), jnp.float32)
                inside = lax.rem(own, LANES)
                for g in range(high // LANES):
                    here = jnp.take_along_axis(tables[f][g], inside, axis=1)
                    found = jnp.where(lax.div(own, LANES) == g, here, found)
            for m in range(4):
                wide[i, f, pl.ds(m, nb, stride=4), :] = found[0:nb]
            factor = wide[i, f]
            for z in range(depth):
                value = chunks[inner[0]][f, z]
                if inner[0] != outer[0]:
                    value = jnp.where(is_inner(me, count), value, chunks[outer[0]][f, z])
                coded[f, z, :, place] = value * factor


def scale(count, groups, chunks, peaks, labels):
    fields, depth, rows, width = chunks[0].shape
    return pl.pallas_call(
        functools.partial(scale_kernel, count, groups),
        out_shape=[array((fields, depth, rows, width * count)), array((fields, groups))],
        in_specs=[vmem()] * (len(chunks) + 2),
        out_specs=[vmem()] * 2,
        scratch_shapes=[
            pltpu.VMEM((count, fields, rows, width), jnp.float32),
        ],
        compiler_params=kernel_params(),
    )(*chunks, peaks, labels)


def ring(axis, shift):
    count = lax.axis_size(axis)
    return [(i, (i + shift) % count) for i in range(count)]


def exchange_pairs(count, k):
    if count & (count - 1) == 0:
        return [(i, i ^ k) for i in range(count)]
    return [(i, (i + k) % count) for i in range(count)]


def round_pairs(count, i):
    inner, outer = rounds_of(count)[i]
    pairs = []
    for a in range(count):
        k = inner if 0 < a < count - 1 else outer
        if k is not None:
            pairs.append(exchange_pairs(count, k)[a])
    return pairs


def steps_over(axis):
    count = lax.axis_size(axis)
    span, shifts = 1, []
    while span < count:
        shifts.append(min(span, count - span))
        span += shifts[-1]
    return shifts


def with_others(value, axis, shifts):
    count = lax.axis_size(axis)
    others = [lax.ppermute(value, axis, exchange_pairs(count, k)) for k in shifts]
    return functools.reduce(jnp.maximum, others, value)


def per_device(density, momentum, energy, membership, slot_of_brick):
    count = lax.axis_size("section")
    groups = 2 * lax.axis_size("sim") * count
    conserved = jnp.concatenate([density[None], momentum, energy[None]], axis=0)
    matrix, first_x, last_x, labels = pack(conserved, membership, slot_of_brick)
    left = lax.ppermute(last_x, "section", ring("section", 1))
    right = lax.ppermute(first_x, "section", ring("section", -1))
    far = [lax.ppermute(labels, "section", ring("section", d)) for d in range(2, count - 1)]
    inside, down, up = own_fluxes(conserved)
    left, right, inside = lax.optimization_barrier((left, right, inside))
    first_y, last_y, columns = edge_rows(conserved, left, right)
    first_y, last_y, *far = lax.optimization_barrier((first_y, last_y, *far))
    top = lax.ppermute(last_y, "sim", ring("sim", 1))
    bottom = lax.ppermute(first_y, "sim", ring("sim", -1))
    chunks, blocks, rims = transform_bricks(count, inside, down, up, columns, matrix)
    early = early_rounds(count)
    moved = [lax.ppermute(chunks[i], "section", round_pairs(count, i)) for i in range(early)]
    top = lax.ppermute(last_y, "sim", ring("sim", 1))
    bottom = lax.ppermute(first_y, "sim", ring("sim", -1))
    chunks, blocks = mend(count, chunks[early:], top, bottom, blocks, rims, matrix)
    last = len(rounds_of(count)) - 1
    for i in range(early, last):
        moved.append(lax.ppermute(chunks[i - early], "section", round_pairs(count, i)))
    peaks = group_maxima(count, groups, membership.shape[0], blocks, [labels, left, *far, right])
    for i, shift in enumerate(steps_over("sim")):
        if i == 1:
            peaks, leaving = lax.optimization_barrier((peaks, chunks[last - early]))
            moved.append(lax.ppermute(leaving, "section", round_pairs(count, last)))
        peaks = with_others(peaks, "sim", [shift])
    peaks, moved[0] = lax.optimization_barrier((peaks, moved[0]))
    for shift in steps_over("section"):
        peaks = with_others(peaks, "section", [shift])
    return tuple(scale(count, groups, [*moved, chunks[-1]], peaks, labels))


def solution(mesh):
    placed = (
        P(None, "sim", "section"),
        P(None, None, "sim", "section"),
        P(None, "sim", "section"),
        P(("sim", "section"), None),
        P("sim", None),
    )
    return jax.shard_map(
        per_device,
        mesh=mesh,
        in_specs=placed,
        out_specs=(P(None, None, ("sim", "section"), None), P()),
        check_vma=False,
    )
```

```python
import functools

import jax
import jax.numpy as jnp
import numpy as np
from jax import lax
from jax.experimental import pallas as pl
from jax.experimental.pallas import tpu as pltpu
from jax.sharding import PartitionSpec as P

GAMMA_LESS = 0.4
COURANT = 0.05
DIFFUSE = 0.1
EPSILON = 1e-06
FIELDS = 5
PAD = 8
COLUMN_ROWS = 8
LABEL_ROWS = 8
LANES = 128
EVEN = 0.5
WIDE = float(np.sqrt(0.5) * np.cos(np.pi / 8))
NARROW = float(np.sqrt(0.5) * np.cos(3 * np.pi / 8))
VMEM_LIMIT = 48 * 1024 * 1024


def vmem():
    return pl.BlockSpec(memory_space=pltpu.VMEM)


def lanes_of(shape):
    return lax.broadcasted_iota(jnp.int32, shape, 1)


def butterfly(a, b, c, d):
    s, t, u, v = a + d, b + c, a - d, b - c
    return (
        EVEN * (s + t),
        WIDE * u + NARROW * v,
        EVEN * (s - t),
        NARROW * u - WIDE * v,
    )


def cosine(k, d):
    factor = 0.5 if k == 0 else np.sqrt(0.5)
    return float(factor * np.cos(np.pi * (2 * d + 1) * k / 8))


def write_matrix(matrix, width):
    step = 16
    row = lax.broadcasted_iota(jnp.int32, (step, width), 0)
    column = lanes_of((step, width))
    quarter = width // 4
    k, j, d = lax.div(column, quarter), lax.rem(column, quarter), lax.rem(row, 4)
    entry = jnp.zeros((step, width), jnp.float32)
    for a in range(4):
        for b in range(4):
            entry = jnp.where(jnp.logical_and(k == a, d == b), cosine(a, b), entry)
    high = entry.astype(jnp.bfloat16).astype(jnp.float32)
    low = entry - high
    zero = jnp.zeros((step, width), jnp.bfloat16)
    for start in range(0, width, step):
        own = j == lax.div(row + start, 4)
        upper = jnp.where(own, high, 0.0).astype(jnp.bfloat16)
        lower = jnp.where(own, low, 0.0).astype(jnp.bfloat16)
        matrix[start : start + step, 0:width] = upper
        matrix[start : start + step, width : 2 * width] = lower
        matrix[width + start : width + start + step, 0:width] = upper
        matrix[width + start : width + start + step, width : 2 * width] = zero


def kernel_params():
    return pltpu.CompilerParams(vmem_limit_bytes=VMEM_LIMIT)


def array(shape, dtype=jnp.float32):
    return jax.ShapeDtypeStruct(shape, dtype)


def pack_kernel(conserved, membership, slots, first_x, last_x, labels):
    fields, depth, y, width = conserved.shape
    quarter = y // 4
    lane = lanes_of((y, width))
    first = jnp.zeros((y, width), jnp.float32)
    last = jnp.zeros((y, width), jnp.float32)
    for j in range(fields * depth):
        value = conserved[j // depth, j % depth]
        first = jnp.where(lane == j, pltpu.roll(value, j, 1) if j else value, first)
        last = jnp.where(lane == j, pltpu.roll(value, j + 1, 1), last)
    rows, columns = membership.shape
    labels[...] = jnp.zeros(labels.shape, jnp.float32)
    for t in range(columns // LANES):
        part = membership[:, t * LANES : (t + 1) * LANES].astype(jnp.float32)
        labels[t * rows : (t + 1) * rows, :] = part
    labels[LABEL_ROWS - 1 : LABEL_ROWS, 0 : slots.shape[1]] = slots[...].astype(jnp.float32)
    own = labels[...]
    for column, out in ((first, first_x), (last, last_x)):
        packed = column[0:quarter]
        for c in range(1, 4):
            packed = packed + pltpu.roll(column[c * quarter : (c + 1) * quarter], 32 * c, 1)
        out[0:quarter, :] = packed
        out[quarter:, :] = own


def pack(conserved, membership, slots):
    y, width = conserved.shape[2:]
    shapes = [
        array((y // 4 + LABEL_ROWS, width)),
        array((y // 4 + LABEL_ROWS, width)),
        array((LABEL_ROWS, width)),
    ]
    return pl.pallas_call(
        pack_kernel,
        out_shape=shapes,
        in_specs=[vmem()] * 3,
        out_specs=[vmem()] * 3,
        compiler_params=kernel_params(),
    )(conserved, membership, slots)


def slot_of(labels, brick):
    row = labels[LABEL_ROWS - 1 : LABEL_ROWS, :]
    return jnp.max(jnp.where(lanes_of(row.shape) == brick, row, 0.0)).astype(jnp.int32)


def fluxes(c):
    rho, mx, my, mz, e = c
    inverse = 1.0 / rho
    u, v = mx * inverse, my * inverse
    pressure = GAMMA_LESS * (e - 0.5 * (mx * mx + my * my + mz * mz) * inverse)
    total = e + pressure
    flux_x = (mx, mx * u + pressure, my * u, mz * u, total * u)
    flux_y = (my, mx * v, my * v + pressure, mz * v, total * v)
    return flux_x, flux_y


def column_terms(own, depth, sign):
    fields = [pltpu.roll(own, LANES - depth * f, 1) if f else own for f in range(FIELDS)]
    flux_x, unused = fluxes(fields)
    return [DIFFUSE * fields[f] + sign * flux_x[f] for f in range(FIELDS)]


def row_terms(c):
    rows, width = c[0].shape
    lane = lanes_of((rows, width))
    flux_x, flux_y = fluxes(c)
    terms = []
    for f in range(FIELDS):
        base = DIFFUSE * c[f]
        gx, gy = COURANT * flux_x[f], COURANT * flux_y[f]
        from_left = jnp.where(lane == 0, 0.0, pltpu.roll(base + gx, 1, 1))
        from_right = jnp.where(lane == width - 1, 0.0, pltpu.roll(base - gx, width - 1, 1))
        terms.append(((1.0 - 4.0 * DIFFUSE) * c[f] + from_left + from_right, base + gy, base - gy))
    return terms


def beside(low, high, z):
    rows, width = low.shape
    lane = lanes_of((rows, width))
    at_left = pltpu.roll(low, LANES - z, 1) if z else low
    at_right = pltpu.roll(high, LANES - 1 - z, 1)
    return jnp.where(lane == 0, at_left, jnp.where(lane == width - 1, at_right, 0.0))


def fold_rows(across, down, up, j, origin, number, stride):
    t = {}
    for o in range(-3, 7):
        t[o] = (
            across[j, pl.ds(origin + o, number, stride=stride), :]
            + down[j, pl.ds(origin + o - 1, number, stride=stride), :]
            + up[j, pl.ds(origin + o + 1, number, stride=stride), :]
        )
    residual = [
        t[m] - (9.0 / 16.0) * (t[m - 1] + t[m + 1]) + (1.0 / 16.0) * (t[m - 3] + t[m + 3])
        for m in range(4)
    ]
    return butterfly(*residual)


def halves(value):
    high = value.astype(jnp.bfloat16)
    return high, (value - high.astype(jnp.float32)).astype(jnp.bfloat16)


def over_lanes(peak):
    peak = jnp.maximum(peak, pltpu.roll(peak, 64, 1))
    return jnp.maximum(peak, pltpu.roll(peak, 32, 1))


def partner_of(me, k, count):
    if count & (count - 1) == 0:
        return me ^ k
    return lax.rem(me + k, count)


def sender_of(me, k, count):
    if count & (count - 1) == 0:
        return me ^ k
    return lax.rem(me - k + count, count)


def flux_kernel(conserved, across, down, up, matrix):
    fields, depth, y, width = conserved.shape
    write_matrix(matrix, width)
    step = 16

    def flux_rows(i, carry):
        r = pl.ds(pl.multiple_of(i * step, step), step)
        padded = pl.ds(pl.multiple_of(i * step + PAD, PAD), step)
        for z in range(depth):
            for f, (a, d, u) in enumerate(row_terms([conserved[f, z, r, :] for f in range(fields)])):
                j = f * depth + z
                across[j, r, :] = a
                down[j, padded, :] = d
                up[j, padded, :] = u
        return carry

    lax.fori_loop(0, y // step, flux_rows, 0)


def own_fluxes(conserved):
    fields, depth, y, width = conserved.shape
    total = fields * depth
    tall = array((total, y + 2 * PAD, width))
    return pl.pallas_call(
        flux_kernel,
        out_shape=[array((total, y, width)), tall, tall, array((2 * width, 2 * width), jnp.bfloat16)],
        in_specs=[vmem()],
        out_specs=[vmem()] * 4,
        compiler_params=kernel_params(),
        cost_estimate=pl.CostEstimate(flops=40 * total * y * width, bytes_accessed=16 * total * y * width, transcendentals=0),
    )(conserved)


def edge_kernel(conserved, left, right, first_y, last_y, columns):
    fields, depth, y, width = conserved.shape
    total, quarter = fields * depth, y // 4
    for side, column in enumerate((left, right)):
        for c in range(4):
            value = column[0:quarter, :]
            value = pltpu.roll(value, LANES - 32 * c, 1) if c else value
            columns[side, c * quarter : (c + 1) * quarter, :] = value
        place = 4 * total + 4 * side
        first_y[place : place + 4, :] = columns[side, 0:4, :]
        last_y[place : place + 4, :] = columns[side, y - 4 : y, :]
    for j in range(total):
        first_y[4 * j : 4 * j + 4, :] = conserved[j // depth, j % depth, 0:4, :]
        last_y[4 * j : 4 * j + 4, :] = conserved[j // depth, j % depth, y - 4 : y, :]


def edge_rows(conserved, left, right):
    fields, depth, y, width = conserved.shape
    message = array((4 * fields * depth + COLUMN_ROWS, width))
    return pl.pallas_call(
        edge_kernel,
        out_shape=[message, message, array((2, y, width))],
        in_specs=[vmem()] * 3,
        out_specs=[vmem()] * 3,
        compiler_params=kernel_params(),
    )(conserved, left, right)


def brick_kernel(count, *refs):
    inside, down, up, columns, matrix = refs[:5]
    outs, refs = refs[5 : 5 + count], refs[5 + count :]
    blocks, rim_a, rim_d, rim_u, across, edges, split, coefficients, staged = refs
    total, y, width = inside.shape
    depth = total // FIELDS
    nb = y // 4
    rows = y // count

    for side in range(2):
        for f, value in enumerate(column_terms(columns[side], depth, COURANT if side == 0 else -COURANT)):
            edges[side, f] = value

    step = 24
    for start in range(0, y, step):
        for f in range(FIELDS):
            low, high = edges[0, f, start : start + step, :], edges[1, f, start : start + step, :]
            for z in range(depth):
                j = f * depth + z
                value = inside[j, start : start + step, :] + beside(low, high, z)
                across[j, PAD + start : PAD + start + step, :] = value
    for j in range(total):
        for source, rim in ((across, rim_a), (down, rim_d), (up, rim_u)):
            rim[j, 0:8, :] = source[j, PAD : PAD + 8, :]
            rim[j, 8:16, :] = source[j, y : y + 8, :]

    for f in range(FIELDS):
        rows_of = [fold_rows(across, down, up, f * depth + z, PAD, nb, 4) for z in range(4)]
        mixed = [butterfly(*[rows_of[z][m] for z in range(4)]) for m in range(4)]
        for k in range(4):
            high, low = halves(jnp.concatenate([mixed[m][k] for m in range(4)], axis=0))
            split[f, k * y : (k + 1) * y, 0:width] = high
            split[f, k * y : (k + 1) * y, width : 2 * width] = low
        product = jnp.dot(split[f], matrix[...], preferred_element_type=jnp.float32)
        result = product[:, 0:width] + product[:, width : 2 * width]
        peak = None
        for k in range(4):
            for m in range(4):
                value = result[k * y + m * nb : k * y + (m + 1) * nb]
                coefficients[f * depth + k, pl.ds(m, nb, stride=4), :] = value
                size = jnp.abs(value)
                peak = size if peak is None else jnp.maximum(peak, size)
        blocks[f] = over_lanes(peak)

    me = lax.axis_index("section")
    if rows % 8 == 0:
        for k in range(count):
            p = partner_of(me, k, count)
            for j in range(total):
                outs[k][j // depth, j % depth] = coefficients[j, pl.ds(pl.multiple_of(p * rows, 8), rows), :]
    else:
        for p in range(count):
            staged[p] = coefficients[:, p * rows : (p + 1) * rows, :]
        for k in range(count):
            p = partner_of(me, k, count)
            for j in range(total):
                outs[k][j // depth, j % depth] = staged[p, j]


def transform_bricks(count, inside, down, up, columns, matrix):
    total, y, width = inside.shape
    depth = total // FIELDS
    rows, tall = y // count, y + 2 * PAD
    chunk = array((FIELDS, depth, rows, width))
    rim = array((total, 2 * PAD, width))
    results = pl.pallas_call(
        functools.partial(brick_kernel, count),
        out_shape=[chunk] * count + [array((FIELDS, y // 4, width))] + [rim] * 3,
        in_specs=[vmem()] * 5,
        out_specs=[vmem()] * (count + 4),
        scratch_shapes=[
            pltpu.VMEM((total, tall, width), jnp.float32),
            pltpu.VMEM((2, FIELDS, y, width), jnp.float32),
            pltpu.VMEM((FIELDS, depth * y, 2 * width), jnp.bfloat16),
            pltpu.VMEM((total, y, width), jnp.float32),
            pltpu.VMEM((1, 1, 8, LANES) if rows % 8 == 0 else (count, total, rows, width), jnp.float32),
        ],
        compiler_params=kernel_params(),
        cost_estimate=pl.CostEstimate(flops=80 * total * y * width, bytes_accessed=16 * total * y * width, transcendentals=0),
    )(inside, down, up, columns, matrix)
    return results[:count], results[count], results[count + 1 :]


def leaving_order(count):
    return [*range(2, count), 1, 0]


def mend_kernel(count, *refs):
    chunks, refs = refs[:count], refs[count:]
    top, bottom, blocks, rim_a, rim_d, rim_u, matrix = refs[:7]
    outs, mended, refs = refs[7 : 7 + count], refs[7 + count], refs[8 + count :]
    halo, columns, across, down, up, folded, split, result, fixed = refs
    fields, depth, rows, width = chunks[0].shape
    total = fields * depth
    nb = blocks.shape[1]

    halo[...] = jnp.ones(halo.shape, jnp.float32)
    columns[...] = jnp.ones(columns.shape, jnp.float32)
    for j in range(total):
        halo[j, 4:8, :] = top[4 * j : 4 * j + 4, :]
        halo[j, 8:12, :] = bottom[4 * j : 4 * j + 4, :]
    for side in range(2):
        place = 4 * total + 4 * side
        columns[side, 4:8, :] = top[place : place + 4, :]
        columns[side, 8:12, :] = bottom[place : place + 4, :]
    low = column_terms(columns[0], depth, COURANT)
    high = column_terms(columns[1], depth, -COURANT)
    for z in range(depth):
        c = [halo[f * depth + z] for f in range(fields)]
        for f, (a, d, u) in enumerate(row_terms(c)):
            j = f * depth + z
            values = (a + beside(low[f], high[f], z), d, u)
            for value, rim, target in zip(values, (rim_a, rim_d, rim_u), (across, down, up)):
                target[j, 0:8, :] = value[0:8]
                target[j, 8:24, :] = rim[j]
                target[j, 24:32, :] = value[8:16]
    for j in range(total):
        for k, value in enumerate(fold_rows(across, down, up, j, PAD, 2, 12)):
            folded[j, 2 * k : 2 * k + 2, :] = value
    for f in range(fields):
        values = butterfly(*[folded[f * depth + z] for z in range(4)])
        for half in range(2):
            both = jnp.concatenate(values[2 * half : 2 * half + 2], axis=0)
            upper, lower = halves(both)
            place = f * 32 + half * 16
            split[place : place + 16, 0:width] = upper
            split[place : place + 16, width : 2 * width] = lower
    product = jnp.dot(split[...], matrix[...], preferred_element_type=jnp.float32)
    result[...] = product[:, 0:width] + product[:, width : 2 * width]
    for j in range(total):
        for side in range(2):
            fixed[side, j] = result[pl.ds(8 * j + side, 4, stride=2), :]
    mended[...] = blocks[...]
    for f in range(fields):
        for side in range(2):
            size = jnp.abs(fixed[side, f * depth])
            for z in range(1, depth):
                size = jnp.maximum(size, jnp.abs(fixed[side, f * depth + z]))
            peak = over_lanes(jnp.max(size, axis=0, keepdims=True))
            row = side * (nb - 1)
            mended[f, row : row + 1, :] = peak

    me = lax.axis_index("section")
    for i, k in enumerate(leaving_order(count)):
        p = partner_of(me, k, count)
        for side, start in ((0, 0), (1, rows - 4)):

            @pl.when(p == side * (count - 1))
            def replace(i=i, side=side, start=start):
                for j in range(total):
                    outs[i][j // depth, j % depth, start : start + 4, :] = fixed[side, j]


def mend(count, chunks, top, bottom, blocks, rims, matrix):
    fields, depth, rows, width = chunks[0].shape
    total = fields * depth
    tall = pltpu.VMEM((total, 4 * PAD, width), jnp.float32)
    results = pl.pallas_call(
        functools.partial(mend_kernel, count),
        out_shape=[array(chunks[0].shape)] * count + [array(blocks.shape)],
        in_specs=[vmem()] * (count + 7),
        out_specs=[vmem()] * (count + 1),
        input_output_aliases={k: k for k in range(count)},
        scratch_shapes=[
            pltpu.VMEM((total, 2 * PAD, width), jnp.float32),
            pltpu.VMEM((2, 2 * PAD, width), jnp.float32),
            tall,
            tall,
            tall,
            pltpu.VMEM((total, 8, width), jnp.float32),
            pltpu.VMEM((8 * total, 2 * width), jnp.bfloat16),
            pltpu.VMEM((8 * total, width), jnp.float32),
            pltpu.VMEM((2, total, 4, width), jnp.float32),
        ],
        compiler_params=kernel_params(),
    )(*[chunks[k] for k in leaving_order(count)], top, bottom, blocks, *rims, matrix)
    return dict(zip(leaving_order(count), results)), results[count]


def group_kernel(count, groups, own_rows, *refs):
    blocks, refs = refs[0], refs[1:]
    messages, (peaks, gathered, listed, packed, table) = refs[:count], refs[count:]
    nb = blocks.shape[1]
    me = lax.axis_index("section")
    slot = slot_of(messages[0], me)
    within = lax.rem(slot, 4) * 32
    tile = lax.div(slot, 4)
    for d, message in enumerate(messages):
        height = gathered.shape[1]
        value = message[message.shape[0] - height :, :]
        if count > 4:
            value = pltpu.roll(value, lax.rem(height - tile * own_rows, height), 0)
        gathered[lax.rem(me + count - d, count)] = value
    for q in range(count):
        listed[q * own_rows : (q + 1) * own_rows, :] = gathered[q, 0:own_rows, :]
    part = nb // 4
    band = lax.div(lanes_of((part, LANES)), 32)
    labels = jnp.zeros((part, LANES), jnp.float32)
    for c in range(4):
        turned = pltpu.roll(listed[c * part : (c + 1) * part, :], lax.rem(32 * c - within + LANES, LANES), 1)
        labels = jnp.where(band == c, turned, labels)
    for f in range(FIELDS):
        own = jnp.zeros((part, LANES), jnp.float32)
        for c in range(4):
            own = jnp.where(band == c, blocks[f, c * part : (c + 1) * part, :], own)
        packed[f, 0:part, :] = own
    lane8 = lanes_of((8, LANES))
    sub8 = lax.broadcasted_iota(jnp.int32, (8, LANES), 0)
    label_rows = [jnp.broadcast_to(labels[r : r + 1], (8, LANES)) for r in range(part)]

    def group_tile(g, carry):
        wanted = (sub8 + g * 8).astype(jnp.float32)
        matches = [label_rows[r] == wanted for r in range(part)]
        found = jnp.zeros((8, LANES), jnp.float32)
        for f in range(FIELDS):
            best = jnp.zeros((8, LANES), jnp.float32)
            for r in range(part):
                row = jnp.broadcast_to(packed[f, r : r + 1, :], (8, LANES))
                best = jnp.maximum(best, jnp.where(matches[r], row, 0.0))
            found = jnp.where(lane8 == f, jnp.max(best, axis=1, keepdims=True), found)
        table[pl.ds(pl.multiple_of(g * 8, 8), 8), :] = found
        return carry

    high = table.shape[0]
    if groups < high:
        table[...] = jnp.zeros((high, LANES), jnp.float32)
    lax.fori_loop(0, pl.cdiv(groups, 8), group_tile, 0)
    for g in range(high // LANES):
        peaks[:, g * LANES : (g + 1) * LANES] = jnp.transpose(table[g * LANES : (g + 1) * LANES, :])[0:8]


def group_maxima(count, groups, own_rows, blocks, messages):
    high = pl.cdiv(groups, LANES) * LANES
    nb = blocks.shape[1]
    return pl.pallas_call(
        functools.partial(group_kernel, count, groups, own_rows),
        out_shape=array((8, high)),
        in_specs=[vmem()] * (count + 1),
        out_specs=vmem(),
        scratch_shapes=[
            pltpu.VMEM((count, messages[0].shape[0], LANES), jnp.float32),
            pltpu.VMEM((nb, LANES), jnp.float32),
            pltpu.VMEM((FIELDS, 8, LANES), jnp.float32),
            pltpu.VMEM((high, LANES), jnp.float32),
        ],
        compiler_params=kernel_params(),
    )(blocks, *messages)


def scale_kernel(count, groups, *refs):
    chunks, refs = refs[:count], refs[count:]
    peaks, labels, coded, group_peak, done, wide, sems = refs
    fields, depth, rows, width = chunks[0].shape
    nb = rows // 4
    high = peaks.shape[1]
    me = lax.axis_index("section")
    group_peak[...] = peaks[0:fields, 0:groups]
    own_labels = labels[...].astype(jnp.int32)
    lane = lanes_of((8, LANES))
    inverse = 1.0 / (peaks[...] + EPSILON)
    places, owns = [], []
    for k in leaving_order(count):
        slot = slot_of(labels, sender_of(me, k, count))
        tile = own_labels
        if count > 4:
            tile = pltpu.roll(tile, lax.rem(LABEL_ROWS - lax.div(slot, 4) * nb, LABEL_ROWS), 0)
        within = lax.rem(slot, 4) * 32 + lax.rem(lane, 32)
        owns.append(jnp.take_along_axis(tile, within, axis=1))
        places.append(pl.ds(pl.multiple_of(slot * width, width), width))
    copies = []
    for f in range(fields):
        tables = [
            jnp.broadcast_to(inverse[f : f + 1, g * LANES : (g + 1) * LANES], (8, LANES)) for g in range(high // LANES)
        ]
        for i in range(count):
            if high == LANES:
                found = jnp.take_along_axis(tables[0], owns[i], axis=1)
            else:
                found = jnp.zeros((8, LANES), jnp.float32)
                inside = lax.rem(owns[i], LANES)
                for g in range(high // LANES):
                    here = jnp.take_along_axis(tables[g], inside, axis=1)
                    found = jnp.where(lax.div(owns[i], LANES) == g, here, found)
            for m in range(4):
                wide[i, f, pl.ds(m, nb, stride=4), :] = found[0:nb]
            factor = wide[i, f]
            for z in range(depth):
                done[f, z, :, places[i]] = chunks[i][f, z] * factor
        copies.append(pltpu.make_async_copy(done.at[f], coded.at[f], sems.at[f]))
        copies[-1].start()
    for copy in copies:
        copy.wait()


def scale(count, groups, chunks, peaks, labels):
    fields, depth, rows, width = chunks[0].shape
    whole = (fields, depth, rows, width * count)
    return pl.pallas_call(
        functools.partial(scale_kernel, count, groups),
        out_shape=[array(whole), array((fields, groups))],
        in_specs=[vmem()] * (count + 2),
        out_specs=[pl.BlockSpec(memory_space=pl.ANY), vmem()],
        scratch_shapes=[
            pltpu.VMEM(whole, jnp.float32),
            pltpu.VMEM((count, fields, rows, width), jnp.float32),
            pltpu.SemaphoreType.DMA((fields,)),
        ],
        compiler_params=kernel_params(),
    )(*chunks, peaks, labels)


def ring(axis, shift):
    count = lax.axis_size(axis)
    return [(i, (i + shift) % count) for i in range(count)]


def exchange_pairs(count, k):
    if count & (count - 1) == 0:
        return [(i, i ^ k) for i in range(count)]
    return [(i, (i + k) % count) for i in range(count)]


def steps_over(axis):
    count = lax.axis_size(axis)
    span, shifts = 1, []
    while span < count:
        shifts.append(min(span, count - span))
        span += shifts[-1]
    return shifts


def with_others(value, axis, shifts):
    count = lax.axis_size(axis)
    others = [lax.ppermute(value, axis, exchange_pairs(count, k)) for k in shifts]
    return functools.reduce(jnp.maximum, others, value)


def per_device(density, momentum, energy, membership, slot_of_brick):
    count = lax.axis_size("section")
    groups = 2 * lax.axis_size("sim") * count
    conserved = jnp.concatenate([density[None], momentum, energy[None]], axis=0)
    first_x, last_x, labels = pack(conserved, membership, slot_of_brick)
    left = lax.ppermute(last_x, "section", ring("section", 1))
    right = lax.ppermute(first_x, "section", ring("section", -1))
    far = [lax.ppermute(labels, "section", ring("section", d)) for d in range(2, count - 1)]
    inside, down, up, matrix = own_fluxes(conserved)
    left, right, inside = lax.optimization_barrier((left, right, inside))
    first_y, last_y, columns = edge_rows(conserved, left, right)
    top = lax.ppermute(last_y, "sim", ring("sim", 1))
    bottom = lax.ppermute(first_y, "sim", ring("sim", -1))
    chunks, blocks, rims = transform_bricks(count, inside, down, up, columns, matrix)
    blocks, *far = lax.optimization_barrier((blocks, *far))
    chunks, blocks = mend(count, chunks, top, bottom, blocks, rims, matrix)
    moved = {0: chunks[0]}
    for k in leaving_order(count)[:-1]:
        moved[k] = lax.ppermute(chunks[k], "section", exchange_pairs(count, k))
    peaks = group_maxima(count, groups, membership.shape[0], blocks, [labels, left, *far, right])
    for shift in steps_over("sim"):
        peaks = with_others(peaks, "sim", [shift])
    for shift in steps_over("section"):
        peaks = with_others(peaks, "section", [shift])
    return tuple(scale(count, groups, [moved[k] for k in leaving_order(count)], peaks, labels))


def solution(mesh):
    placed = (
        P(None, "sim", "section"),
        P(None, None, "sim", "section"),
        P(None, "sim", "section"),
        P(("sim", "section"), None),
        P("sim", None),
    )
    return jax.shard_map(
        per_device,
        mesh=mesh,
        in_specs=placed,
        out_specs=(P(None, None, ("sim", "section"), None), P()),
        check_vma=False,
    )
```

```python
import functools

import jax
import jax.numpy as jnp
import numpy as np
from jax import lax
from jax.experimental import pallas as pl
from jax.experimental.pallas import tpu as pltpu
from jax.sharding import PartitionSpec as P

GAMMA_LESS = 0.4
COURANT = 0.05
DIFFUSE = 0.1
EPSILON = 1e-06
FIELDS = 5
PAD = 8
COLUMN_ROWS = 8
LABEL_ROWS = 8
LANES = 128
EVEN = 0.5
WIDE = float(np.sqrt(0.5) * np.cos(np.pi / 8))
NARROW = float(np.sqrt(0.5) * np.cos(3 * np.pi / 8))
VMEM_LIMIT = 48 * 1024 * 1024


def vmem():
    return pl.BlockSpec(memory_space=pltpu.VMEM)


def lanes_of(shape):
    return lax.broadcasted_iota(jnp.int32, shape, 1)


def butterfly(a, b, c, d):
    s, t, u, v = a + d, b + c, a - d, b - c
    return (
        EVEN * (s + t),
        WIDE * u + NARROW * v,
        EVEN * (s - t),
        NARROW * u - WIDE * v,
    )


def cosine(k, d):
    factor = 0.5 if k == 0 else np.sqrt(0.5)
    return float(factor * np.cos(np.pi * (2 * d + 1) * k / 8))


def write_matrix(matrix, width):
    step = 16
    row = lax.broadcasted_iota(jnp.int32, (step, width), 0)
    column = lanes_of((step, width))
    quarter = width // 4
    k, j, d = lax.div(column, quarter), lax.rem(column, quarter), lax.rem(row, 4)
    entry = jnp.zeros((step, width), jnp.float32)
    for a in range(4):
        for b in range(4):
            entry = jnp.where(jnp.logical_and(k == a, d == b), cosine(a, b), entry)
    high = entry.astype(jnp.bfloat16).astype(jnp.float32)
    low = entry - high
    zero = jnp.zeros((step, width), jnp.bfloat16)
    for start in range(0, width, step):
        own = j == lax.div(row + start, 4)
        upper = jnp.where(own, high, 0.0).astype(jnp.bfloat16)
        lower = jnp.where(own, low, 0.0).astype(jnp.bfloat16)
        matrix[start : start + step, 0:width] = upper
        matrix[start : start + step, width : 2 * width] = lower
        matrix[width + start : width + start + step, 0:width] = upper
        matrix[width + start : width + start + step, width : 2 * width] = zero


def kernel_params():
    return pltpu.CompilerParams(vmem_limit_bytes=VMEM_LIMIT)


def array(shape, dtype=jnp.float32):
    return jax.ShapeDtypeStruct(shape, dtype)


def pack_kernel(conserved, membership, slots, first_x, last_x, labels):
    fields, depth, y, width = conserved.shape
    quarter = y // 4
    lane = lanes_of((y, width))
    first = jnp.zeros((y, width), jnp.float32)
    last = jnp.zeros((y, width), jnp.float32)
    for j in range(fields * depth):
        value = conserved[j // depth, j % depth]
        first = jnp.where(lane == j, pltpu.roll(value, j, 1) if j else value, first)
        last = jnp.where(lane == j, pltpu.roll(value, j + 1, 1), last)
    rows, columns = membership.shape
    labels[...] = jnp.zeros(labels.shape, jnp.float32)
    for t in range(columns // LANES):
        part = membership[:, t * LANES : (t + 1) * LANES].astype(jnp.float32)
        labels[t * rows : (t + 1) * rows, :] = part
    labels[LABEL_ROWS - 1 : LABEL_ROWS, 0 : slots.shape[1]] = slots[...].astype(jnp.float32)
    own = labels[...]
    for column, out in ((first, first_x), (last, last_x)):
        packed = column[0:quarter]
        for c in range(1, 4):
            packed = packed + pltpu.roll(column[c * quarter : (c + 1) * quarter], 32 * c, 1)
        out[0:quarter, :] = packed
        out[quarter:, :] = own


def pack(conserved, membership, slots):
    y, width = conserved.shape[2:]
    shapes = [
        array((y // 4 + LABEL_ROWS, width)),
        array((y // 4 + LABEL_ROWS, width)),
        array((LABEL_ROWS, width)),
    ]
    return pl.pallas_call(
        pack_kernel,
        out_shape=shapes,
        in_specs=[vmem()] * 3,
        out_specs=[vmem()] * 3,
        compiler_params=kernel_params(),
    )(conserved, membership, slots)


def slot_of(labels, brick):
    row = labels[LABEL_ROWS - 1 : LABEL_ROWS, :]
    return jnp.max(jnp.where(lanes_of(row.shape) == brick, row, 0.0)).astype(jnp.int32)


def fluxes(c):
    rho, mx, my, mz, e = c
    inverse = 1.0 / rho
    u, v = mx * inverse, my * inverse
    pressure = GAMMA_LESS * (e - 0.5 * (mx * mx + my * my + mz * mz) * inverse)
    total = e + pressure
    flux_x = (mx, mx * u + pressure, my * u, mz * u, total * u)
    flux_y = (my, mx * v, my * v + pressure, mz * v, total * v)
    return flux_x, flux_y


def column_terms(own, depth, sign):
    fields = [pltpu.roll(own, LANES - depth * f, 1) if f else own for f in range(FIELDS)]
    flux_x, unused = fluxes(fields)
    return [DIFFUSE * fields[f] + sign * flux_x[f] for f in range(FIELDS)]


def row_terms(c):
    rows, width = c[0].shape
    lane = lanes_of((rows, width))
    flux_x, flux_y = fluxes(c)
    terms = []
    for f in range(FIELDS):
        base = DIFFUSE * c[f]
        gx, gy = COURANT * flux_x[f], COURANT * flux_y[f]
        from_left = jnp.where(lane == 0, 0.0, pltpu.roll(base + gx, 1, 1))
        from_right = jnp.where(lane == width - 1, 0.0, pltpu.roll(base - gx, width - 1, 1))
        terms.append(((1.0 - 4.0 * DIFFUSE) * c[f] + from_left + from_right, base + gy, base - gy))
    return terms


def beside(low, high, z):
    rows, width = low.shape
    lane = lanes_of((rows, width))
    at_left = pltpu.roll(low, LANES - z, 1) if z else low
    at_right = pltpu.roll(high, LANES - 1 - z, 1)
    return jnp.where(lane == 0, at_left, jnp.where(lane == width - 1, at_right, 0.0))


def fold_rows(across, down, up, j, origin, number, stride):
    t = {}
    for o in range(-3, 7):
        t[o] = (
            across[j, pl.ds(origin + o, number, stride=stride), :]
            + down[j, pl.ds(origin + o - 1, number, stride=stride), :]
            + up[j, pl.ds(origin + o + 1, number, stride=stride), :]
        )
    residual = [
        t[m] - (9.0 / 16.0) * (t[m - 1] + t[m + 1]) + (1.0 / 16.0) * (t[m - 3] + t[m + 3])
        for m in range(4)
    ]
    return butterfly(*residual)


def halves(value):
    high = value.astype(jnp.bfloat16)
    return high, (value - high.astype(jnp.float32)).astype(jnp.bfloat16)


def over_lanes(peak):
    peak = jnp.maximum(peak, pltpu.roll(peak, 64, 1))
    return jnp.maximum(peak, pltpu.roll(peak, 32, 1))


def partner_of(me, k, count):
    if count & (count - 1) == 0:
        return me ^ k
    return lax.rem(me + k, count)


def sender_of(me, k, count):
    if count & (count - 1) == 0:
        return me ^ k
    return lax.rem(me - k + count, count)


def flux_kernel(conserved, across, down, up, matrix):
    fields, depth, y, width = conserved.shape
    write_matrix(matrix, width)
    step = 16

    def flux_rows(i, carry):
        r = pl.ds(pl.multiple_of(i * step, step), step)
        padded = pl.ds(pl.multiple_of(i * step + PAD, PAD), step)
        for z in range(depth):
            for f, (a, d, u) in enumerate(row_terms([conserved[f, z, r, :] for f in range(fields)])):
                j = f * depth + z
                across[j, r, :] = a
                down[j, padded, :] = d
                up[j, padded, :] = u
        return carry

    lax.fori_loop(0, y // step, flux_rows, 0)


def own_fluxes(conserved):
    fields, depth, y, width = conserved.shape
    total = fields * depth
    tall = array((total, y + 2 * PAD, width))
    return pl.pallas_call(
        flux_kernel,
        out_shape=[array((total, y, width)), tall, tall, array((2 * width, 2 * width), jnp.bfloat16)],
        in_specs=[vmem()],
        out_specs=[vmem()] * 4,
        compiler_params=kernel_params(),
        cost_estimate=pl.CostEstimate(flops=40 * total * y * width, bytes_accessed=16 * total * y * width, transcendentals=0),
    )(conserved)


def edge_kernel(conserved, left, right, first_y, last_y, columns):
    fields, depth, y, width = conserved.shape
    total, quarter = fields * depth, y // 4
    for side, column in enumerate((left, right)):
        for c in range(4):
            value = column[0:quarter, :]
            value = pltpu.roll(value, LANES - 32 * c, 1) if c else value
            columns[side, c * quarter : (c + 1) * quarter, :] = value
        place = 4 * total + 4 * side
        first_y[place : place + 4, :] = columns[side, 0:4, :]
        last_y[place : place + 4, :] = columns[side, y - 4 : y, :]
    for j in range(total):
        first_y[4 * j : 4 * j + 4, :] = conserved[j // depth, j % depth, 0:4, :]
        last_y[4 * j : 4 * j + 4, :] = conserved[j // depth, j % depth, y - 4 : y, :]


def edge_rows(conserved, left, right):
    fields, depth, y, width = conserved.shape
    message = array((4 * fields * depth + COLUMN_ROWS, width))
    return pl.pallas_call(
        edge_kernel,
        out_shape=[message, message, array((2, y, width))],
        in_specs=[vmem()] * 3,
        out_specs=[vmem()] * 3,
        compiler_params=kernel_params(),
    )(conserved, left, right)


def brick_kernel(count, *refs):
    inside, down, up, columns, matrix = refs[:5]
    outs, refs = refs[5 : 5 + count], refs[5 + count :]
    blocks, rim_a, rim_d, rim_u, across, edges, split, coefficients, staged = refs
    total, y, width = inside.shape
    depth = total // FIELDS
    nb = y // 4
    rows = y // count

    for side in range(2):
        for f, value in enumerate(column_terms(columns[side], depth, COURANT if side == 0 else -COURANT)):
            edges[side, f] = value

    step = 24
    for start in range(0, y, step):
        for f in range(FIELDS):
            low, high = edges[0, f, start : start + step, :], edges[1, f, start : start + step, :]
            for z in range(depth):
                j = f * depth + z
                value = inside[j, start : start + step, :] + beside(low, high, z)
                across[j, PAD + start : PAD + start + step, :] = value
    for j in range(total):
        for source, rim in ((across, rim_a), (down, rim_d), (up, rim_u)):
            rim[j, 0:8, :] = source[j, PAD : PAD + 8, :]
            rim[j, 8:16, :] = source[j, y : y + 8, :]

    for f in range(FIELDS):
        rows_of = [fold_rows(across, down, up, f * depth + z, PAD, nb, 4) for z in range(4)]
        mixed = [butterfly(*[rows_of[z][m] for z in range(4)]) for m in range(4)]
        for k in range(4):
            high, low = halves(jnp.concatenate([mixed[m][k] for m in range(4)], axis=0))
            split[f, k * y : (k + 1) * y, 0:width] = high
            split[f, k * y : (k + 1) * y, width : 2 * width] = low
        product = jnp.dot(split[f], matrix[...], preferred_element_type=jnp.float32)
        result = product[:, 0:width] + product[:, width : 2 * width]
        peak = None
        for k in range(4):
            for m in range(4):
                value = result[k * y + m * nb : k * y + (m + 1) * nb]
                coefficients[f * depth + k, pl.ds(m, nb, stride=4), :] = value
                size = jnp.abs(value)
                peak = size if peak is None else jnp.maximum(peak, size)
        blocks[f] = over_lanes(peak)

    me = lax.axis_index("section")
    if rows % 8 == 0:
        for k in range(count):
            p = partner_of(me, k, count)
            for j in range(total):
                outs[k][j // depth, j % depth] = coefficients[j, pl.ds(pl.multiple_of(p * rows, 8), rows), :]
    else:
        for p in range(count):
            staged[p] = coefficients[:, p * rows : (p + 1) * rows, :]
        for k in range(count):
            p = partner_of(me, k, count)
            for j in range(total):
                outs[k][j // depth, j % depth] = staged[p, j]


def transform_bricks(count, inside, down, up, columns, matrix):
    total, y, width = inside.shape
    depth = total // FIELDS
    rows, tall = y // count, y + 2 * PAD
    chunk = array((FIELDS, depth, rows, width))
    rim = array((total, 2 * PAD, width))
    results = pl.pallas_call(
        functools.partial(brick_kernel, count),
        out_shape=[chunk] * count + [array((FIELDS, y // 4, width))] + [rim] * 3,
        in_specs=[vmem()] * 5,
        out_specs=[vmem()] * (count + 4),
        scratch_shapes=[
            pltpu.VMEM((total, tall, width), jnp.float32),
            pltpu.VMEM((2, FIELDS, y, width), jnp.float32),
            pltpu.VMEM((FIELDS, depth * y, 2 * width), jnp.bfloat16),
            pltpu.VMEM((total, y, width), jnp.float32),
            pltpu.VMEM((1, 1, 8, LANES) if rows % 8 == 0 else (count, total, rows, width), jnp.float32),
        ],
        compiler_params=kernel_params(),
        cost_estimate=pl.CostEstimate(flops=80 * total * y * width, bytes_accessed=16 * total * y * width, transcendentals=0),
    )(inside, down, up, columns, matrix)
    return results[:count], results[count], results[count + 1 :]


def leaving_order(count):
    return [*range(2, count), 1, 0]


def mend_kernel(count, *refs):
    chunks, refs = refs[:count], refs[count:]
    top, bottom, blocks, rim_a, rim_d, rim_u, matrix = refs[:7]
    outs, mended, refs = refs[7 : 7 + count], refs[7 + count], refs[8 + count :]
    halo, columns, across, down, up, folded, split, result, fixed = refs
    fields, depth, rows, width = chunks[0].shape
    total = fields * depth
    nb = blocks.shape[1]

    halo[...] = jnp.ones(halo.shape, jnp.float32)
    columns[...] = jnp.ones(columns.shape, jnp.float32)
    for j in range(total):
        halo[j, 4:8, :] = top[4 * j : 4 * j + 4, :]
        halo[j, 8:12, :] = bottom[4 * j : 4 * j + 4, :]
    for side in range(2):
        place = 4 * total + 4 * side
        columns[side, 4:8, :] = top[place : place + 4, :]
        columns[side, 8:12, :] = bottom[place : place + 4, :]
    low = column_terms(columns[0], depth, COURANT)
    high = column_terms(columns[1], depth, -COURANT)
    for z in range(depth):
        c = [halo[f * depth + z] for f in range(fields)]
        for f, (a, d, u) in enumerate(row_terms(c)):
            j = f * depth + z
            values = (a + beside(low[f], high[f], z), d, u)
            for value, rim, target in zip(values, (rim_a, rim_d, rim_u), (across, down, up)):
                target[j, 0:8, :] = value[0:8]
                target[j, 8:24, :] = rim[j]
                target[j, 24:32, :] = value[8:16]
    for j in range(total):
        for k, value in enumerate(fold_rows(across, down, up, j, PAD, 2, 12)):
            folded[j, 2 * k : 2 * k + 2, :] = value
    for f in range(fields):
        values = butterfly(*[folded[f * depth + z] for z in range(4)])
        for half in range(2):
            both = jnp.concatenate(values[2 * half : 2 * half + 2], axis=0)
            upper, lower = halves(both)
            place = f * 32 + half * 16
            split[place : place + 16, 0:width] = upper
            split[place : place + 16, width : 2 * width] = lower
    product = jnp.dot(split[...], matrix[...], preferred_element_type=jnp.float32)
    result[...] = product[:, 0:width] + product[:, width : 2 * width]
    for j in range(total):
        for side in range(2):
            fixed[side, j] = result[pl.ds(8 * j + side, 4, stride=2), :]
    mended[...] = blocks[...]
    for f in range(fields):
        for side in range(2):
            size = jnp.abs(fixed[side, f * depth])
            for z in range(1, depth):
                size = jnp.maximum(size, jnp.abs(fixed[side, f * depth + z]))
            peak = over_lanes(jnp.max(size, axis=0, keepdims=True))
            row = side * (nb - 1)
            mended[f, row : row + 1, :] = peak

    me = lax.axis_index("section")
    for i, k in enumerate(leaving_order(count)):
        p = partner_of(me, k, count)
        for side, start in ((0, 0), (1, rows - 4)):

            @pl.when(p == side * (count - 1))
            def replace(i=i, side=side, start=start):
                for j in range(total):
                    outs[i][j // depth, j % depth, start : start + 4, :] = fixed[side, j]


def mend(count, chunks, top, bottom, blocks, rims, matrix):
    fields, depth, rows, width = chunks[0].shape
    total = fields * depth
    tall = pltpu.VMEM((total, 4 * PAD, width), jnp.float32)
    results = pl.pallas_call(
        functools.partial(mend_kernel, count),
        out_shape=[array(chunks[0].shape)] * count + [array(blocks.shape)],
        in_specs=[vmem()] * (count + 7),
        out_specs=[vmem()] * (count + 1),
        input_output_aliases={k: k for k in range(count)},
        scratch_shapes=[
            pltpu.VMEM((total, 2 * PAD, width), jnp.float32),
            pltpu.VMEM((2, 2 * PAD, width), jnp.float32),
            tall,
            tall,
            tall,
            pltpu.VMEM((total, 8, width), jnp.float32),
            pltpu.VMEM((8 * total, 2 * width), jnp.bfloat16),
            pltpu.VMEM((8 * total, width), jnp.float32),
            pltpu.VMEM((2, total, 4, width), jnp.float32),
        ],
        compiler_params=kernel_params(),
    )(*[chunks[k] for k in leaving_order(count)], top, bottom, blocks, *rims, matrix)
    return dict(zip(leaving_order(count), results)), results[count]


def group_kernel(count, groups, own_rows, *refs):
    blocks, refs = refs[0], refs[1:]
    messages, (peaks, gathered, listed, packed, table) = refs[:count], refs[count:]
    nb = blocks.shape[1]
    me = lax.axis_index("section")
    slot = slot_of(messages[0], me)
    within = lax.rem(slot, 4) * 32
    tile = lax.div(slot, 4)
    for d, message in enumerate(messages):
        height = gathered.shape[1]
        value = message[message.shape[0] - height :, :]
        if count > 4:
            value = pltpu.roll(value, lax.rem(height - tile * own_rows, height), 0)
        gathered[lax.rem(me + count - d, count)] = value
    for q in range(count):
        listed[q * own_rows : (q + 1) * own_rows, :] = gathered[q, 0:own_rows, :]
    part = nb // 4
    band = lax.div(lanes_of((part, LANES)), 32)
    labels = jnp.zeros((part, LANES), jnp.float32)
    for c in range(4):
        turned = pltpu.roll(listed[c * part : (c + 1) * part, :], lax.rem(32 * c - within + LANES, LANES), 1)
        labels = jnp.where(band == c, turned, labels)
    for f in range(FIELDS):
        own = jnp.zeros((part, LANES), jnp.float32)
        for c in range(4):
            own = jnp.where(band == c, blocks[f, c * part : (c + 1) * part, :], own)
        packed[f, 0:part, :] = own
    lane8 = lanes_of((8, LANES))
    sub8 = lax.broadcasted_iota(jnp.int32, (8, LANES), 0)
    label_rows = [jnp.broadcast_to(labels[r : r + 1], (8, LANES)) for r in range(part)]

    def group_tile(g, carry):
        wanted = (sub8 + g * 8).astype(jnp.float32)
        matches = [label_rows[r] == wanted for r in range(part)]
        found = jnp.zeros((8, LANES), jnp.float32)
        for f in range(FIELDS):
            best = jnp.zeros((8, LANES), jnp.float32)
            for r in range(part):
                row = jnp.broadcast_to(packed[f, r : r + 1, :], (8, LANES))
                best = jnp.maximum(best, jnp.where(matches[r], row, 0.0))
            found = jnp.where(lane8 == f, jnp.max(best, axis=1, keepdims=True), found)
        table[pl.ds(pl.multiple_of(g * 8, 8), 8), :] = found
        return carry

    high = table.shape[0]
    if groups < high:
        table[...] = jnp.zeros((high, LANES), jnp.float32)
    lax.fori_loop(0, pl.cdiv(groups, 8), group_tile, 0)
    for g in range(high // LANES):
        peaks[:, g * LANES : (g + 1) * LANES] = jnp.transpose(table[g * LANES : (g + 1) * LANES, :])[0:8]


def group_maxima(count, groups, own_rows, blocks, messages):
    high = pl.cdiv(groups, LANES) * LANES
    nb = blocks.shape[1]
    return pl.pallas_call(
        functools.partial(group_kernel, count, groups, own_rows),
        out_shape=array((8, high)),
        in_specs=[vmem()] * (count + 1),
        out_specs=vmem(),
        scratch_shapes=[
            pltpu.VMEM((count, messages[0].shape[0], LANES), jnp.float32),
            pltpu.VMEM((nb, LANES), jnp.float32),
            pltpu.VMEM((FIELDS, 8, LANES), jnp.float32),
            pltpu.VMEM((high, LANES), jnp.float32),
        ],
        compiler_params=kernel_params(),
    )(blocks, *messages)


def scale_kernel(count, groups, *refs):
    chunks, refs = refs[:count], refs[count:]
    peaks, labels, coded, group_peak, wide = refs
    fields, depth, rows, width = chunks[0].shape
    nb = rows // 4
    high = peaks.shape[1]
    me = lax.axis_index("section")
    group_peak[...] = peaks[0:fields, 0:groups]
    own_labels = labels[...].astype(jnp.int32)
    lane = lanes_of((8, LANES))
    inverse = 1.0 / (peaks[...] + EPSILON)
    tables = [
        [jnp.broadcast_to(inverse[f : f + 1, g * LANES : (g + 1) * LANES], (8, LANES)) for g in range(high // LANES)]
        for f in range(fields)
    ]
    for i, k in enumerate(leaving_order(count)):
        slot = slot_of(labels, sender_of(me, k, count))
        tile = own_labels
        if count > 4:
            tile = pltpu.roll(tile, lax.rem(LABEL_ROWS - lax.div(slot, 4) * nb, LABEL_ROWS), 0)
        within = lax.rem(slot, 4) * 32 + lax.rem(lane, 32)
        own = jnp.take_along_axis(tile, within, axis=1)
        place = pl.ds(pl.multiple_of(slot * width, width), width)
        for f in range(fields):
            if high == LANES:
                found = jnp.take_along_axis(tables[f][0], own, axis=1)
            else:
                found = jnp.zeros((8, LANES), jnp.float32)
                inside = lax.rem(own, LANES)
                for g in range(high // LANES):
                    here = jnp.take_along_axis(tables[f][g], inside, axis=1)
                    found = jnp.where(lax.div(own, LANES) == g, here, found)
            for m in range(4):
                wide[i, f, pl.ds(m, nb, stride=4), :] = found[0:nb]
            factor = wide[i, f]
            for z in range(depth):
                coded[f, z, :, place] = chunks[i][f, z] * factor


def scale(count, groups, chunks, peaks, labels):
    fields, depth, rows, width = chunks[0].shape
    return pl.pallas_call(
        functools.partial(scale_kernel, count, groups),
        out_shape=[array((fields, depth, rows, width * count)), array((fields, groups))],
        in_specs=[vmem()] * (count + 2),
        out_specs=[vmem()] * 2,
        scratch_shapes=[
            pltpu.VMEM((count, fields, rows, width), jnp.float32),
        ],
        compiler_params=kernel_params(),
    )(*chunks, peaks, labels)


def ring(axis, shift):
    count = lax.axis_size(axis)
    return [(i, (i + shift) % count) for i in range(count)]


def exchange_pairs(count, k):
    if count & (count - 1) == 0:
        return [(i, i ^ k) for i in range(count)]
    return [(i, (i + k) % count) for i in range(count)]


def steps_over(axis):
    count = lax.axis_size(axis)
    span, shifts = 1, []
    while span < count:
        shifts.append(min(span, count - span))
        span += shifts[-1]
    return shifts


def with_others(value, axis, shifts):
    count = lax.axis_size(axis)
    others = [lax.ppermute(value, axis, exchange_pairs(count, k)) for k in shifts]
    return functools.reduce(jnp.maximum, others, value)


def per_device(density, momentum, energy, membership, slot_of_brick):
    count = lax.axis_size("section")
    groups = 2 * lax.axis_size("sim") * count
    conserved = jnp.concatenate([density[None], momentum, energy[None]], axis=0)
    first_x, last_x, labels = pack(conserved, membership, slot_of_brick)
    left = lax.ppermute(last_x, "section", ring("section", 1))
    right = lax.ppermute(first_x, "section", ring("section", -1))
    far = [lax.ppermute(labels, "section", ring("section", d)) for d in range(2, count - 1)]
    inside, down, up, matrix = own_fluxes(conserved)
    left, right, inside = lax.optimization_barrier((left, right, inside))
    first_y, last_y, columns = edge_rows(conserved, left, right)
    top = lax.ppermute(last_y, "sim", ring("sim", 1))
    bottom = lax.ppermute(first_y, "sim", ring("sim", -1))
    chunks, blocks, rims = transform_bricks(count, inside, down, up, columns, matrix)
    blocks, *far = lax.optimization_barrier((blocks, *far))
    chunks, blocks = mend(count, chunks, top, bottom, blocks, rims, matrix)
    moved = {0: chunks[0]}
    for k in leaving_order(count)[:-1]:
        moved[k] = lax.ppermute(chunks[k], "section", exchange_pairs(count, k))
    peaks = group_maxima(count, groups, membership.shape[0], blocks, [labels, left, *far, right])
    for shift in steps_over("sim"):
        peaks = with_others(peaks, "sim", [shift])
    for shift in steps_over("section"):
        peaks = with_others(peaks, "section", [shift])
    return tuple(scale(count, groups, [moved[k] for k in leaving_order(count)], peaks, labels))


def solution(mesh):
    placed = (
        P(None, "sim", "section"),
        P(None, None, "sim", "section"),
        P(None, "sim", "section"),
        P(("sim", "section"), None),
        P("sim", None),
    )
    return jax.shard_map(
        per_device,
        mesh=mesh,
        in_specs=placed,
        out_specs=(P(None, None, ("sim", "section"), None), P()),
        check_vma=False,
    )
```

```python
import functools

import jax
import jax.numpy as jnp
import numpy as np
from jax import lax
from jax.experimental import pallas as pl
from jax.experimental.pallas import tpu as pltpu
from jax.sharding import PartitionSpec as P

GAMMA_LESS = 0.4
COURANT = 0.05
DIFFUSE = 0.1
EPSILON = 1e-06
FIELDS = 5
PAD = 8
COLUMN_ROWS = 8
LABEL_ROWS = 8
LANES = 128
EVEN = 0.5
WIDE = float(np.sqrt(0.5) * np.cos(np.pi / 8))
NARROW = float(np.sqrt(0.5) * np.cos(3 * np.pi / 8))
VMEM_LIMIT = 48 * 1024 * 1024


def vmem():
    return pl.BlockSpec(memory_space=pltpu.VMEM)


def lanes_of(shape):
    return lax.broadcasted_iota(jnp.int32, shape, 1)


def butterfly(a, b, c, d):
    s, t, u, v = a + d, b + c, a - d, b - c
    return (
        EVEN * (s + t),
        WIDE * u + NARROW * v,
        EVEN * (s - t),
        NARROW * u - WIDE * v,
    )


def cosine(k, d):
    factor = 0.5 if k == 0 else np.sqrt(0.5)
    return float(factor * np.cos(np.pi * (2 * d + 1) * k / 8))


def write_matrix(matrix, width):
    step = 16
    row = lax.broadcasted_iota(jnp.int32, (step, width), 0)
    column = lanes_of((step, width))
    quarter = width // 4
    k, j, d = lax.div(column, quarter), lax.rem(column, quarter), lax.rem(row, 4)
    entry = jnp.zeros((step, width), jnp.float32)
    for a in range(4):
        for b in range(4):
            entry = jnp.where(jnp.logical_and(k == a, d == b), cosine(a, b), entry)
    high = entry.astype(jnp.bfloat16).astype(jnp.float32)
    low = entry - high
    zero = jnp.zeros((step, width), jnp.bfloat16)
    for start in range(0, width, step):
        own = j == lax.div(row + start, 4)
        upper = jnp.where(own, high, 0.0).astype(jnp.bfloat16)
        lower = jnp.where(own, low, 0.0).astype(jnp.bfloat16)
        matrix[start : start + step, 0:width] = upper
        matrix[start : start + step, width : 2 * width] = lower
        matrix[width + start : width + start + step, 0:width] = upper
        matrix[width + start : width + start + step, width : 2 * width] = zero


def kernel_params():
    return pltpu.CompilerParams(vmem_limit_bytes=VMEM_LIMIT)


def array(shape, dtype=jnp.float32):
    return jax.ShapeDtypeStruct(shape, dtype)


def pack_kernel(conserved, membership, slots, first_x, last_x, labels):
    fields, depth, y, width = conserved.shape
    quarter = y // 4
    lane = lanes_of((y, width))
    first = jnp.zeros((y, width), jnp.float32)
    last = jnp.zeros((y, width), jnp.float32)
    for j in range(fields * depth):
        value = conserved[j // depth, j % depth]
        first = jnp.where(lane == j, pltpu.roll(value, j, 1) if j else value, first)
        last = jnp.where(lane == j, pltpu.roll(value, j + 1, 1), last)
    rows, columns = membership.shape
    labels[...] = jnp.zeros(labels.shape, jnp.float32)
    for t in range(columns // LANES):
        part = membership[:, t * LANES : (t + 1) * LANES].astype(jnp.float32)
        labels[t * rows : (t + 1) * rows, :] = part
    labels[LABEL_ROWS - 1 : LABEL_ROWS, 0 : slots.shape[1]] = slots[...].astype(jnp.float32)
    own = labels[...]
    for column, out in ((first, first_x), (last, last_x)):
        packed = column[0:quarter]
        for c in range(1, 4):
            packed = packed + pltpu.roll(column[c * quarter : (c + 1) * quarter], 32 * c, 1)
        out[0:quarter, :] = packed
        out[quarter:, :] = own


def pack(conserved, membership, slots):
    y, width = conserved.shape[2:]
    shapes = [
        array((y // 4 + LABEL_ROWS, width)),
        array((y // 4 + LABEL_ROWS, width)),
        array((LABEL_ROWS, width)),
    ]
    return pl.pallas_call(
        pack_kernel,
        out_shape=shapes,
        in_specs=[vmem()] * 3,
        out_specs=[vmem()] * 3,
        compiler_params=kernel_params(),
    )(conserved, membership, slots)


def slot_of(labels, brick):
    row = labels[LABEL_ROWS - 1 : LABEL_ROWS, :]
    return jnp.max(jnp.where(lanes_of(row.shape) == brick, row, 0.0)).astype(jnp.int32)


def fluxes(c):
    rho, mx, my, mz, e = c
    inverse = 1.0 / rho
    u, v = mx * inverse, my * inverse
    pressure = GAMMA_LESS * (e - 0.5 * (mx * mx + my * my + mz * mz) * inverse)
    total = e + pressure
    flux_x = (mx, mx * u + pressure, my * u, mz * u, total * u)
    flux_y = (my, mx * v, my * v + pressure, mz * v, total * v)
    return flux_x, flux_y


def column_terms(own, depth, sign):
    fields = [pltpu.roll(own, LANES - depth * f, 1) if f else own for f in range(FIELDS)]
    flux_x, unused = fluxes(fields)
    return [DIFFUSE * fields[f] + sign * flux_x[f] for f in range(FIELDS)]


def row_terms(c):
    rows, width = c[0].shape
    lane = lanes_of((rows, width))
    flux_x, flux_y = fluxes(c)
    terms = []
    for f in range(FIELDS):
        base = DIFFUSE * c[f]
        gx, gy = COURANT * flux_x[f], COURANT * flux_y[f]
        from_left = jnp.where(lane == 0, 0.0, pltpu.roll(base + gx, 1, 1))
        from_right = jnp.where(lane == width - 1, 0.0, pltpu.roll(base - gx, width - 1, 1))
        terms.append(((1.0 - 4.0 * DIFFUSE) * c[f] + from_left + from_right, base + gy, base - gy))
    return terms


def beside(low, high, z):
    rows, width = low.shape
    lane = lanes_of((rows, width))
    at_left = pltpu.roll(low, LANES - z, 1) if z else low
    at_right = pltpu.roll(high, LANES - 1 - z, 1)
    return jnp.where(lane == 0, at_left, jnp.where(lane == width - 1, at_right, 0.0))


def fold_rows(across, down, up, j, origin, number, stride):
    t = {}
    for o in range(-3, 7):
        t[o] = (
            across[j, pl.ds(origin + o, number, stride=stride), :]
            + down[j, pl.ds(origin + o - 1, number, stride=stride), :]
            + up[j, pl.ds(origin + o + 1, number, stride=stride), :]
        )
    residual = [
        t[m] - (9.0 / 16.0) * (t[m - 1] + t[m + 1]) + (1.0 / 16.0) * (t[m - 3] + t[m + 3])
        for m in range(4)
    ]
    return butterfly(*residual)


def halves(value):
    high = value.astype(jnp.bfloat16)
    return high, (value - high.astype(jnp.float32)).astype(jnp.bfloat16)


def over_lanes(peak):
    peak = jnp.maximum(peak, pltpu.roll(peak, 64, 1))
    return jnp.maximum(peak, pltpu.roll(peak, 32, 1))


def partner_of(me, k, count):
    if count & (count - 1) == 0:
        return me ^ k
    return lax.rem(me + k, count)


def sender_of(me, k, count):
    if count & (count - 1) == 0:
        return me ^ k
    return lax.rem(me - k + count, count)


def flux_kernel(conserved, across, down, up, matrix):
    fields, depth, y, width = conserved.shape
    write_matrix(matrix, width)
    step = 16

    def flux_rows(i, carry):
        r = pl.ds(pl.multiple_of(i * step, step), step)
        padded = pl.ds(pl.multiple_of(i * step + PAD, PAD), step)
        for z in range(depth):
            for f, (a, d, u) in enumerate(row_terms([conserved[f, z, r, :] for f in range(fields)])):
                j = f * depth + z
                across[j, r, :] = a
                down[j, padded, :] = d
                up[j, padded, :] = u
        return carry

    lax.fori_loop(0, y // step, flux_rows, 0)


def own_fluxes(conserved):
    fields, depth, y, width = conserved.shape
    total = fields * depth
    tall = array((total, y + 2 * PAD, width))
    return pl.pallas_call(
        flux_kernel,
        out_shape=[array((total, y, width)), tall, tall, array((2 * width, 2 * width), jnp.bfloat16)],
        in_specs=[vmem()],
        out_specs=[vmem()] * 4,
        compiler_params=kernel_params(),
        cost_estimate=pl.CostEstimate(flops=40 * total * y * width, bytes_accessed=16 * total * y * width, transcendentals=0),
    )(conserved)


def edge_kernel(conserved, left, right, first_y, last_y, columns):
    fields, depth, y, width = conserved.shape
    total, quarter = fields * depth, y // 4
    for side, column in enumerate((left, right)):
        for c in range(4):
            value = column[0:quarter, :]
            value = pltpu.roll(value, LANES - 32 * c, 1) if c else value
            columns[side, c * quarter : (c + 1) * quarter, :] = value
        place = 4 * total + 4 * side
        first_y[place : place + 4, :] = columns[side, 0:4, :]
        last_y[place : place + 4, :] = columns[side, y - 4 : y, :]
    for j in range(total):
        first_y[4 * j : 4 * j + 4, :] = conserved[j // depth, j % depth, 0:4, :]
        last_y[4 * j : 4 * j + 4, :] = conserved[j // depth, j % depth, y - 4 : y, :]


def edge_rows(conserved, left, right):
    fields, depth, y, width = conserved.shape
    message = array((4 * fields * depth + COLUMN_ROWS, width))
    return pl.pallas_call(
        edge_kernel,
        out_shape=[message, message, array((2, y, width))],
        in_specs=[vmem()] * 3,
        out_specs=[vmem()] * 3,
        compiler_params=kernel_params(),
    )(conserved, left, right)


def brick_kernel(count, *refs):
    inside, down, up, columns, matrix = refs[:5]
    outs, refs = refs[5 : 5 + count], refs[5 + count :]
    blocks, rim_a, rim_d, rim_u, across, edges, split, coefficients, staged = refs
    total, y, width = inside.shape
    depth = total // FIELDS
    nb = y // 4
    rows = y // count

    for side in range(2):
        for f, value in enumerate(column_terms(columns[side], depth, COURANT if side == 0 else -COURANT)):
            edges[side, f] = value

    step = 24
    for start in range(0, y, step):
        for f in range(FIELDS):
            low, high = edges[0, f, start : start + step, :], edges[1, f, start : start + step, :]
            for z in range(depth):
                j = f * depth + z
                value = inside[j, start : start + step, :] + beside(low, high, z)
                across[j, PAD + start : PAD + start + step, :] = value
    for j in range(total):
        for source, rim in ((across, rim_a), (down, rim_d), (up, rim_u)):
            rim[j, 0:8, :] = source[j, PAD : PAD + 8, :]
            rim[j, 8:16, :] = source[j, y : y + 8, :]

    for f in range(FIELDS):
        rows_of = [fold_rows(across, down, up, f * depth + z, PAD, nb, 4) for z in range(4)]
        mixed = [butterfly(*[rows_of[z][m] for z in range(4)]) for m in range(4)]
        for k in range(4):
            high, low = halves(jnp.concatenate([mixed[m][k] for m in range(4)], axis=0))
            split[f, k * y : (k + 1) * y, 0:width] = high
            split[f, k * y : (k + 1) * y, width : 2 * width] = low
        product = jnp.dot(split[f], matrix[...], preferred_element_type=jnp.float32)
        result = product[:, 0:width] + product[:, width : 2 * width]
        peak = None
        for k in range(4):
            for m in range(4):
                value = result[k * y + m * nb : k * y + (m + 1) * nb]
                coefficients[f * depth + k, pl.ds(m, nb, stride=4), :] = value
                size = jnp.abs(value)
                peak = size if peak is None else jnp.maximum(peak, size)
        blocks[f] = over_lanes(peak)

    me = lax.axis_index("section")
    if rows % 8 == 0:
        for k in range(count):
            p = partner_of(me, k, count)
            for j in range(total):
                outs[k][j // depth, j % depth] = coefficients[j, pl.ds(pl.multiple_of(p * rows, 8), rows), :]
    else:
        for p in range(count):
            staged[p] = coefficients[:, p * rows : (p + 1) * rows, :]
        for k in range(count):
            p = partner_of(me, k, count)
            for j in range(total):
                outs[k][j // depth, j % depth] = staged[p, j]


def transform_bricks(count, inside, down, up, columns, matrix):
    total, y, width = inside.shape
    depth = total // FIELDS
    rows, tall = y // count, y + 2 * PAD
    chunk = array((FIELDS, depth, rows, width))
    rim = array((total, 2 * PAD, width))
    results = pl.pallas_call(
        functools.partial(brick_kernel, count),
        out_shape=[chunk] * count + [array((FIELDS, y // 4, width))] + [rim] * 3,
        in_specs=[vmem()] * 5,
        out_specs=[vmem()] * (count + 4),
        scratch_shapes=[
            pltpu.VMEM((total, tall, width), jnp.float32),
            pltpu.VMEM((2, FIELDS, y, width), jnp.float32),
            pltpu.VMEM((FIELDS, depth * y, 2 * width), jnp.bfloat16),
            pltpu.VMEM((total, y, width), jnp.float32),
            pltpu.VMEM((1, 1, 8, LANES) if rows % 8 == 0 else (count, total, rows, width), jnp.float32),
        ],
        compiler_params=kernel_params(),
        cost_estimate=pl.CostEstimate(flops=80 * total * y * width, bytes_accessed=16 * total * y * width, transcendentals=0),
    )(inside, down, up, columns, matrix)
    return results[:count], results[count], results[count + 1 :]


def leaving_order(count):
    return [*range(2, count), 1, 0]


def mend_kernel(count, *refs):
    chunks, refs = refs[:count], refs[count:]
    top, bottom, blocks, rim_a, rim_d, rim_u, matrix = refs[:7]
    outs, mended, refs = refs[7 : 7 + count], refs[7 + count], refs[8 + count :]
    halo, columns, across, down, up, folded, split, result, fixed = refs
    fields, depth, rows, width = chunks[0].shape
    total = fields * depth
    nb = blocks.shape[1]

    halo[...] = jnp.ones(halo.shape, jnp.float32)
    columns[...] = jnp.ones(columns.shape, jnp.float32)
    for j in range(total):
        halo[j, 4:8, :] = top[4 * j : 4 * j + 4, :]
        halo[j, 8:12, :] = bottom[4 * j : 4 * j + 4, :]
    for side in range(2):
        place = 4 * total + 4 * side
        columns[side, 4:8, :] = top[place : place + 4, :]
        columns[side, 8:12, :] = bottom[place : place + 4, :]
    low = column_terms(columns[0], depth, COURANT)
    high = column_terms(columns[1], depth, -COURANT)
    for z in range(depth):
        c = [halo[f * depth + z] for f in range(fields)]
        for f, (a, d, u) in enumerate(row_terms(c)):
            j = f * depth + z
            values = (a + beside(low[f], high[f], z), d, u)
            for value, rim, target in zip(values, (rim_a, rim_d, rim_u), (across, down, up)):
                target[j, 0:8, :] = value[0:8]
                target[j, 8:24, :] = rim[j]
                target[j, 24:32, :] = value[8:16]
    for j in range(total):
        for k, value in enumerate(fold_rows(across, down, up, j, PAD, 2, 12)):
            folded[j, 2 * k : 2 * k + 2, :] = value
    for f in range(fields):
        values = butterfly(*[folded[f * depth + z] for z in range(4)])
        for half in range(2):
            both = jnp.concatenate(values[2 * half : 2 * half + 2], axis=0)
            upper, lower = halves(both)
            place = f * 32 + half * 16
            split[place : place + 16, 0:width] = upper
            split[place : place + 16, width : 2 * width] = lower
    product = jnp.dot(split[...], matrix[...], preferred_element_type=jnp.float32)
    result[...] = product[:, 0:width] + product[:, width : 2 * width]
    for j in range(total):
        for side in range(2):
            fixed[side, j] = result[pl.ds(8 * j + side, 4, stride=2), :]
    mended[...] = blocks[...]
    for f in range(fields):
        for side in range(2):
            size = jnp.abs(fixed[side, f * depth])
            for z in range(1, depth):
                size = jnp.maximum(size, jnp.abs(fixed[side, f * depth + z]))
            peak = over_lanes(jnp.max(size, axis=0, keepdims=True))
            row = side * (nb - 1)
            mended[f, row : row + 1, :] = peak

    me = lax.axis_index("section")
    for i, k in enumerate(leaving_order(count)):
        p = partner_of(me, k, count)
        for side, start in ((0, 0), (1, rows - 4)):

            @pl.when(p == side * (count - 1))
            def replace(i=i, side=side, start=start):
                for j in range(total):
                    outs[i][j // depth, j % depth, start : start + 4, :] = fixed[side, j]


def mend(count, chunks, top, bottom, blocks, rims, matrix):
    fields, depth, rows, width = chunks[0].shape
    total = fields * depth
    tall = pltpu.VMEM((total, 4 * PAD, width), jnp.float32)
    results = pl.pallas_call(
        functools.partial(mend_kernel, count),
        out_shape=[array(chunks[0].shape)] * count + [array(blocks.shape)],
        in_specs=[vmem()] * (count + 7),
        out_specs=[vmem()] * (count + 1),
        input_output_aliases={k: k for k in range(count)},
        scratch_shapes=[
            pltpu.VMEM((total, 2 * PAD, width), jnp.float32),
            pltpu.VMEM((2, 2 * PAD, width), jnp.float32),
            tall,
            tall,
            tall,
            pltpu.VMEM((total, 8, width), jnp.float32),
            pltpu.VMEM((8 * total, 2 * width), jnp.bfloat16),
            pltpu.VMEM((8 * total, width), jnp.float32),
            pltpu.VMEM((2, total, 4, width), jnp.float32),
        ],
        compiler_params=kernel_params(),
    )(*[chunks[k] for k in leaving_order(count)], top, bottom, blocks, *rims, matrix)
    return dict(zip(leaving_order(count), results)), results[count]


def group_kernel(count, groups, own_rows, *refs):
    blocks, refs = refs[0], refs[1:]
    messages, (peaks, gathered, listed, packed, table) = refs[:count], refs[count:]
    nb = blocks.shape[1]
    me = lax.axis_index("section")
    slot = slot_of(messages[0], me)
    within = lax.rem(slot, 4) * 32
    tile = lax.div(slot, 4)
    for d, message in enumerate(messages):
        height = gathered.shape[1]
        value = message[message.shape[0] - height :, :]
        if count > 4:
            value = pltpu.roll(value, lax.rem(height - tile * own_rows, height), 0)
        gathered[lax.rem(me + count - d, count)] = value
    for q in range(count):
        listed[q * own_rows : (q + 1) * own_rows, :] = gathered[q, 0:own_rows, :]
    part = nb // 4
    band = lax.div(lanes_of((part, LANES)), 32)
    labels = jnp.zeros((part, LANES), jnp.float32)
    for c in range(4):
        turned = pltpu.roll(listed[c * part : (c + 1) * part, :], lax.rem(32 * c - within + LANES, LANES), 1)
        labels = jnp.where(band == c, turned, labels)
    for f in range(FIELDS):
        own = jnp.zeros((part, LANES), jnp.float32)
        for c in range(4):
            own = jnp.where(band == c, blocks[f, c * part : (c + 1) * part, :], own)
        packed[f, 0:part, :] = own
    lane8 = lanes_of((8, LANES))
    sub8 = lax.broadcasted_iota(jnp.int32, (8, LANES), 0)
    label_rows = [jnp.broadcast_to(labels[r : r + 1], (8, LANES)) for r in range(part)]

    def group_tile(g, carry):
        wanted = (sub8 + g * 8).astype(jnp.float32)
        matches = [label_rows[r] == wanted for r in range(part)]
        found = jnp.zeros((8, LANES), jnp.float32)
        for f in range(FIELDS):
            best = jnp.zeros((8, LANES), jnp.float32)
            for r in range(part):
                row = jnp.broadcast_to(packed[f, r : r + 1, :], (8, LANES))
                best = jnp.maximum(best, jnp.where(matches[r], row, 0.0))
            found = jnp.where(lane8 == f, jnp.max(best, axis=1, keepdims=True), found)
        table[pl.ds(pl.multiple_of(g * 8, 8), 8), :] = found
        return carry

    high = table.shape[0]
    if groups < high:
        table[...] = jnp.zeros((high, LANES), jnp.float32)
    lax.fori_loop(0, pl.cdiv(groups, 8), group_tile, 0)
    for g in range(high // LANES):
        peaks[:, g * LANES : (g + 1) * LANES] = jnp.transpose(table[g * LANES : (g + 1) * LANES, :])[0:8]


def group_maxima(count, groups, own_rows, blocks, messages):
    high = pl.cdiv(groups, LANES) * LANES
    nb = blocks.shape[1]
    return pl.pallas_call(
        functools.partial(group_kernel, count, groups, own_rows),
        out_shape=array((8, high)),
        in_specs=[vmem()] * (count + 1),
        out_specs=vmem(),
        scratch_shapes=[
            pltpu.VMEM((count, messages[0].shape[0], LANES), jnp.float32),
            pltpu.VMEM((nb, LANES), jnp.float32),
            pltpu.VMEM((FIELDS, 8, LANES), jnp.float32),
            pltpu.VMEM((high, LANES), jnp.float32),
        ],
        compiler_params=kernel_params(),
    )(blocks, *messages)


def scale_kernel(count, groups, *refs):
    chunks, refs = refs[:count], refs[count:]
    peaks, labels, coded, group_peak, wide = refs
    fields, depth, rows, width = chunks[0].shape
    nb = rows // 4
    high = peaks.shape[1]
    me = lax.axis_index("section")
    group_peak[...] = peaks[0:fields, 0:groups]
    own_labels = labels[...].astype(jnp.int32)
    lane = lanes_of((8, LANES))
    inverse = 1.0 / (peaks[...] + EPSILON)
    tables = [
        [jnp.broadcast_to(inverse[f : f + 1, g * LANES : (g + 1) * LANES], (8, LANES)) for g in range(high // LANES)]
        for f in range(fields)
    ]
    for i, k in enumerate(leaving_order(count)):
        slot = slot_of(labels, sender_of(me, k, count))
        tile = own_labels
        if count > 4:
            tile = pltpu.roll(tile, lax.rem(LABEL_ROWS - lax.div(slot, 4) * nb, LABEL_ROWS), 0)
        within = lax.rem(slot, 4) * 32 + lax.rem(lane, 32)
        own = jnp.take_along_axis(tile, within, axis=1)
        place = pl.ds(pl.multiple_of(slot * width, width), width)
        for f in range(fields):
            if high == LANES:
                found = jnp.take_along_axis(tables[f][0], own, axis=1)
            else:
                found = jnp.zeros((8, LANES), jnp.float32)
                inside = lax.rem(own, LANES)
                for g in range(high // LANES):
                    here = jnp.take_along_axis(tables[f][g], inside, axis=1)
                    found = jnp.where(lax.div(own, LANES) == g, here, found)
            for m in range(4):
                wide[i, f, pl.ds(m, nb, stride=4), :] = found[0:nb]
            factor = wide[i, f]
            for z in range(depth):
                coded[f, z, :, place] = chunks[i][f, z] * factor


def scale(count, groups, chunks, peaks, labels):
    fields, depth, rows, width = chunks[0].shape
    return pl.pallas_call(
        functools.partial(scale_kernel, count, groups),
        out_shape=[array((fields, depth, rows, width * count)), array((fields, groups))],
        in_specs=[vmem()] * (count + 2),
        out_specs=[vmem()] * 2,
        scratch_shapes=[
            pltpu.VMEM((count, fields, rows, width), jnp.float32),
        ],
        compiler_params=kernel_params(),
    )(*chunks, peaks, labels)


def ring(axis, shift):
    count = lax.axis_size(axis)
    return [(i, (i + shift) % count) for i in range(count)]


def exchange_pairs(count, k):
    if count & (count - 1) == 0:
        return [(i, i ^ k) for i in range(count)]
    return [(i, (i + k) % count) for i in range(count)]


def steps_over(axis):
    count = lax.axis_size(axis)
    span, shifts = 1, []
    while span < count:
        shifts.append(min(span, count - span))
        span += shifts[-1]
    return shifts


def with_others(value, axis, shifts):
    count = lax.axis_size(axis)
    others = [lax.ppermute(value, axis, exchange_pairs(count, k)) for k in shifts]
    return functools.reduce(jnp.maximum, others, value)


def per_device(density, momentum, energy, membership, slot_of_brick):
    count = lax.axis_size("section")
    groups = 2 * lax.axis_size("sim") * count
    conserved = jnp.concatenate([density[None], momentum, energy[None]], axis=0)
    first_x, last_x, labels = pack(conserved, membership, slot_of_brick)
    left = lax.ppermute(last_x, "section", ring("section", 1))
    right = lax.ppermute(first_x, "section", ring("section", -1))
    far = [lax.ppermute(labels, "section", ring("section", d)) for d in range(2, count - 1)]
    inside, down, up, matrix = own_fluxes(conserved)
    left, right, inside = lax.optimization_barrier((left, right, inside))
    first_y, last_y, columns = edge_rows(conserved, left, right)
    top = lax.ppermute(last_y, "sim", ring("sim", 1))
    bottom = lax.ppermute(first_y, "sim", ring("sim", -1))
    chunks, blocks, rims = transform_bricks(count, inside, down, up, columns, matrix)
    chunks, blocks = mend(count, chunks, top, bottom, blocks, rims, matrix)
    moved = {0: chunks[0]}
    second = leaving_order(count)[min(1, count - 2)]
    chunks[second], *far = lax.optimization_barrier((chunks[second], *far))
    for k in leaving_order(count)[:-1]:
        moved[k] = lax.ppermute(chunks[k], "section", exchange_pairs(count, k))
    peaks = group_maxima(count, groups, membership.shape[0], blocks, [labels, left, *far, right])
    for shift in steps_over("sim"):
        peaks = with_others(peaks, "sim", [shift])
    for shift in steps_over("section"):
        peaks = with_others(peaks, "section", [shift])
    return tuple(scale(count, groups, [moved[k] for k in leaving_order(count)], peaks, labels))


def solution(mesh):
    placed = (
        P(None, "sim", "section"),
        P(None, None, "sim", "section"),
        P(None, "sim", "section"),
        P(("sim", "section"), None),
        P("sim", None),
    )
    return jax.shard_map(
        per_device,
        mesh=mesh,
        in_specs=placed,
        out_specs=(P(None, None, ("sim", "section"), None), P()),
        check_vma=False,
    )
```

```python
import functools

import jax
import jax.numpy as jnp
import numpy as np
from jax import lax
from jax.experimental import pallas as pl
from jax.experimental.pallas import tpu as pltpu
from jax.sharding import PartitionSpec as P

GAMMA_LESS = 0.4
COURANT = 0.05
DIFFUSE = 0.1
EPSILON = 1e-06
FIELDS = 5
PAD = 8
COLUMN_ROWS = 8
LABEL_ROWS = 8
LANES = 128
EVEN = 0.5
WIDE = float(np.sqrt(0.5) * np.cos(np.pi / 8))
NARROW = float(np.sqrt(0.5) * np.cos(3 * np.pi / 8))
VMEM_LIMIT = 48 * 1024 * 1024


def vmem():
    return pl.BlockSpec(memory_space=pltpu.VMEM)


def lanes_of(shape):
    return lax.broadcasted_iota(jnp.int32, shape, 1)


def butterfly(a, b, c, d):
    s, t, u, v = a + d, b + c, a - d, b - c
    return (
        EVEN * (s + t),
        WIDE * u + NARROW * v,
        EVEN * (s - t),
        NARROW * u - WIDE * v,
    )


def cosine(k, d):
    factor = 0.5 if k == 0 else np.sqrt(0.5)
    return float(factor * np.cos(np.pi * (2 * d + 1) * k / 8))


def write_matrix(matrix, width):
    step = 16
    row = lax.broadcasted_iota(jnp.int32, (step, width), 0)
    column = lanes_of((step, width))
    quarter = width // 4
    k, j, d = lax.div(column, quarter), lax.rem(column, quarter), lax.rem(row, 4)
    entry = jnp.zeros((step, width), jnp.float32)
    for a in range(4):
        for b in range(4):
            entry = jnp.where(jnp.logical_and(k == a, d == b), cosine(a, b), entry)
    high = entry.astype(jnp.bfloat16).astype(jnp.float32)
    low = entry - high
    zero = jnp.zeros((step, width), jnp.bfloat16)
    for start in range(0, width, step):
        own = j == lax.div(row + start, 4)
        upper = jnp.where(own, high, 0.0).astype(jnp.bfloat16)
        lower = jnp.where(own, low, 0.0).astype(jnp.bfloat16)
        matrix[start : start + step, 0:width] = upper
        matrix[start : start + step, width : 2 * width] = lower
        matrix[width + start : width + start + step, 0:width] = upper
        matrix[width + start : width + start + step, width : 2 * width] = zero


def kernel_params():
    return pltpu.CompilerParams(vmem_limit_bytes=VMEM_LIMIT)


def array(shape, dtype=jnp.float32):
    return jax.ShapeDtypeStruct(shape, dtype)


def pack_kernel(conserved, membership, slots, first_x, last_x, labels):
    fields, depth, y, width = conserved.shape
    quarter = y // 4
    lane = lanes_of((y, width))
    first = jnp.zeros((y, width), jnp.float32)
    last = jnp.zeros((y, width), jnp.float32)
    for j in range(fields * depth):
        value = conserved[j // depth, j % depth]
        first = jnp.where(lane == j, pltpu.roll(value, j, 1) if j else value, first)
        last = jnp.where(lane == j, pltpu.roll(value, j + 1, 1), last)
    rows, columns = membership.shape
    labels[...] = jnp.zeros(labels.shape, jnp.float32)
    for t in range(columns // LANES):
        part = membership[:, t * LANES : (t + 1) * LANES].astype(jnp.float32)
        labels[t * rows : (t + 1) * rows, :] = part
    labels[LABEL_ROWS - 1 : LABEL_ROWS, 0 : slots.shape[1]] = slots[...].astype(jnp.float32)
    own = labels[...]
    for column, out in ((first, first_x), (last, last_x)):
        packed = column[0:quarter]
        for c in range(1, 4):
            packed = packed + pltpu.roll(column[c * quarter : (c + 1) * quarter], 32 * c, 1)
        out[0:quarter, :] = packed
        out[quarter:, :] = own


def pack(conserved, membership, slots):
    y, width = conserved.shape[2:]
    shapes = [
        array((y // 4 + LABEL_ROWS, width)),
        array((y // 4 + LABEL_ROWS, width)),
        array((LABEL_ROWS, width)),
    ]
    return pl.pallas_call(
        pack_kernel,
        out_shape=shapes,
        in_specs=[vmem()] * 3,
        out_specs=[vmem()] * 3,
        compiler_params=kernel_params(),
    )(conserved, membership, slots)


def slot_of(labels, brick):
    row = labels[LABEL_ROWS - 1 : LABEL_ROWS, :]
    return jnp.max(jnp.where(lanes_of(row.shape) == brick, row, 0.0)).astype(jnp.int32)


def fluxes(c):
    rho, mx, my, mz, e = c
    inverse = 1.0 / rho
    u, v = mx * inverse, my * inverse
    pressure = GAMMA_LESS * (e - 0.5 * (mx * mx + my * my + mz * mz) * inverse)
    total = e + pressure
    flux_x = (mx, mx * u + pressure, my * u, mz * u, total * u)
    flux_y = (my, mx * v, my * v + pressure, mz * v, total * v)
    return flux_x, flux_y


def column_terms(own, depth, sign):
    fields = [pltpu.roll(own, LANES - depth * f, 1) if f else own for f in range(FIELDS)]
    flux_x, unused = fluxes(fields)
    return [DIFFUSE * fields[f] + sign * flux_x[f] for f in range(FIELDS)]


def row_terms(c):
    rows, width = c[0].shape
    lane = lanes_of((rows, width))
    flux_x, flux_y = fluxes(c)
    terms = []
    for f in range(FIELDS):
        base = DIFFUSE * c[f]
        gx, gy = COURANT * flux_x[f], COURANT * flux_y[f]
        from_left = jnp.where(lane == 0, 0.0, pltpu.roll(base + gx, 1, 1))
        from_right = jnp.where(lane == width - 1, 0.0, pltpu.roll(base - gx, width - 1, 1))
        terms.append(((1.0 - 4.0 * DIFFUSE) * c[f] + from_left + from_right, base + gy, base - gy))
    return terms


def beside(low, high, z):
    rows, width = low.shape
    lane = lanes_of((rows, width))
    at_left = pltpu.roll(low, LANES - z, 1) if z else low
    at_right = pltpu.roll(high, LANES - 1 - z, 1)
    return jnp.where(lane == 0, at_left, jnp.where(lane == width - 1, at_right, 0.0))


def fold_rows(across, down, up, j, origin, number, stride):
    t = {}
    for o in range(-3, 7):
        t[o] = (
            across[j, pl.ds(origin + o, number, stride=stride), :]
            + down[j, pl.ds(origin + o - 1, number, stride=stride), :]
            + up[j, pl.ds(origin + o + 1, number, stride=stride), :]
        )
    residual = [
        t[m] - (9.0 / 16.0) * (t[m - 1] + t[m + 1]) + (1.0 / 16.0) * (t[m - 3] + t[m + 3])
        for m in range(4)
    ]
    return butterfly(*residual)


def halves(value):
    high = value.astype(jnp.bfloat16)
    return high, (value - high.astype(jnp.float32)).astype(jnp.bfloat16)


def over_lanes(peak):
    peak = jnp.maximum(peak, pltpu.roll(peak, 64, 1))
    return jnp.maximum(peak, pltpu.roll(peak, 32, 1))


def partner_of(me, k, count):
    if count & (count - 1) == 0:
        return me ^ k
    return lax.rem(me + k, count)


def sender_of(me, k, count):
    if count & (count - 1) == 0:
        return me ^ k
    return lax.rem(me - k + count, count)


def flux_kernel(conserved, across, down, up, matrix):
    fields, depth, y, width = conserved.shape
    write_matrix(matrix, width)
    step = 16

    def flux_rows(i, carry):
        r = pl.ds(pl.multiple_of(i * step, step), step)
        padded = pl.ds(pl.multiple_of(i * step + PAD, PAD), step)
        for z in range(depth):
            for f, (a, d, u) in enumerate(row_terms([conserved[f, z, r, :] for f in range(fields)])):
                j = f * depth + z
                across[j, r, :] = a
                down[j, padded, :] = d
                up[j, padded, :] = u
        return carry

    lax.fori_loop(0, y // step, flux_rows, 0)


def own_fluxes(conserved):
    fields, depth, y, width = conserved.shape
    total = fields * depth
    tall = array((total, y + 2 * PAD, width))
    return pl.pallas_call(
        flux_kernel,
        out_shape=[array((total, y, width)), tall, tall, array((2 * width, 2 * width), jnp.bfloat16)],
        in_specs=[vmem()],
        out_specs=[vmem()] * 4,
        compiler_params=kernel_params(),
        cost_estimate=pl.CostEstimate(flops=40 * total * y * width, bytes_accessed=16 * total * y * width, transcendentals=0),
    )(conserved)


def edge_kernel(conserved, left, right, first_y, last_y, columns):
    fields, depth, y, width = conserved.shape
    total, quarter = fields * depth, y // 4
    for side, column in enumerate((left, right)):
        for c in range(4):
            value = column[0:quarter, :]
            value = pltpu.roll(value, LANES - 32 * c, 1) if c else value
            columns[side, c * quarter : (c + 1) * quarter, :] = value
        place = 4 * total + 4 * side
        first_y[place : place + 4, :] = columns[side, 0:4, :]
        last_y[place : place + 4, :] = columns[side, y - 4 : y, :]
    for j in range(total):
        first_y[4 * j : 4 * j + 4, :] = conserved[j // depth, j % depth, 0:4, :]
        last_y[4 * j : 4 * j + 4, :] = conserved[j // depth, j % depth, y - 4 : y, :]


def edge_rows(conserved, left, right):
    fields, depth, y, width = conserved.shape
    message = array((4 * fields * depth + COLUMN_ROWS, width))
    return pl.pallas_call(
        edge_kernel,
        out_shape=[message, message, array((2, y, width))],
        in_specs=[vmem()] * 3,
        out_specs=[vmem()] * 3,
        compiler_params=kernel_params(),
    )(conserved, left, right)


def brick_kernel(count, *refs):
    inside, down, up, columns, matrix = refs[:5]
    outs, refs = refs[5 : 5 + count], refs[5 + count :]
    blocks, rim_a, rim_d, rim_u, across, edges, split, coefficients, staged = refs
    total, y, width = inside.shape
    depth = total // FIELDS
    nb = y // 4
    rows = y // count

    for side in range(2):
        for f, value in enumerate(column_terms(columns[side], depth, COURANT if side == 0 else -COURANT)):
            edges[side, f] = value

    step = 24
    for start in range(0, y, step):
        for f in range(FIELDS):
            low, high = edges[0, f, start : start + step, :], edges[1, f, start : start + step, :]
            for z in range(depth):
                j = f * depth + z
                value = inside[j, start : start + step, :] + beside(low, high, z)
                across[j, PAD + start : PAD + start + step, :] = value
    for j in range(total):
        for source, rim in ((across, rim_a), (down, rim_d), (up, rim_u)):
            rim[j, 0:8, :] = source[j, PAD : PAD + 8, :]
            rim[j, 8:16, :] = source[j, y : y + 8, :]

    for f in range(FIELDS):
        rows_of = [fold_rows(across, down, up, f * depth + z, PAD, nb, 4) for z in range(4)]
        mixed = [butterfly(*[rows_of[z][m] for z in range(4)]) for m in range(4)]
        for k in range(4):
            high, low = halves(jnp.concatenate([mixed[m][k] for m in range(4)], axis=0))
            split[f, k * y : (k + 1) * y, 0:width] = high
            split[f, k * y : (k + 1) * y, width : 2 * width] = low
        product = jnp.dot(split[f], matrix[...], preferred_element_type=jnp.float32)
        result = product[:, 0:width] + product[:, width : 2 * width]
        peak = None
        for k in range(4):
            for m in range(4):
                value = result[k * y + m * nb : k * y + (m + 1) * nb]
                coefficients[f * depth + k, pl.ds(m, nb, stride=4), :] = value
                size = jnp.abs(value)
                peak = size if peak is None else jnp.maximum(peak, size)
        blocks[f] = over_lanes(peak)

    me = lax.axis_index("section")
    if rows % 8 == 0:
        for k in range(count):
            p = partner_of(me, k, count)
            for j in range(total):
                outs[k][j // depth, j % depth] = coefficients[j, pl.ds(pl.multiple_of(p * rows, 8), rows), :]
    else:
        for p in range(count):
            staged[p] = coefficients[:, p * rows : (p + 1) * rows, :]
        for k in range(count):
            p = partner_of(me, k, count)
            for j in range(total):
                outs[k][j // depth, j % depth] = staged[p, j]


def transform_bricks(count, inside, down, up, columns, matrix):
    total, y, width = inside.shape
    depth = total // FIELDS
    rows, tall = y // count, y + 2 * PAD
    chunk = array((FIELDS, depth, rows, width))
    rim = array((total, 2 * PAD, width))
    results = pl.pallas_call(
        functools.partial(brick_kernel, count),
        out_shape=[chunk] * count + [array((FIELDS, y // 4, width))] + [rim] * 3,
        in_specs=[vmem()] * 5,
        out_specs=[vmem()] * (count + 4),
        scratch_shapes=[
            pltpu.VMEM((total, tall, width), jnp.float32),
            pltpu.VMEM((2, FIELDS, y, width), jnp.float32),
            pltpu.VMEM((FIELDS, depth * y, 2 * width), jnp.bfloat16),
            pltpu.VMEM((total, y, width), jnp.float32),
            pltpu.VMEM((1, 1, 8, LANES) if rows % 8 == 0 else (count, total, rows, width), jnp.float32),
        ],
        compiler_params=kernel_params(),
        cost_estimate=pl.CostEstimate(flops=80 * total * y * width, bytes_accessed=16 * total * y * width, transcendentals=0),
    )(inside, down, up, columns, matrix)
    return results[:count], results[count], results[count + 1 :]


def leaving_order(count):
    return [*range(2, count), 1, 0]


def mend_kernel(count, *refs):
    chunks, refs = refs[:count], refs[count:]
    top, bottom, blocks, rim_a, rim_d, rim_u, matrix = refs[:7]
    outs, mended, refs = refs[7 : 7 + count], refs[7 + count], refs[8 + count :]
    halo, columns, across, down, up, folded, split, result, fixed = refs
    fields, depth, rows, width = chunks[0].shape
    total = fields * depth
    nb = blocks.shape[1]

    halo[...] = jnp.ones(halo.shape, jnp.float32)
    columns[...] = jnp.ones(columns.shape, jnp.float32)
    for j in range(total):
        halo[j, 4:8, :] = top[4 * j : 4 * j + 4, :]
        halo[j, 8:12, :] = bottom[4 * j : 4 * j + 4, :]
    for side in range(2):
        place = 4 * total + 4 * side
        columns[side, 4:8, :] = top[place : place + 4, :]
        columns[side, 8:12, :] = bottom[place : place + 4, :]
    low = column_terms(columns[0], depth, COURANT)
    high = column_terms(columns[1], depth, -COURANT)
    for z in range(depth):
        c = [halo[f * depth + z] for f in range(fields)]
        for f, (a, d, u) in enumerate(row_terms(c)):
            j = f * depth + z
            values = (a + beside(low[f], high[f], z), d, u)
            for value, rim, target in zip(values, (rim_a, rim_d, rim_u), (across, down, up)):
                target[j, 0:8, :] = value[0:8]
                target[j, 8:24, :] = rim[j]
                target[j, 24:32, :] = value[8:16]
    for j in range(total):
        for k, value in enumerate(fold_rows(across, down, up, j, PAD, 2, 12)):
            folded[j, 2 * k : 2 * k + 2, :] = value
    for f in range(fields):
        values = butterfly(*[folded[f * depth + z] for z in range(4)])
        for half in range(2):
            both = jnp.concatenate(values[2 * half : 2 * half + 2], axis=0)
            upper, lower = halves(both)
            place = f * 32 + half * 16
            split[place : place + 16, 0:width] = upper
            split[place : place + 16, width : 2 * width] = lower
    product = jnp.dot(split[...], matrix[...], preferred_element_type=jnp.float32)
    result[...] = product[:, 0:width] + product[:, width : 2 * width]
    for j in range(total):
        for side in range(2):
            fixed[side, j] = result[pl.ds(8 * j + side, 4, stride=2), :]
    mended[...] = blocks[...]
    for f in range(fields):
        for side in range(2):
            size = jnp.abs(fixed[side, f * depth])
            for z in range(1, depth):
                size = jnp.maximum(size, jnp.abs(fixed[side, f * depth + z]))
            peak = over_lanes(jnp.max(size, axis=0, keepdims=True))
            row = side * (nb - 1)
            mended[f, row : row + 1, :] = peak

    me = lax.axis_index("section")
    for i, k in enumerate(leaving_order(count)):
        p = partner_of(me, k, count)
        for side, start in ((0, 0), (1, rows - 4)):

            @pl.when(p == side * (count - 1))
            def replace(i=i, side=side, start=start):
                for j in range(total):
                    outs[i][j // depth, j % depth, start : start + 4, :] = fixed[side, j]


def mend(count, chunks, top, bottom, blocks, rims, matrix):
    fields, depth, rows, width = chunks[0].shape
    total = fields * depth
    tall = pltpu.VMEM((total, 4 * PAD, width), jnp.float32)
    results = pl.pallas_call(
        functools.partial(mend_kernel, count),
        out_shape=[array(chunks[0].shape)] * count + [array(blocks.shape)],
        in_specs=[vmem()] * (count + 7),
        out_specs=[vmem()] * (count + 1),
        input_output_aliases={k: k for k in range(count)},
        scratch_shapes=[
            pltpu.VMEM((total, 2 * PAD, width), jnp.float32),
            pltpu.VMEM((2, 2 * PAD, width), jnp.float32),
            tall,
            tall,
            tall,
            pltpu.VMEM((total, 8, width), jnp.float32),
            pltpu.VMEM((8 * total, 2 * width), jnp.bfloat16),
            pltpu.VMEM((8 * total, width), jnp.float32),
            pltpu.VMEM((2, total, 4, width), jnp.float32),
        ],
        compiler_params=kernel_params(),
    )(*[chunks[k] for k in leaving_order(count)], top, bottom, blocks, *rims, matrix)
    return dict(zip(leaving_order(count), results)), results[count]


def group_kernel(count, groups, own_rows, *refs):
    blocks, refs = refs[0], refs[1:]
    messages, (peaks, gathered, listed, packed, table) = refs[:count], refs[count:]
    nb = blocks.shape[1]
    me = lax.axis_index("section")
    slot = slot_of(messages[0], me)
    within = lax.rem(slot, 4) * 32
    tile = lax.div(slot, 4)
    for d, message in enumerate(messages):
        height = gathered.shape[1]
        value = message[message.shape[0] - height :, :]
        if count > 4:
            value = pltpu.roll(value, lax.rem(height - tile * own_rows, height), 0)
        gathered[lax.rem(me + count - d, count)] = value
    for q in range(count):
        listed[q * own_rows : (q + 1) * own_rows, :] = gathered[q, 0:own_rows, :]
    part = nb // 4
    band = lax.div(lanes_of((part, LANES)), 32)
    labels = jnp.zeros((part, LANES), jnp.float32)
    for c in range(4):
        turned = pltpu.roll(listed[c * part : (c + 1) * part, :], lax.rem(32 * c - within + LANES, LANES), 1)
        labels = jnp.where(band == c, turned, labels)
    for f in range(FIELDS):
        own = jnp.zeros((part, LANES), jnp.float32)
        for c in range(4):
            own = jnp.where(band == c, blocks[f, c * part : (c + 1) * part, :], own)
        packed[f, 0:part, :] = own
    lane8 = lanes_of((8, LANES))
    sub8 = lax.broadcasted_iota(jnp.int32, (8, LANES), 0)
    label_rows = [jnp.broadcast_to(labels[r : r + 1], (8, LANES)) for r in range(part)]

    def group_tile(g, carry):
        wanted = (sub8 + g * 8).astype(jnp.float32)
        matches = [label_rows[r] == wanted for r in range(part)]
        found = jnp.zeros((8, LANES), jnp.float32)
        for f in range(FIELDS):
            best = jnp.zeros((8, LANES), jnp.float32)
            for r in range(part):
                row = jnp.broadcast_to(packed[f, r : r + 1, :], (8, LANES))
                best = jnp.maximum(best, jnp.where(matches[r], row, 0.0))
            found = jnp.where(lane8 == f, jnp.max(best, axis=1, keepdims=True), found)
        table[pl.ds(pl.multiple_of(g * 8, 8), 8), :] = found
        return carry

    high = table.shape[0]
    if groups < high:
        table[...] = jnp.zeros((high, LANES), jnp.float32)
    lax.fori_loop(0, pl.cdiv(groups, 8), group_tile, 0)
    for g in range(high // LANES):
        peaks[:, g * LANES : (g + 1) * LANES] = jnp.transpose(table[g * LANES : (g + 1) * LANES, :])[0:8]


def group_maxima(count, groups, own_rows, blocks, messages):
    high = pl.cdiv(groups, LANES) * LANES
    nb = blocks.shape[1]
    return pl.pallas_call(
        functools.partial(group_kernel, count, groups, own_rows),
        out_shape=array((8, high)),
        in_specs=[vmem()] * (count + 1),
        out_specs=vmem(),
        scratch_shapes=[
            pltpu.VMEM((count, messages[0].shape[0], LANES), jnp.float32),
            pltpu.VMEM((nb, LANES), jnp.float32),
            pltpu.VMEM((FIELDS, 8, LANES), jnp.float32),
            pltpu.VMEM((high, LANES), jnp.float32),
        ],
        compiler_params=kernel_params(),
    )(blocks, *messages)


def scale_kernel(count, groups, *refs):
    chunks, refs = refs[:count], refs[count:]
    peaks, labels, coded, group_peak, wide = refs
    fields, depth, rows, width = chunks[0].shape
    nb = rows // 4
    high = peaks.shape[1]
    me = lax.axis_index("section")
    group_peak[...] = peaks[0:fields, 0:groups]
    own_labels = labels[...].astype(jnp.int32)
    lane = lanes_of((8, LANES))
    inverse = 1.0 / (peaks[...] + EPSILON)
    tables = [
        [jnp.broadcast_to(inverse[f : f + 1, g * LANES : (g + 1) * LANES], (8, LANES)) for g in range(high // LANES)]
        for f in range(fields)
    ]
    for i, k in enumerate(leaving_order(count)):
        slot = slot_of(labels, sender_of(me, k, count))
        tile = own_labels
        if count > 4:
            tile = pltpu.roll(tile, lax.rem(LABEL_ROWS - lax.div(slot, 4) * nb, LABEL_ROWS), 0)
        within = lax.rem(slot, 4) * 32 + lax.rem(lane, 32)
        own = jnp.take_along_axis(tile, within, axis=1)
        place = pl.ds(pl.multiple_of(slot * width, width), width)
        for f in range(fields):
            if high == LANES:
                found = jnp.take_along_axis(tables[f][0], own, axis=1)
            else:
                found = jnp.zeros((8, LANES), jnp.float32)
                inside = lax.rem(own, LANES)
                for g in range(high // LANES):
                    here = jnp.take_along_axis(tables[f][g], inside, axis=1)
                    found = jnp.where(lax.div(own, LANES) == g, here, found)
            for m in range(4):
                wide[i, f, pl.ds(m, nb, stride=4), :] = found[0:nb]
            factor = wide[i, f]
            for z in range(depth):
                coded[f, z, :, place] = chunks[i][f, z] * factor


def scale(count, groups, chunks, peaks, labels):
    fields, depth, rows, width = chunks[0].shape
    return pl.pallas_call(
        functools.partial(scale_kernel, count, groups),
        out_shape=[array((fields, depth, rows, width * count)), array((fields, groups))],
        in_specs=[vmem()] * (count + 2),
        out_specs=[vmem()] * 2,
        scratch_shapes=[
            pltpu.VMEM((count, fields, rows, width), jnp.float32),
        ],
        compiler_params=kernel_params(),
    )(*chunks, peaks, labels)


def ring(axis, shift):
    count = lax.axis_size(axis)
    return [(i, (i + shift) % count) for i in range(count)]


def exchange_pairs(count, k):
    if count & (count - 1) == 0:
        return [(i, i ^ k) for i in range(count)]
    return [(i, (i + k) % count) for i in range(count)]


def steps_over(axis):
    count = lax.axis_size(axis)
    span, shifts = 1, []
    while span < count:
        shifts.append(min(span, count - span))
        span += shifts[-1]
    return shifts


def with_others(value, axis, shifts):
    count = lax.axis_size(axis)
    others = [lax.ppermute(value, axis, exchange_pairs(count, k)) for k in shifts]
    return functools.reduce(jnp.maximum, others, value)


def per_device(density, momentum, energy, membership, slot_of_brick):
    count = lax.axis_size("section")
    groups = 2 * lax.axis_size("sim") * count
    conserved = jnp.concatenate([density[None], momentum, energy[None]], axis=0)
    first_x, last_x, labels = pack(conserved, membership, slot_of_brick)
    left = lax.ppermute(last_x, "section", ring("section", 1))
    right = lax.ppermute(first_x, "section", ring("section", -1))
    far = [lax.ppermute(labels, "section", ring("section", d)) for d in range(2, count - 1)]
    inside, down, up, matrix = own_fluxes(conserved)
    left, right, inside = lax.optimization_barrier((left, right, inside))
    first_y, last_y, columns = edge_rows(conserved, left, right)
    top = lax.ppermute(last_y, "sim", ring("sim", 1))
    bottom = lax.ppermute(first_y, "sim", ring("sim", -1))
    chunks, blocks, rims = transform_bricks(count, inside, down, up, columns, matrix)
    blocks, *far = lax.optimization_barrier((blocks, *far))
    chunks, blocks = mend(count, chunks, top, bottom, blocks, rims, matrix)
    moved = {0: chunks[0]}
    for k in leaving_order(count)[:-1]:
        moved[k] = lax.ppermute(chunks[k], "section", exchange_pairs(count, k))
    peaks = group_maxima(count, groups, membership.shape[0], blocks, [labels, left, *far, right])
    for shift in steps_over("sim"):
        peaks = with_others(peaks, "sim", [shift])
    if count <= 4:
        peaks, moved[1] = lax.optimization_barrier((peaks, moved[1]))
        peaks = with_others(peaks, "section", range(1, count))
    else:
        for shift in steps_over("section"):
            peaks = with_others(peaks, "section", [shift])
    return tuple(scale(count, groups, [moved[k] for k in leaving_order(count)], peaks, labels))


def solution(mesh):
    placed = (
        P(None, "sim", "section"),
        P(None, None, "sim", "section"),
        P(None, "sim", "section"),
        P(("sim", "section"), None),
        P("sim", None),
    )
    return jax.shard_map(
        per_device,
        mesh=mesh,
        in_specs=placed,
        out_specs=(P(None, None, ("sim", "section"), None), P()),
        check_vma=False,
    )
```

```python
import functools

import jax
import jax.numpy as jnp
import numpy as np
from jax import lax
from jax.experimental import pallas as pl
from jax.experimental.pallas import tpu as pltpu
from jax.sharding import PartitionSpec as P

GAMMA_LESS = 0.4
COURANT = 0.05
DIFFUSE = 0.1
EPSILON = 1e-06
FIELDS = 5
PAD = 8
COLUMN_ROWS = 8
LABEL_ROWS = 8
LANES = 128
EVEN = 0.5
WIDE = float(np.sqrt(0.5) * np.cos(np.pi / 8))
NARROW = float(np.sqrt(0.5) * np.cos(3 * np.pi / 8))
VMEM_LIMIT = 48 * 1024 * 1024


def vmem():
    return pl.BlockSpec(memory_space=pltpu.VMEM)


def lanes_of(shape):
    return lax.broadcasted_iota(jnp.int32, shape, 1)


def butterfly(a, b, c, d):
    s, t, u, v = a + d, b + c, a - d, b - c
    return (
        EVEN * (s + t),
        WIDE * u + NARROW * v,
        EVEN * (s - t),
        NARROW * u - WIDE * v,
    )


def cosine(k, d):
    factor = 0.5 if k == 0 else np.sqrt(0.5)
    return float(factor * np.cos(np.pi * (2 * d + 1) * k / 8))


def write_matrix(matrix, width):
    step = 16
    row = lax.broadcasted_iota(jnp.int32, (step, width), 0)
    column = lanes_of((step, width))
    quarter = width // 4
    k, j, d = lax.div(column, quarter), lax.rem(column, quarter), lax.rem(row, 4)
    entry = jnp.zeros((step, width), jnp.float32)
    for a in range(4):
        for b in range(4):
            entry = jnp.where(jnp.logical_and(k == a, d == b), cosine(a, b), entry)
    high = entry.astype(jnp.bfloat16).astype(jnp.float32)
    low = entry - high
    zero = jnp.zeros((step, width), jnp.bfloat16)
    for start in range(0, width, step):
        own = j == lax.div(row + start, 4)
        upper = jnp.where(own, high, 0.0).astype(jnp.bfloat16)
        lower = jnp.where(own, low, 0.0).astype(jnp.bfloat16)
        matrix[start : start + step, 0:width] = upper
        matrix[start : start + step, width : 2 * width] = lower
        matrix[width + start : width + start + step, 0:width] = upper
        matrix[width + start : width + start + step, width : 2 * width] = zero


def kernel_params():
    return pltpu.CompilerParams(vmem_limit_bytes=VMEM_LIMIT)


def array(shape, dtype=jnp.float32):
    return jax.ShapeDtypeStruct(shape, dtype)


def pack_kernel(conserved, membership, slots, first_x, last_x, labels):
    fields, depth, y, width = conserved.shape
    quarter = y // 4
    lane = lanes_of((y, width))
    first = jnp.zeros((y, width), jnp.float32)
    last = jnp.zeros((y, width), jnp.float32)
    for j in range(fields * depth):
        value = conserved[j // depth, j % depth]
        first = jnp.where(lane == j, pltpu.roll(value, j, 1) if j else value, first)
        last = jnp.where(lane == j, pltpu.roll(value, j + 1, 1), last)
    rows, columns = membership.shape
    labels[...] = jnp.zeros(labels.shape, jnp.float32)
    for t in range(columns // LANES):
        part = membership[:, t * LANES : (t + 1) * LANES].astype(jnp.float32)
        labels[t * rows : (t + 1) * rows, :] = part
    labels[LABEL_ROWS - 1 : LABEL_ROWS, 0 : slots.shape[1]] = slots[...].astype(jnp.float32)
    own = labels[...]
    for column, out in ((first, first_x), (last, last_x)):
        packed = column[0:quarter]
        for c in range(1, 4):
            packed = packed + pltpu.roll(column[c * quarter : (c + 1) * quarter], 32 * c, 1)
        out[0:quarter, :] = packed
        out[quarter:, :] = own


def pack(conserved, membership, slots):
    y, width = conserved.shape[2:]
    shapes = [
        array((y // 4 + LABEL_ROWS, width)),
        array((y // 4 + LABEL_ROWS, width)),
        array((LABEL_ROWS, width)),
    ]
    return pl.pallas_call(
        pack_kernel,
        out_shape=shapes,
        in_specs=[vmem()] * 3,
        out_specs=[vmem()] * 3,
        compiler_params=kernel_params(),
    )(conserved, membership, slots)


def slot_of(labels, brick):
    row = labels[LABEL_ROWS - 1 : LABEL_ROWS, :]
    return jnp.max(jnp.where(lanes_of(row.shape) == brick, row, 0.0)).astype(jnp.int32)


def fluxes(c):
    rho, mx, my, mz, e = c
    inverse = 1.0 / rho
    u, v = mx * inverse, my * inverse
    pressure = GAMMA_LESS * (e - 0.5 * (mx * mx + my * my + mz * mz) * inverse)
    total = e + pressure
    flux_x = (mx, mx * u + pressure, my * u, mz * u, total * u)
    flux_y = (my, mx * v, my * v + pressure, mz * v, total * v)
    return flux_x, flux_y


def column_terms(own, depth, sign):
    fields = [pltpu.roll(own, LANES - depth * f, 1) if f else own for f in range(FIELDS)]
    flux_x, unused = fluxes(fields)
    return [DIFFUSE * fields[f] + sign * flux_x[f] for f in range(FIELDS)]


def row_terms(c):
    rows, width = c[0].shape
    lane = lanes_of((rows, width))
    flux_x, flux_y = fluxes(c)
    terms = []
    for f in range(FIELDS):
        base = DIFFUSE * c[f]
        gx, gy = COURANT * flux_x[f], COURANT * flux_y[f]
        from_left = jnp.where(lane == 0, 0.0, pltpu.roll(base + gx, 1, 1))
        from_right = jnp.where(lane == width - 1, 0.0, pltpu.roll(base - gx, width - 1, 1))
        terms.append(((1.0 - 4.0 * DIFFUSE) * c[f] + from_left + from_right, base + gy, base - gy))
    return terms


def beside(low, high, z):
    rows, width = low.shape
    lane = lanes_of((rows, width))
    at_left = pltpu.roll(low, LANES - z, 1) if z else low
    at_right = pltpu.roll(high, LANES - 1 - z, 1)
    return jnp.where(lane == 0, at_left, jnp.where(lane == width - 1, at_right, 0.0))


def fold_rows(across, down, up, j, origin, number, stride):
    t = {}
    for o in range(-3, 7):
        t[o] = (
            across[j, pl.ds(origin + o, number, stride=stride), :]
            + down[j, pl.ds(origin + o - 1, number, stride=stride), :]
            + up[j, pl.ds(origin + o + 1, number, stride=stride), :]
        )
    residual = [
        t[m] - (9.0 / 16.0) * (t[m - 1] + t[m + 1]) + (1.0 / 16.0) * (t[m - 3] + t[m + 3])
        for m in range(4)
    ]
    return butterfly(*residual)


def halves(value):
    high = value.astype(jnp.bfloat16)
    return high, (value - high.astype(jnp.float32)).astype(jnp.bfloat16)


def over_lanes(peak):
    peak = jnp.maximum(peak, pltpu.roll(peak, 64, 1))
    return jnp.maximum(peak, pltpu.roll(peak, 32, 1))


def partner_of(me, k, count):
    if count & (count - 1) == 0:
        return me ^ k
    return lax.rem(me + k, count)


def sender_of(me, k, count):
    if count & (count - 1) == 0:
        return me ^ k
    return lax.rem(me - k + count, count)


def flux_kernel(conserved, across, down, up, matrix):
    fields, depth, y, width = conserved.shape
    write_matrix(matrix, width)
    step = 16

    def flux_rows(i, carry):
        r = pl.ds(pl.multiple_of(i * step, step), step)
        padded = pl.ds(pl.multiple_of(i * step + PAD, PAD), step)
        for z in range(depth):
            for f, (a, d, u) in enumerate(row_terms([conserved[f, z, r, :] for f in range(fields)])):
                j = f * depth + z
                across[j, r, :] = a
                down[j, padded, :] = d
                up[j, padded, :] = u
        return carry

    lax.fori_loop(0, y // step, flux_rows, 0)


def own_fluxes(conserved):
    fields, depth, y, width = conserved.shape
    total = fields * depth
    tall = array((total, y + 2 * PAD, width))
    return pl.pallas_call(
        flux_kernel,
        out_shape=[array((total, y, width)), tall, tall, array((2 * width, 2 * width), jnp.bfloat16)],
        in_specs=[vmem()],
        out_specs=[vmem()] * 4,
        compiler_params=kernel_params(),
        cost_estimate=pl.CostEstimate(flops=40 * total * y * width, bytes_accessed=16 * total * y * width, transcendentals=0),
    )(conserved)


def edge_kernel(conserved, left, right, first_y, last_y, columns):
    fields, depth, y, width = conserved.shape
    total, quarter = fields * depth, y // 4
    for side, column in enumerate((left, right)):
        for c in range(4):
            value = column[0:quarter, :]
            value = pltpu.roll(value, LANES - 32 * c, 1) if c else value
            columns[side, c * quarter : (c + 1) * quarter, :] = value
        place = 4 * total + 4 * side
        first_y[place : place + 4, :] = columns[side, 0:4, :]
        last_y[place : place + 4, :] = columns[side, y - 4 : y, :]
    for j in range(total):
        first_y[4 * j : 4 * j + 4, :] = conserved[j // depth, j % depth, 0:4, :]
        last_y[4 * j : 4 * j + 4, :] = conserved[j // depth, j % depth, y - 4 : y, :]


def edge_rows(conserved, left, right):
    fields, depth, y, width = conserved.shape
    message = array((4 * fields * depth + COLUMN_ROWS, width))
    return pl.pallas_call(
        edge_kernel,
        out_shape=[message, message, array((2, y, width))],
        in_specs=[vmem()] * 3,
        out_specs=[vmem()] * 3,
        compiler_params=kernel_params(),
    )(conserved, left, right)


def brick_kernel(count, *refs):
    inside, down, up, columns, matrix = refs[:5]
    outs, refs = refs[5 : 5 + count], refs[5 + count :]
    blocks, rim_a, rim_d, rim_u, across, edges, split, coefficients, staged = refs
    total, y, width = inside.shape
    depth = total // FIELDS
    nb = y // 4
    rows = y // count

    for side in range(2):
        for f, value in enumerate(column_terms(columns[side], depth, COURANT if side == 0 else -COURANT)):
            edges[side, f] = value

    step = 24
    for start in range(0, y, step):
        for f in range(FIELDS):
            low, high = edges[0, f, start : start + step, :], edges[1, f, start : start + step, :]
            for z in range(depth):
                j = f * depth + z
                value = inside[j, start : start + step, :] + beside(low, high, z)
                across[j, PAD + start : PAD + start + step, :] = value
    for j in range(total):
        for source, rim in ((across, rim_a), (down, rim_d), (up, rim_u)):
            rim[j, 0:8, :] = source[j, PAD : PAD + 8, :]
            rim[j, 8:16, :] = source[j, y : y + 8, :]

    for f in range(FIELDS):
        rows_of = [fold_rows(across, down, up, f * depth + z, PAD, nb, 4) for z in range(4)]
        mixed = [butterfly(*[rows_of[z][m] for z in range(4)]) for m in range(4)]
        for k in range(4):
            high, low = halves(jnp.concatenate([mixed[m][k] for m in range(4)], axis=0))
            split[f, k * y : (k + 1) * y, 0:width] = high
            split[f, k * y : (k + 1) * y, width : 2 * width] = low
        product = jnp.dot(split[f], matrix[...], preferred_element_type=jnp.float32)
        result = product[:, 0:width] + product[:, width : 2 * width]
        peak = None
        for k in range(4):
            for m in range(4):
                value = result[k * y + m * nb : k * y + (m + 1) * nb]
                coefficients[f * depth + k, pl.ds(m, nb, stride=4), :] = value
                size = jnp.abs(value)
                peak = size if peak is None else jnp.maximum(peak, size)
        blocks[f] = over_lanes(peak)

    me = lax.axis_index("section")
    if rows % 8 == 0:
        for k in range(count):
            p = partner_of(me, k, count)
            for j in range(total):
                outs[k][j // depth, j % depth] = coefficients[j, pl.ds(pl.multiple_of(p * rows, 8), rows), :]
    else:
        for p in range(count):
            staged[p] = coefficients[:, p * rows : (p + 1) * rows, :]
        for k in range(count):
            p = partner_of(me, k, count)
            for j in range(total):
                outs[k][j // depth, j % depth] = staged[p, j]


def transform_bricks(count, inside, down, up, columns, matrix):
    total, y, width = inside.shape
    depth = total // FIELDS
    rows, tall = y // count, y + 2 * PAD
    chunk = array((FIELDS, depth, rows, width))
    rim = array((total, 2 * PAD, width))
    results = pl.pallas_call(
        functools.partial(brick_kernel, count),
        out_shape=[chunk] * count + [array((FIELDS, y // 4, width))] + [rim] * 3,
        in_specs=[vmem()] * 5,
        out_specs=[vmem()] * (count + 4),
        scratch_shapes=[
            pltpu.VMEM((total, tall, width), jnp.float32),
            pltpu.VMEM((2, FIELDS, y, width), jnp.float32),
            pltpu.VMEM((FIELDS, depth * y, 2 * width), jnp.bfloat16),
            pltpu.VMEM((total, y, width), jnp.float32),
            pltpu.VMEM((1, 1, 8, LANES) if rows % 8 == 0 else (count, total, rows, width), jnp.float32),
        ],
        compiler_params=kernel_params(),
        cost_estimate=pl.CostEstimate(flops=80 * total * y * width, bytes_accessed=16 * total * y * width, transcendentals=0),
    )(inside, down, up, columns, matrix)
    return results[:count], results[count], results[count + 1 :]


def leaving_order(count):
    return [*range(2, count), 1, 0]


def mend_kernel(count, *refs):
    chunks, refs = refs[:count], refs[count:]
    top, bottom, blocks, rim_a, rim_d, rim_u, matrix = refs[:7]
    outs, mended, refs = refs[7 : 7 + count], refs[7 + count], refs[8 + count :]
    halo, columns, across, down, up, folded, split, result, fixed = refs
    fields, depth, rows, width = chunks[0].shape
    total = fields * depth
    nb = blocks.shape[1]

    halo[...] = jnp.ones(halo.shape, jnp.float32)
    columns[...] = jnp.ones(columns.shape, jnp.float32)
    for j in range(total):
        halo[j, 4:8, :] = top[4 * j : 4 * j + 4, :]
        halo[j, 8:12, :] = bottom[4 * j : 4 * j + 4, :]
    for side in range(2):
        place = 4 * total + 4 * side
        columns[side, 4:8, :] = top[place : place + 4, :]
        columns[side, 8:12, :] = bottom[place : place + 4, :]
    low = column_terms(columns[0], depth, COURANT)
    high = column_terms(columns[1], depth, -COURANT)
    for z in range(depth):
        c = [halo[f * depth + z] for f in range(fields)]
        for f, (a, d, u) in enumerate(row_terms(c)):
            j = f * depth + z
            values = (a + beside(low[f], high[f], z), d, u)
            for value, rim, target in zip(values, (rim_a, rim_d, rim_u), (across, down, up)):
                target[j, 0:8, :] = value[0:8]
                target[j, 8:24, :] = rim[j]
                target[j, 24:32, :] = value[8:16]
    for j in range(total):
        for k, value in enumerate(fold_rows(across, down, up, j, PAD, 2, 12)):
            folded[j, 2 * k : 2 * k + 2, :] = value
    for f in range(fields):
        values = butterfly(*[folded[f * depth + z] for z in range(4)])
        for half in range(2):
            both = jnp.concatenate(values[2 * half : 2 * half + 2], axis=0)
            upper, lower = halves(both)
            place = f * 32 + half * 16
            split[place : place + 16, 0:width] = upper
            split[place : place + 16, width : 2 * width] = lower
    product = jnp.dot(split[...], matrix[...], preferred_element_type=jnp.float32)
    result[...] = product[:, 0:width] + product[:, width : 2 * width]
    for j in range(total):
        for side in range(2):
            fixed[side, j] = result[pl.ds(8 * j + side, 4, stride=2), :]
    mended[...] = blocks[...]
    for f in range(fields):
        for side in range(2):
            size = jnp.abs(fixed[side, f * depth])
            for z in range(1, depth):
                size = jnp.maximum(size, jnp.abs(fixed[side, f * depth + z]))
            peak = over_lanes(jnp.max(size, axis=0, keepdims=True))
            row = side * (nb - 1)
            mended[f, row : row + 1, :] = peak

    me = lax.axis_index("section")
    for i, k in enumerate(leaving_order(count)):
        p = partner_of(me, k, count)
        for side, start in ((0, 0), (1, rows - 4)):

            @pl.when(p == side * (count - 1))
            def replace(i=i, side=side, start=start):
                for j in range(total):
                    outs[i][j // depth, j % depth, start : start + 4, :] = fixed[side, j]


def mend(count, chunks, top, bottom, blocks, rims, matrix):
    fields, depth, rows, width = chunks[0].shape
    total = fields * depth
    tall = pltpu.VMEM((total, 4 * PAD, width), jnp.float32)
    results = pl.pallas_call(
        functools.partial(mend_kernel, count),
        out_shape=[array(chunks[0].shape)] * count + [array(blocks.shape)],
        in_specs=[vmem()] * (count + 7),
        out_specs=[vmem()] * (count + 1),
        input_output_aliases={k: k for k in range(count)},
        scratch_shapes=[
            pltpu.VMEM((total, 2 * PAD, width), jnp.float32),
            pltpu.VMEM((2, 2 * PAD, width), jnp.float32),
            tall,
            tall,
            tall,
            pltpu.VMEM((total, 8, width), jnp.float32),
            pltpu.VMEM((8 * total, 2 * width), jnp.bfloat16),
            pltpu.VMEM((8 * total, width), jnp.float32),
            pltpu.VMEM((2, total, 4, width), jnp.float32),
        ],
        compiler_params=kernel_params(),
    )(*[chunks[k] for k in leaving_order(count)], top, bottom, blocks, *rims, matrix)
    return dict(zip(leaving_order(count), results)), results[count]


def group_kernel(count, groups, own_rows, *refs):
    blocks, refs = refs[0], refs[1:]
    messages, (peaks, gathered, listed, packed, table) = refs[:count], refs[count:]
    nb = blocks.shape[1]
    me = lax.axis_index("section")
    slot = slot_of(messages[0], me)
    within = lax.rem(slot, 4) * 32
    tile = lax.div(slot, 4)
    for d, message in enumerate(messages):
        height = gathered.shape[1]
        value = message[message.shape[0] - height :, :]
        if count > 4:
            value = pltpu.roll(value, lax.rem(height - tile * own_rows, height), 0)
        gathered[lax.rem(me + count - d, count)] = value
    for q in range(count):
        listed[q * own_rows : (q + 1) * own_rows, :] = gathered[q, 0:own_rows, :]
    part = nb // 4
    band = lax.div(lanes_of((part, LANES)), 32)
    labels = jnp.zeros((part, LANES), jnp.float32)
    for c in range(4):
        turned = pltpu.roll(listed[c * part : (c + 1) * part, :], lax.rem(32 * c - within + LANES, LANES), 1)
        labels = jnp.where(band == c, turned, labels)
    for f in range(FIELDS):
        own = jnp.zeros((part, LANES), jnp.float32)
        for c in range(4):
            own = jnp.where(band == c, blocks[f, c * part : (c + 1) * part, :], own)
        packed[f, 0:part, :] = own
    lane8 = lanes_of((8, LANES))
    sub8 = lax.broadcasted_iota(jnp.int32, (8, LANES), 0)
    label_rows = [jnp.broadcast_to(labels[r : r + 1], (8, LANES)) for r in range(part)]

    def group_tile(g, carry):
        wanted = (sub8 + g * 8).astype(jnp.float32)
        matches = [label_rows[r] == wanted for r in range(part)]
        found = jnp.zeros((8, LANES), jnp.float32)
        for f in range(FIELDS):
            best = jnp.zeros((8, LANES), jnp.float32)
            for r in range(part):
                row = jnp.broadcast_to(packed[f, r : r + 1, :], (8, LANES))
                best = jnp.maximum(best, jnp.where(matches[r], row, 0.0))
            found = jnp.where(lane8 == f, jnp.max(best, axis=1, keepdims=True), found)
        table[pl.ds(pl.multiple_of(g * 8, 8), 8), :] = found
        return carry

    high = table.shape[0]
    if groups < high:
        table[...] = jnp.zeros((high, LANES), jnp.float32)
    lax.fori_loop(0, pl.cdiv(groups, 8), group_tile, 0)
    for g in range(high // LANES):
        peaks[:, g * LANES : (g + 1) * LANES] = jnp.transpose(table[g * LANES : (g + 1) * LANES, :])[0:8]


def group_maxima(count, groups, own_rows, blocks, messages):
    high = pl.cdiv(groups, LANES) * LANES
    nb = blocks.shape[1]
    return pl.pallas_call(
        functools.partial(group_kernel, count, groups, own_rows),
        out_shape=array((8, high)),
        in_specs=[vmem()] * (count + 1),
        out_specs=vmem(),
        scratch_shapes=[
            pltpu.VMEM((count, messages[0].shape[0], LANES), jnp.float32),
            pltpu.VMEM((nb, LANES), jnp.float32),
            pltpu.VMEM((FIELDS, 8, LANES), jnp.float32),
            pltpu.VMEM((high, LANES), jnp.float32),
        ],
        compiler_params=kernel_params(),
    )(blocks, *messages)


def scale_kernel(count, groups, *refs):
    chunks, refs = refs[:count], refs[count:]
    peaks, labels, coded, group_peak, wide = refs
    fields, depth, rows, width = chunks[0].shape
    nb = rows // 4
    high = peaks.shape[1]
    me = lax.axis_index("section")
    group_peak[...] = peaks[0:fields, 0:groups]
    own_labels = labels[...].astype(jnp.int32)
    lane = lanes_of((8, LANES))
    inverse = 1.0 / (peaks[...] + EPSILON)
    tables = [
        [jnp.broadcast_to(inverse[f : f + 1, g * LANES : (g + 1) * LANES], (8, LANES)) for g in range(high // LANES)]
        for f in range(fields)
    ]
    for i, k in enumerate(leaving_order(count)):
        slot = slot_of(labels, sender_of(me, k, count))
        tile = own_labels
        if count > 4:
            tile = pltpu.roll(tile, lax.rem(LABEL_ROWS - lax.div(slot, 4) * nb, LABEL_ROWS), 0)
        within = lax.rem(slot, 4) * 32 + lax.rem(lane, 32)
        own = jnp.take_along_axis(tile, within, axis=1)
        place = pl.ds(pl.multiple_of(slot * width, width), width)
        for f in range(fields):
            if high == LANES:
                found = jnp.take_along_axis(tables[f][0], own, axis=1)
            else:
                found = jnp.zeros((8, LANES), jnp.float32)
                inside = lax.rem(own, LANES)
                for g in range(high // LANES):
                    here = jnp.take_along_axis(tables[f][g], inside, axis=1)
                    found = jnp.where(lax.div(own, LANES) == g, here, found)
            for m in range(4):
                wide[i, f, pl.ds(m, nb, stride=4), :] = found[0:nb]
            factor = wide[i, f]
            for z in range(depth):
                coded[f, z, :, place] = chunks[i][f, z] * factor


def scale(count, groups, chunks, peaks, labels):
    fields, depth, rows, width = chunks[0].shape
    return pl.pallas_call(
        functools.partial(scale_kernel, count, groups),
        out_shape=[array((fields, depth, rows, width * count)), array((fields, groups))],
        in_specs=[vmem()] * (count + 2),
        out_specs=[vmem()] * 2,
        scratch_shapes=[
            pltpu.VMEM((count, fields, rows, width), jnp.float32),
        ],
        compiler_params=kernel_params(),
    )(*chunks, peaks, labels)


def ring(axis, shift):
    count = lax.axis_size(axis)
    return [(i, (i + shift) % count) for i in range(count)]


def exchange_pairs(count, k):
    if count & (count - 1) == 0:
        return [(i, i ^ k) for i in range(count)]
    return [(i, (i + k) % count) for i in range(count)]


def steps_over(axis):
    count = lax.axis_size(axis)
    span, shifts = 1, []
    while span < count:
        shifts.append(min(span, count - span))
        span += shifts[-1]
    return shifts


def with_others(value, axis, shifts):
    count = lax.axis_size(axis)
    others = [lax.ppermute(value, axis, exchange_pairs(count, k)) for k in shifts]
    return functools.reduce(jnp.maximum, others, value)


def per_device(density, momentum, energy, membership, slot_of_brick):
    count = lax.axis_size("section")
    groups = 2 * lax.axis_size("sim") * count
    conserved = jnp.concatenate([density[None], momentum, energy[None]], axis=0)
    first_x, last_x, labels = pack(conserved, membership, slot_of_brick)
    left = lax.ppermute(last_x, "section", ring("section", 1))
    right = lax.ppermute(first_x, "section", ring("section", -1))
    far = [lax.ppermute(labels, "section", ring("section", d)) for d in range(2, count - 1)]
    inside, down, up, matrix = own_fluxes(conserved)
    left, right, inside = lax.optimization_barrier((left, right, inside))
    first_y, last_y, columns = edge_rows(conserved, left, right)
    top = lax.ppermute(last_y, "sim", ring("sim", 1))
    bottom = lax.ppermute(first_y, "sim", ring("sim", -1))
    chunks, blocks, rims = transform_bricks(count, inside, down, up, columns, matrix)
    blocks, *far = lax.optimization_barrier((blocks, *far))
    chunks, blocks = mend(count, chunks, top, bottom, blocks, rims, matrix)
    moved = {0: chunks[0]}
    for k in leaving_order(count)[:-1]:
        moved[k] = lax.ppermute(chunks[k], "section", exchange_pairs(count, k))
    peaks = group_maxima(count, groups, membership.shape[0], blocks, [labels, left, *far, right])
    for shift in steps_over("sim"):
        peaks = with_others(peaks, "sim", [shift])
    for shift in reversed(steps_over("section")):
        peaks = with_others(peaks, "section", [shift])
    return tuple(scale(count, groups, [moved[k] for k in leaving_order(count)], peaks, labels))


def solution(mesh):
    placed = (
        P(None, "sim", "section"),
        P(None, None, "sim", "section"),
        P(None, "sim", "section"),
        P(("sim", "section"), None),
        P("sim", None),
    )
    return jax.shard_map(
        per_device,
        mesh=mesh,
        in_specs=placed,
        out_specs=(P(None, None, ("sim", "section"), None), P()),
        check_vma=False,
    )
```

```python
import functools

import jax
import jax.numpy as jnp
import numpy as np
from jax import lax
from jax.experimental import pallas as pl
from jax.experimental.pallas import tpu as pltpu
from jax.sharding import PartitionSpec as P

GAMMA_LESS = 0.4
COURANT = 0.05
DIFFUSE = 0.1
EPSILON = 1e-06
FIELDS = 5
PAD = 8
COLUMN_ROWS = 8
LABEL_ROWS = 8
LANES = 128
EVEN = 0.5
WIDE = float(np.sqrt(0.5) * np.cos(np.pi / 8))
NARROW = float(np.sqrt(0.5) * np.cos(3 * np.pi / 8))
VMEM_LIMIT = 48 * 1024 * 1024


def vmem():
    return pl.BlockSpec(memory_space=pltpu.VMEM)


def lanes_of(shape):
    return lax.broadcasted_iota(jnp.int32, shape, 1)


def butterfly(a, b, c, d):
    s, t, u, v = a + d, b + c, a - d, b - c
    return (
        EVEN * (s + t),
        WIDE * u + NARROW * v,
        EVEN * (s - t),
        NARROW * u - WIDE * v,
    )


def cosine(k, d):
    factor = 0.5 if k == 0 else np.sqrt(0.5)
    return float(factor * np.cos(np.pi * (2 * d + 1) * k / 8))


def write_matrix(matrix, width):
    step = 16
    row = lax.broadcasted_iota(jnp.int32, (step, width), 0)
    column = lanes_of((step, width))
    quarter = width // 4
    k, j, d = lax.div(column, quarter), lax.rem(column, quarter), lax.rem(row, 4)
    entry = jnp.zeros((step, width), jnp.float32)
    for a in range(4):
        for b in range(4):
            entry = jnp.where(jnp.logical_and(k == a, d == b), cosine(a, b), entry)
    high = entry.astype(jnp.bfloat16).astype(jnp.float32)
    low = entry - high
    zero = jnp.zeros((step, width), jnp.bfloat16)
    for start in range(0, width, step):
        own = j == lax.div(row + start, 4)
        upper = jnp.where(own, high, 0.0).astype(jnp.bfloat16)
        lower = jnp.where(own, low, 0.0).astype(jnp.bfloat16)
        matrix[start : start + step, 0:width] = upper
        matrix[start : start + step, width : 2 * width] = lower
        matrix[width + start : width + start + step, 0:width] = upper
        matrix[width + start : width + start + step, width : 2 * width] = zero


def kernel_params():
    return pltpu.CompilerParams(vmem_limit_bytes=VMEM_LIMIT)


def array(shape, dtype=jnp.float32):
    return jax.ShapeDtypeStruct(shape, dtype)


def pack_kernel(conserved, membership, slots, first_x, last_x, labels):
    fields, depth, y, width = conserved.shape
    quarter = y // 4
    lane = lanes_of((y, width))
    first = jnp.zeros((y, width), jnp.float32)
    last = jnp.zeros((y, width), jnp.float32)
    for j in range(fields * depth):
        value = conserved[j // depth, j % depth]
        first = jnp.where(lane == j, pltpu.roll(value, j, 1) if j else value, first)
        last = jnp.where(lane == j, pltpu.roll(value, j + 1, 1), last)
    rows, columns = membership.shape
    labels[...] = jnp.zeros(labels.shape, jnp.float32)
    for t in range(columns // LANES):
        part = membership[:, t * LANES : (t + 1) * LANES].astype(jnp.float32)
        labels[t * rows : (t + 1) * rows, :] = part
    labels[LABEL_ROWS - 1 : LABEL_ROWS, 0 : slots.shape[1]] = slots[...].astype(jnp.float32)
    own = labels[...]
    for column, out in ((first, first_x), (last, last_x)):
        packed = column[0:quarter]
        for c in range(1, 4):
            packed = packed + pltpu.roll(column[c * quarter : (c + 1) * quarter], 32 * c, 1)
        out[0:quarter, :] = packed
        out[quarter:, :] = own


def pack(conserved, membership, slots):
    y, width = conserved.shape[2:]
    shapes = [
        array((y // 4 + LABEL_ROWS, width)),
        array((y // 4 + LABEL_ROWS, width)),
        array((LABEL_ROWS, width)),
    ]
    return pl.pallas_call(
        pack_kernel,
        out_shape=shapes,
        in_specs=[vmem()] * 3,
        out_specs=[vmem()] * 3,
        compiler_params=kernel_params(),
    )(conserved, membership, slots)


def slot_of(labels, brick):
    row = labels[LABEL_ROWS - 1 : LABEL_ROWS, :]
    return jnp.max(jnp.where(lanes_of(row.shape) == brick, row, 0.0)).astype(jnp.int32)


def fluxes(c):
    rho, mx, my, mz, e = c
    inverse = 1.0 / rho
    u, v = mx * inverse, my * inverse
    pressure = GAMMA_LESS * (e - 0.5 * (mx * mx + my * my + mz * mz) * inverse)
    total = e + pressure
    flux_x = (mx, mx * u + pressure, my * u, mz * u, total * u)
    flux_y = (my, mx * v, my * v + pressure, mz * v, total * v)
    return flux_x, flux_y


def column_terms(own, depth, sign):
    fields = [pltpu.roll(own, LANES - depth * f, 1) if f else own for f in range(FIELDS)]
    flux_x, unused = fluxes(fields)
    return [DIFFUSE * fields[f] + sign * flux_x[f] for f in range(FIELDS)]


def row_terms(c):
    rows, width = c[0].shape
    lane = lanes_of((rows, width))
    flux_x, flux_y = fluxes(c)
    terms = []
    for f in range(FIELDS):
        base = DIFFUSE * c[f]
        gx, gy = COURANT * flux_x[f], COURANT * flux_y[f]
        from_left = jnp.where(lane == 0, 0.0, pltpu.roll(base + gx, 1, 1))
        from_right = jnp.where(lane == width - 1, 0.0, pltpu.roll(base - gx, width - 1, 1))
        terms.append(((1.0 - 4.0 * DIFFUSE) * c[f] + from_left + from_right, base + gy, base - gy))
    return terms


def beside(low, high, z):
    rows, width = low.shape
    lane = lanes_of((rows, width))
    at_left = pltpu.roll(low, LANES - z, 1) if z else low
    at_right = pltpu.roll(high, LANES - 1 - z, 1)
    return jnp.where(lane == 0, at_left, jnp.where(lane == width - 1, at_right, 0.0))


def fold_rows(across, down, up, j, origin, number, stride):
    t = {}
    for o in range(-3, 7):
        t[o] = (
            across[j, pl.ds(origin + o, number, stride=stride), :]
            + down[j, pl.ds(origin + o - 1, number, stride=stride), :]
            + up[j, pl.ds(origin + o + 1, number, stride=stride), :]
        )
    residual = [
        t[m] - (9.0 / 16.0) * (t[m - 1] + t[m + 1]) + (1.0 / 16.0) * (t[m - 3] + t[m + 3])
        for m in range(4)
    ]
    return butterfly(*residual)


def halves(value):
    high = value.astype(jnp.bfloat16)
    return high, (value - high.astype(jnp.float32)).astype(jnp.bfloat16)


def over_lanes(peak):
    peak = jnp.maximum(peak, pltpu.roll(peak, 64, 1))
    return jnp.maximum(peak, pltpu.roll(peak, 32, 1))


def partner_of(me, k, count):
    if count & (count - 1) == 0:
        return me ^ k
    return lax.rem(me + k, count)


def sender_of(me, k, count):
    if count & (count - 1) == 0:
        return me ^ k
    return lax.rem(me - k + count, count)


def flux_kernel(conserved, across, down, up, matrix):
    fields, depth, y, width = conserved.shape
    write_matrix(matrix, width)
    step = 16

    def flux_rows(i, carry):
        r = pl.ds(pl.multiple_of(i * step, step), step)
        padded = pl.ds(pl.multiple_of(i * step + PAD, PAD), step)
        for z in range(depth):
            for f, (a, d, u) in enumerate(row_terms([conserved[f, z, r, :] for f in range(fields)])):
                j = f * depth + z
                across[j, r, :] = a
                down[j, padded, :] = d
                up[j, padded, :] = u
        return carry

    lax.fori_loop(0, y // step, flux_rows, 0)


def own_fluxes(conserved):
    fields, depth, y, width = conserved.shape
    total = fields * depth
    tall = array((total, y + 2 * PAD, width))
    return pl.pallas_call(
        flux_kernel,
        out_shape=[array((total, y, width)), tall, tall, array((2 * width, 2 * width), jnp.bfloat16)],
        in_specs=[vmem()],
        out_specs=[vmem()] * 4,
        compiler_params=kernel_params(),
        cost_estimate=pl.CostEstimate(flops=40 * total * y * width, bytes_accessed=16 * total * y * width, transcendentals=0),
    )(conserved)


def edge_kernel(conserved, left, right, first_y, last_y, columns):
    fields, depth, y, width = conserved.shape
    total, quarter = fields * depth, y // 4
    for side, column in enumerate((left, right)):
        for c in range(4):
            value = column[0:quarter, :]
            value = pltpu.roll(value, LANES - 32 * c, 1) if c else value
            columns[side, c * quarter : (c + 1) * quarter, :] = value
        place = 4 * total + 4 * side
        first_y[place : place + 4, :] = columns[side, 0:4, :]
        last_y[place : place + 4, :] = columns[side, y - 4 : y, :]
    for j in range(total):
        first_y[4 * j : 4 * j + 4, :] = conserved[j // depth, j % depth, 0:4, :]
        last_y[4 * j : 4 * j + 4, :] = conserved[j // depth, j % depth, y - 4 : y, :]


def edge_rows(conserved, left, right):
    fields, depth, y, width = conserved.shape
    message = array((4 * fields * depth + COLUMN_ROWS, width))
    return pl.pallas_call(
        edge_kernel,
        out_shape=[message, message, array((2, y, width))],
        in_specs=[vmem()] * 3,
        out_specs=[vmem()] * 3,
        compiler_params=kernel_params(),
    )(conserved, left, right)


def brick_kernel(count, *refs):
    inside, down, up, columns, matrix = refs[:5]
    outs, refs = refs[5 : 5 + count], refs[5 + count :]
    blocks, rim_a, rim_d, rim_u, across, edges, split, coefficients, staged = refs
    total, y, width = inside.shape
    depth = total // FIELDS
    nb = y // 4
    rows = y // count

    for side in range(2):
        for f, value in enumerate(column_terms(columns[side], depth, COURANT if side == 0 else -COURANT)):
            edges[side, f] = value

    step = 24
    for start in range(0, y, step):
        for f in range(FIELDS):
            low, high = edges[0, f, start : start + step, :], edges[1, f, start : start + step, :]
            for z in range(depth):
                j = f * depth + z
                value = inside[j, start : start + step, :] + beside(low, high, z)
                across[j, PAD + start : PAD + start + step, :] = value
    for j in range(total):
        for source, rim in ((across, rim_a), (down, rim_d), (up, rim_u)):
            rim[j, 0:8, :] = source[j, PAD : PAD + 8, :]
            rim[j, 8:16, :] = source[j, y : y + 8, :]

    for f in range(FIELDS):
        rows_of = [fold_rows(across, down, up, f * depth + z, PAD, nb, 4) for z in range(4)]
        mixed = [butterfly(*[rows_of[z][m] for z in range(4)]) for m in range(4)]
        for k in range(4):
            high, low = halves(jnp.concatenate([mixed[m][k] for m in range(4)], axis=0))
            split[f, k * y : (k + 1) * y, 0:width] = high
            split[f, k * y : (k + 1) * y, width : 2 * width] = low
        product = jnp.dot(split[f], matrix[...], preferred_element_type=jnp.float32)
        result = product[:, 0:width] + product[:, width : 2 * width]
        peak = None
        for k in range(4):
            for m in range(4):
                value = result[k * y + m * nb : k * y + (m + 1) * nb]
                coefficients[f * depth + k, pl.ds(m, nb, stride=4), :] = value
                size = jnp.abs(value)
                peak = size if peak is None else jnp.maximum(peak, size)
        blocks[f] = over_lanes(peak)

    me = lax.axis_index("section")
    if rows % 8 == 0:
        for k in range(count):
            p = partner_of(me, k, count)
            for j in range(total):
                outs[k][j // depth, j % depth] = coefficients[j, pl.ds(pl.multiple_of(p * rows, 8), rows), :]
    else:
        for p in range(count):
            staged[p] = coefficients[:, p * rows : (p + 1) * rows, :]
        for k in range(count):
            p = partner_of(me, k, count)
            for j in range(total):
                outs[k][j // depth, j % depth] = staged[p, j]


def transform_bricks(count, inside, down, up, columns, matrix):
    total, y, width = inside.shape
    depth = total // FIELDS
    rows, tall = y // count, y + 2 * PAD
    chunk = array((FIELDS, depth, rows, width))
    rim = array((total, 2 * PAD, width))
    results = pl.pallas_call(
        functools.partial(brick_kernel, count),
        out_shape=[chunk] * count + [array((FIELDS, y // 4, width))] + [rim] * 3,
        in_specs=[vmem()] * 5,
        out_specs=[vmem()] * (count + 4),
        scratch_shapes=[
            pltpu.VMEM((total, tall, width), jnp.float32),
            pltpu.VMEM((2, FIELDS, y, width), jnp.float32),
            pltpu.VMEM((FIELDS, depth * y, 2 * width), jnp.bfloat16),
            pltpu.VMEM((total, y, width), jnp.float32),
            pltpu.VMEM((1, 1, 8, LANES) if rows % 8 == 0 else (count, total, rows, width), jnp.float32),
        ],
        compiler_params=kernel_params(),
        cost_estimate=pl.CostEstimate(flops=80 * total * y * width, bytes_accessed=16 * total * y * width, transcendentals=0),
    )(inside, down, up, columns, matrix)
    return results[:count], results[count], results[count + 1 :]


def leaving_order(count):
    return [*range(count - 1, 0, -1), 0]


def mend_kernel(count, *refs):
    chunks, refs = refs[:count], refs[count:]
    top, bottom, blocks, rim_a, rim_d, rim_u, matrix = refs[:7]
    outs, mended, refs = refs[7 : 7 + count], refs[7 + count], refs[8 + count :]
    halo, columns, across, down, up, folded, split, result, fixed = refs
    fields, depth, rows, width = chunks[0].shape
    total = fields * depth
    nb = blocks.shape[1]

    halo[...] = jnp.ones(halo.shape, jnp.float32)
    columns[...] = jnp.ones(columns.shape, jnp.float32)
    for j in range(total):
        halo[j, 4:8, :] = top[4 * j : 4 * j + 4, :]
        halo[j, 8:12, :] = bottom[4 * j : 4 * j + 4, :]
    for side in range(2):
        place = 4 * total + 4 * side
        columns[side, 4:8, :] = top[place : place + 4, :]
        columns[side, 8:12, :] = bottom[place : place + 4, :]
    low = column_terms(columns[0], depth, COURANT)
    high = column_terms(columns[1], depth, -COURANT)
    for z in range(depth):
        c = [halo[f * depth + z] for f in range(fields)]
        for f, (a, d, u) in enumerate(row_terms(c)):
            j = f * depth + z
            values = (a + beside(low[f], high[f], z), d, u)
            for value, rim, target in zip(values, (rim_a, rim_d, rim_u), (across, down, up)):
                target[j, 0:8, :] = value[0:8]
                target[j, 8:24, :] = rim[j]
                target[j, 24:32, :] = value[8:16]
    for j in range(total):
        for k, value in enumerate(fold_rows(across, down, up, j, PAD, 2, 12)):
            folded[j, 2 * k : 2 * k + 2, :] = value
    for f in range(fields):
        values = butterfly(*[folded[f * depth + z] for z in range(4)])
        for half in range(2):
            both = jnp.concatenate(values[2 * half : 2 * half + 2], axis=0)
            upper, lower = halves(both)
            place = f * 32 + half * 16
            split[place : place + 16, 0:width] = upper
            split[place : place + 16, width : 2 * width] = lower
    product = jnp.dot(split[...], matrix[...], preferred_element_type=jnp.float32)
    result[...] = product[:, 0:width] + product[:, width : 2 * width]
    for j in range(total):
        for side in range(2):
            fixed[side, j] = result[pl.ds(8 * j + side, 4, stride=2), :]
    mended[...] = blocks[...]
    for f in range(fields):
        for side in range(2):
            size = jnp.abs(fixed[side, f * depth])
            for z in range(1, depth):
                size = jnp.maximum(size, jnp.abs(fixed[side, f * depth + z]))
            peak = over_lanes(jnp.max(size, axis=0, keepdims=True))
            row = side * (nb - 1)
            mended[f, row : row + 1, :] = peak

    me = lax.axis_index("section")
    for i, k in enumerate(leaving_order(count)):
        p = partner_of(me, k, count)
        for side, start in ((0, 0), (1, rows - 4)):

            @pl.when(p == side * (count - 1))
            def replace(i=i, side=side, start=start):
                for j in range(total):
                    outs[i][j // depth, j % depth, start : start + 4, :] = fixed[side, j]


def mend(count, chunks, top, bottom, blocks, rims, matrix):
    fields, depth, rows, width = chunks[0].shape
    total = fields * depth
    tall = pltpu.VMEM((total, 4 * PAD, width), jnp.float32)
    results = pl.pallas_call(
        functools.partial(mend_kernel, count),
        out_shape=[array(chunks[0].shape)] * count + [array(blocks.shape)],
        in_specs=[vmem()] * (count + 7),
        out_specs=[vmem()] * (count + 1),
        input_output_aliases={k: k for k in range(count)},
        scratch_shapes=[
            pltpu.VMEM((total, 2 * PAD, width), jnp.float32),
            pltpu.VMEM((2, 2 * PAD, width), jnp.float32),
            tall,
            tall,
            tall,
            pltpu.VMEM((total, 8, width), jnp.float32),
            pltpu.VMEM((8 * total, 2 * width), jnp.bfloat16),
            pltpu.VMEM((8 * total, width), jnp.float32),
            pltpu.VMEM((2, total, 4, width), jnp.float32),
        ],
        compiler_params=kernel_params(),
    )(*[chunks[k] for k in leaving_order(count)], top, bottom, blocks, *rims, matrix)
    return dict(zip(leaving_order(count), results)), results[count]


def group_kernel(count, groups, own_rows, *refs):
    blocks, refs = refs[0], refs[1:]
    messages, (peaks, gathered, listed, packed, table) = refs[:count], refs[count:]
    nb = blocks.shape[1]
    me = lax.axis_index("section")
    slot = slot_of(messages[0], me)
    within = lax.rem(slot, 4) * 32
    tile = lax.div(slot, 4)
    for d, message in enumerate(messages):
        height = gathered.shape[1]
        value = message[message.shape[0] - height :, :]
        if count > 4:
            value = pltpu.roll(value, lax.rem(height - tile * own_rows, height), 0)
        gathered[lax.rem(me + count - d, count)] = value
    for q in range(count):
        listed[q * own_rows : (q + 1) * own_rows, :] = gathered[q, 0:own_rows, :]
    part = nb // 4
    band = lax.div(lanes_of((part, LANES)), 32)
    labels = jnp.zeros((part, LANES), jnp.float32)
    for c in range(4):
        turned = pltpu.roll(listed[c * part : (c + 1) * part, :], lax.rem(32 * c - within + LANES, LANES), 1)
        labels = jnp.where(band == c, turned, labels)
    for f in range(FIELDS):
        own = jnp.zeros((part, LANES), jnp.float32)
        for c in range(4):
            own = jnp.where(band == c, blocks[f, c * part : (c + 1) * part, :], own)
        packed[f, 0:part, :] = own
    lane8 = lanes_of((8, LANES))
    sub8 = lax.broadcasted_iota(jnp.int32, (8, LANES), 0)
    label_rows = [jnp.broadcast_to(labels[r : r + 1], (8, LANES)) for r in range(part)]

    def group_tile(g, carry):
        wanted = (sub8 + g * 8).astype(jnp.float32)
        matches = [label_rows[r] == wanted for r in range(part)]
        found = jnp.zeros((8, LANES), jnp.float32)
        for f in range(FIELDS):
            best = jnp.zeros((8, LANES), jnp.float32)
            for r in range(part):
                row = jnp.broadcast_to(packed[f, r : r + 1, :], (8, LANES))
                best = jnp.maximum(best, jnp.where(matches[r], row, 0.0))
            found = jnp.where(lane8 == f, jnp.max(best, axis=1, keepdims=True), found)
        table[pl.ds(pl.multiple_of(g * 8, 8), 8), :] = found
        return carry

    high = table.shape[0]
    if groups < high:
        table[...] = jnp.zeros((high, LANES), jnp.float32)
    lax.fori_loop(0, pl.cdiv(groups, 8), group_tile, 0)
    for g in range(high // LANES):
        peaks[:, g * LANES : (g + 1) * LANES] = jnp.transpose(table[g * LANES : (g + 1) * LANES, :])[0:8]


def group_maxima(count, groups, own_rows, blocks, messages):
    high = pl.cdiv(groups, LANES) * LANES
    nb = blocks.shape[1]
    return pl.pallas_call(
        functools.partial(group_kernel, count, groups, own_rows),
        out_shape=array((8, high)),
        in_specs=[vmem()] * (count + 1),
        out_specs=vmem(),
        scratch_shapes=[
            pltpu.VMEM((count, messages[0].shape[0], LANES), jnp.float32),
            pltpu.VMEM((nb, LANES), jnp.float32),
            pltpu.VMEM((FIELDS, 8, LANES), jnp.float32),
            pltpu.VMEM((high, LANES), jnp.float32),
        ],
        compiler_params=kernel_params(),
    )(blocks, *messages)


def scale_kernel(count, groups, *refs):
    chunks, refs = refs[:count], refs[count:]
    peaks, labels, coded, group_peak, wide = refs
    fields, depth, rows, width = chunks[0].shape
    nb = rows // 4
    high = peaks.shape[1]
    me = lax.axis_index("section")
    group_peak[...] = peaks[0:fields, 0:groups]
    own_labels = labels[...].astype(jnp.int32)
    lane = lanes_of((8, LANES))
    inverse = 1.0 / (peaks[...] + EPSILON)
    tables = [
        [jnp.broadcast_to(inverse[f : f + 1, g * LANES : (g + 1) * LANES], (8, LANES)) for g in range(high // LANES)]
        for f in range(fields)
    ]
    for i, k in enumerate(leaving_order(count)):
        slot = slot_of(labels, sender_of(me, k, count))
        tile = own_labels
        if count > 4:
            tile = pltpu.roll(tile, lax.rem(LABEL_ROWS - lax.div(slot, 4) * nb, LABEL_ROWS), 0)
        within = lax.rem(slot, 4) * 32 + lax.rem(lane, 32)
        own = jnp.take_along_axis(tile, within, axis=1)
        place = pl.ds(pl.multiple_of(slot * width, width), width)
        for f in range(fields):
            if high == LANES:
                found = jnp.take_along_axis(tables[f][0], own, axis=1)
            else:
                found = jnp.zeros((8, LANES), jnp.float32)
                inside = lax.rem(own, LANES)
                for g in range(high // LANES):
                    here = jnp.take_along_axis(tables[f][g], inside, axis=1)
                    found = jnp.where(lax.div(own, LANES) == g, here, found)
            for m in range(4):
                wide[i, f, pl.ds(m, nb, stride=4), :] = found[0:nb]
            factor = wide[i, f]
            for z in range(depth):
                coded[f, z, :, place] = chunks[i][f, z] * factor


def scale(count, groups, chunks, peaks, labels):
    fields, depth, rows, width = chunks[0].shape
    return pl.pallas_call(
        functools.partial(scale_kernel, count, groups),
        out_shape=[array((fields, depth, rows, width * count)), array((fields, groups))],
        in_specs=[vmem()] * (count + 2),
        out_specs=[vmem()] * 2,
        scratch_shapes=[
            pltpu.VMEM((count, fields, rows, width), jnp.float32),
        ],
        compiler_params=kernel_params(),
    )(*chunks, peaks, labels)


def ring(axis, shift):
    count = lax.axis_size(axis)
    return [(i, (i + shift) % count) for i in range(count)]


def exchange_pairs(count, k):
    if count & (count - 1) == 0:
        return [(i, i ^ k) for i in range(count)]
    return [(i, (i + k) % count) for i in range(count)]


def steps_over(axis):
    count = lax.axis_size(axis)
    span, shifts = 1, []
    while span < count:
        shifts.append(min(span, count - span))
        span += shifts[-1]
    return shifts


def with_others(value, axis, shifts):
    count = lax.axis_size(axis)
    others = [lax.ppermute(value, axis, exchange_pairs(count, k)) for k in shifts]
    return functools.reduce(jnp.maximum, others, value)


def per_device(density, momentum, energy, membership, slot_of_brick):
    count = lax.axis_size("section")
    groups = 2 * lax.axis_size("sim") * count
    conserved = jnp.concatenate([density[None], momentum, energy[None]], axis=0)
    first_x, last_x, labels = pack(conserved, membership, slot_of_brick)
    left = lax.ppermute(last_x, "section", ring("section", 1))
    right = lax.ppermute(first_x, "section", ring("section", -1))
    far = [lax.ppermute(labels, "section", ring("section", d)) for d in range(2, count - 1)]
    inside, down, up, matrix = own_fluxes(conserved)
    left, right, inside = lax.optimization_barrier((left, right, inside))
    first_y, last_y, columns = edge_rows(conserved, left, right)
    top = lax.ppermute(last_y, "sim", ring("sim", 1))
    bottom = lax.ppermute(first_y, "sim", ring("sim", -1))
    chunks, blocks, rims = transform_bricks(count, inside, down, up, columns, matrix)
    blocks, *far = lax.optimization_barrier((blocks, *far))
    chunks, blocks = mend(count, chunks, top, bottom, blocks, rims, matrix)
    moved = {0: chunks[0]}
    for k in leaving_order(count)[:-1]:
        moved[k] = lax.ppermute(chunks[k], "section", exchange_pairs(count, k))
    peaks = group_maxima(count, groups, membership.shape[0], blocks, [labels, left, *far, right])
    for shift in steps_over("sim"):
        peaks = with_others(peaks, "sim", [shift])
    for shift in steps_over("section"):
        peaks = with_others(peaks, "section", [shift])
    return tuple(scale(count, groups, [moved[k] for k in leaving_order(count)], peaks, labels))


def solution(mesh):
    placed = (
        P(None, "sim", "section"),
        P(None, None, "sim", "section"),
        P(None, "sim", "section"),
        P(("sim", "section"), None),
        P("sim", None),
    )
    return jax.shard_map(
        per_device,
        mesh=mesh,
        in_specs=placed,
        out_specs=(P(None, None, ("sim", "section"), None), P()),
        check_vma=False,
    )
```
